32 devices in a mesh: grp: 4 (over y, x), rep: 8 (over z, core).
Axes of the slice: x: 2, y: 2, z: 4, core: 2. Of those that a mesh axis runs over, the one named last changes fastest.
Arguments:
- tokens: bfloat16 [8, 1536, 1024], P('rep', 'grp'), may hold values from -6 to 6
- slot_ids: int32 [8, 1536], P('rep', 'grp'), may hold values from -1 to 8, as said below
- cotangent: bfloat16 [8, 1536, 1024], P('rep', 'grp'), may hold values from -6 to 6
- inproj: float32 [1024, 3072], P('grp'), may hold values from -0.25 to 0.25
- outproj: float32 [1024, 1024], P('grp'), may hold values from -1 to 1
- upproj: float32 [1024, 5248], P('grp'), may hold values from -0.1875 to 0.1875
- downproj: float32 [2624, 1024], P('grp'), may hold values from -0.125 to 0.125
- norm_gains: float32 [1024, 2], P('grp'), may hold values from 0.5 to 1.5
- inproj_mean: float32 [1024, 3072], P('grp'), may hold values from -128 to 128
- outproj_mean: float32 [1024, 1024], P('grp'), may hold values from -16 to 16
- upproj_mean: float32 [1024, 5248], P('grp'), may hold values from -32 to 32
- downproj_mean: float32 [2624, 1024], P('grp'), may hold values from -48 to 48
- gains_mean: float32 [1024, 2], P('grp'), may hold values from -192 to 192
- inproj_square: float32 [1024, 3072], P('grp'), may hold values from 49.152 to 196.608
- outproj_square: float32 [1024, 1024], P('grp'), may hold values from 0.768 to 3.072
- upproj_square: float32 [1024, 5248], P('grp'), may hold values from 2.162688 to 8.6016
- downproj_square: float32 [2624, 1024], P('grp'), may hold values from 5.16096 to 20.8896
- gains_square: float32 [1024, 2], P('grp'), may hold values from 11.0592 to 1228.8
Outputs:
- layer_out: bfloat16 [8, 1536, 1024], P('rep', 'grp')
- input_grad: bfloat16 [8, 1536, 1024], P('rep', 'grp')
- newmean_inproj: float32 [1024, 3072], P('grp')
- newsquare_inproj: float32 [1024, 3072], P('grp')
- updated_inproj: float32 [1024, 3072], P('grp')
- newmean_outproj: float32 [1024, 1024], P('grp')
- newsquare_outproj: float32 [1024, 1024], P('grp')
- updated_outproj: float32 [1024, 1024], P('grp')
- newmean_upproj: float32 [1024, 5248], P('grp')
- newsquare_upproj: float32 [1024, 5248], P('grp')
- updated_upproj: float32 [1024, 5248], P('grp')
- newmean_downproj: float32 [2624, 1024], P('grp')
- newsquare_downproj: float32 [2624, 1024], P('grp')
- updated_downproj: float32 [2624, 1024], P('grp')
- newmean_gains: float32 [1024, 2], P('grp')
- newsquare_gains: float32 [1024, 2], P('grp')
- updated_gains: float32 [1024, 2], P('grp')
The draws below stay inside these ranges and needn't reach their ends.
Inputs may be any that keep to these rules, and one draw needn't show every extreme that they name: `slot_ids`: in each group, every device's 384 slots hold its live slots first and empty slots (-1) after them; each device has 336 to 384 live slots, and in every group some device has all of them live and some has exactly 336. Sequence numbers never fall along the live slots of a group; a sequence is the live slots of one number. In every group one sequence has slots on the first and on the last device, and the largest number used is 8.
All inputs are finite; a program needn't handle non-finite values.
Results may differ from the reference program's by a relative error of at most 0.015.
The reference program's roundings to bfloat16 on the way count: a program that leaves them out, or rounds other values in their place, can miss the bound.
Values may be sent and summed in bfloat16 or wider, within the bound.
No kernel may reach another device: no remote copies, remote signals or barrier semaphores. Data moves between devices by JAX's collectives and lax.ppermute only.
A program may use at most 256 MiB of HBM per device.

```python
import math
import jax
import jax.numpy as jnp
from jax import lax

D = 1024
HEADS = 16
HEAD = 64
FF = 2624
TOK_DEV = 384
STEP = 10
SEQ_SLOTS = 9
ROWS = 1536
ALL_TOKENS = 12288
N_GRP = 4
N_REP = 8


def draw_slot_ids(key, part):
    key = jax.random.fold_in(key, 11)
    keys = jax.random.split(key, 7)
    least = TOK_DEV * 7 // 8
    counts = jax.random.randint(keys[0], (N_REP, N_GRP), least, TOK_DEV + 1)
    full_device = jax.random.randint(keys[1], (N_REP, 1), 0, N_GRP)
    thin_device = (full_device + 1 + jax.random.randint(keys[2], (N_REP, 1), 0, N_GRP - 1)) % N_GRP
    devices = jnp.arange(N_GRP, dtype=jnp.int32)[None, :]
    counts = jnp.where(devices == full_device, TOK_DEV, counts)
    counts = jnp.where(devices == thin_device, least, counts).astype(jnp.int32)
    total = jnp.sum(counts, axis=1).astype(jnp.int32)
    before = (jnp.cumsum(counts, axis=1) - counts).astype(jnp.int32)
    start_cut = jax.random.randint(keys[3], (N_REP,), 1, counts[:, 0])
    tail = jax.random.randint(keys[4], (N_REP,), 1, counts[:, N_GRP - 1])
    end_cut = total - tail
    head_cuts = jax.random.randint(keys[5], (N_REP, 3), 0, start_cut[:, None])
    tail_cuts = jax.random.randint(keys[6], (N_REP, 3), end_cut[:, None], total[:, None])
    cuts = jnp.concatenate([start_cut[:, None], end_cut[:, None], head_cuts, tail_cuts], axis=1)
    slots = jnp.arange(ROWS, dtype=jnp.int32)
    device = slots // TOK_DEV
    within = slots % TOK_DEV
    live = within[None, :] < counts[:, device]
    order = before[:, device] + within[None, :]
    numbers = jnp.sum((cuts[:, None, :] <= order[:, :, None]).astype(jnp.int32), axis=2)
    return jnp.where(live, numbers, -1).astype(jnp.int32)


def level_of(key, dims, shards, low, top_value):
    factor_of = 1.0
    for dim, shards_of in shards:
        draws = jax.random.uniform(jax.random.fold_in(jax.random.fold_in(key, 6), dim), (shards_of,), jnp.float32, low / len(shards), top_value / len(shards))
        factor_of = factor_of * jnp.repeat(jnp.exp(draws), dims[dim] // shards_of).reshape((-1,) + (1,) * (len(dims) - 1 - dim))
    return factor_of


def scatter_about(stream_key, dims, scale, most, cuts=(), kind=jnp.bfloat16):
    drawn = jax.random.normal(stream_key, dims, jnp.float32) * scale
    if len(cuts) > 0:
        drawn = level_of(stream_key, dims, cuts, -0.22, 0.18) * drawn
    return jnp.clip(drawn, min=-most, max=most).astype(kind)


def setup_inputs(seed: int = 0) -> dict:
    seeds = jax.random.split(jax.random.key(seed), 19)
    tokens = scatter_about(seeds[0], (N_REP, ROWS, D), 1.0, 6.0, ((0, 8), (1, 4)))
    slot_ids = draw_slot_ids(jax.random.fold_in(seeds[18], 71), 0)
    cotangent = scatter_about(seeds[2], (N_REP, ROWS, D), 1.0, 6.0, ((0, 8), (1, 4)))
    inproj = scatter_about(seeds[3], (D, 3 * D), (D // 2) ** -0.5, 0.25, ((0, 4),), jnp.float32)
    outproj = scatter_about(seeds[4], (D, D), (D // 32) ** -0.5, 1.0, ((0, 4),), jnp.float32)
    upproj = scatter_about(seeds[5], (D, 2 * FF), D ** -0.5, 0.1875, ((0, 4),), jnp.float32)
    downproj = scatter_about(seeds[6], (FF, D), FF ** -0.5, 0.125, ((0, 4),), jnp.float32)
    norm_gains = jnp.clip(1.0 + 0.1 * jax.random.normal(seeds[7], (D, 2), jnp.float32), 0.5, 1.5)
    inproj_mean = scatter_about(seeds[8], (D, 3 * D), (0.22 * ALL_TOKENS ** 0.5), 128.0, ((0, 4),), jnp.float32)
    outproj_mean = scatter_about(seeds[9], (D, D), (0.0275 * ALL_TOKENS ** 0.5), 16.0, ((0, 4),), jnp.float32)
    upproj_mean = scatter_about(seeds[10], (D, 2 * FF), (0.046 * ALL_TOKENS ** 0.5), 32.0, ((0, 4),), jnp.float32)
    downproj_mean = scatter_about(seeds[11], (FF, D), (0.07 * ALL_TOKENS ** 0.5), 48.0, ((0, 4),), jnp.float32)
    gains_mean = scatter_about(seeds[12], (D, 2), (0.27 * ALL_TOKENS ** 0.5), 192.0, ((0, 4),), jnp.float32)
    inproj_square = jnp.clip(jnp.exp(math.log(196.608) - 1.3862944 * jax.random.uniform(seeds[13], (D, 3 * D), jnp.float32) ** level_of(seeds[13], (D, 3 * D), ((0, 4),), -0.2, 0.2)), 49.152, 196.608)
    outproj_square = jnp.clip(jnp.exp(math.log(3.072) - 1.3862944 * jax.random.uniform(seeds[14], (D, D), jnp.float32) ** level_of(seeds[14], (D, D), ((0, 4),), -0.2, 0.2)), 0.768, 3.072)
    upproj_square = jnp.clip(jnp.exp(math.log(8.6016) - 1.3805963 * jax.random.uniform(seeds[15], (D, 2 * FF), jnp.float32) ** level_of(seeds[15], (D, 2 * FF), ((0, 4),), -0.2, 0.2)), 2.162688, 8.6016)
    downproj_square = jnp.clip(jnp.exp(math.log(20.8896) - 1.39812882 * jax.random.uniform(seeds[16], (FF, D), jnp.float32) ** level_of(seeds[16], (FF, D), ((0, 4),), -0.2, 0.2)), 5.16096, 20.8896)
    gains_square = jnp.clip(jnp.exp(math.log(1228.8) - 4.7105307 * jax.random.uniform(seeds[17], (D, 2), jnp.float32) ** level_of(seeds[17], (D, 2), ((0, 4),), -0.2, 0.2)), 11.0592, 1228.8)
    return {"tokens": tokens, "slot_ids": slot_ids, "cotangent": cotangent, "inproj": inproj, "outproj": outproj, "upproj": upproj, "downproj": downproj, "norm_gains": norm_gains, "inproj_mean": inproj_mean, "outproj_mean": outproj_mean, "upproj_mean": upproj_mean, "downproj_mean": downproj_mean, "gains_mean": gains_mean, "inproj_square": inproj_square, "outproj_square": outproj_square, "upproj_square": upproj_square, "downproj_square": downproj_square, "gains_square": gains_square}


rope_base = 160000.0
norm_eps = 1e-05
highest = lax.Precision.HIGHEST
rate_list = (0.1, 0.4, 0.08, 0.05, 0.6)

@jax.custom_vjp
def low(v):
    return lax.optimization_barrier(v.astype(jnp.bfloat16)).astype(jnp.float32)

@jax.custom_vjp
def low_back(v):
    return v

def low_keep(v):
    return (low(v), None)

def low_pass(kept, grad):
    return (grad,)

def back_keep(v):
    return (v, None)

def back_low(kept, grad):
    return (low(grad),)
low.defvjp(low_keep, low_pass)
low_back.defvjp(back_keep, back_low)

def matmul(left, right):
    return jnp.dot(left, right, precision=highest, preferred_element_type=jnp.float32)

def layer_norm(values, gain):
    centred = values - lax.optimization_barrier(jnp.mean(values, axis=-1, keepdims=True))
    spread = lax.optimization_barrier(jnp.mean(centred * centred, axis=-1, keepdims=True))
    return centred * lax.rsqrt(spread + norm_eps) * gain

def positions(ids):
    live = ids >= 0
    counted = jnp.cumsum(live.astype(jnp.int32)).astype(jnp.int32) - 1
    onehot = ((ids[:, None] == jnp.arange(SEQ_SLOTS, dtype=jnp.int32)[None, :]) & live[:, None]).astype(jnp.int32)
    counts = lax.optimization_barrier(jnp.sum(onehot, axis=0)).astype(jnp.int32)
    starts = (jnp.cumsum(counts).astype(jnp.int32) - counts).astype(jnp.int32)
    first = lax.optimization_barrier(jnp.sum(onehot * starts[None, :], axis=1)).astype(jnp.int32)
    return jnp.where(live, counted - first, 0).astype(jnp.int32)

def rope_angles(where_at):
    half = HEAD // 2
    inverse = rope_base ** (-(jnp.arange(half, dtype=jnp.float32) * 2.0 / HEAD))
    angles = where_at.astype(jnp.float32)[:, None] * inverse[None, :]
    return jnp.concatenate([angles, angles], axis=1)

def rotate(values, angles):
    count = values.shape[0]
    half = HEAD // 2
    heads = values.reshape(count, HEADS, HEAD)
    turned = jnp.concatenate([-heads[..., half:], heads[..., :half]], axis=-1)
    result = heads * jnp.cos(angles)[:, None, :] + turned * jnp.sin(angles)[:, None, :]
    return result.reshape(count, D)

def attend(query, keys, values, ids):
    count = query.shape[0]
    scale = HEAD ** (-0.5)
    key_heads = keys.reshape(count, HEADS, HEAD)
    value_heads = values.reshape(count, HEADS, HEAD)
    slots = jnp.arange(count, dtype=jnp.int32)

    @jax.checkpoint
    def block(pieces):
        query_block, block_ids, block_slots = pieces
        scores = jnp.einsum('qhd,khd->hqk', query_block, key_heads, precision=highest) * scale
        allowed = (block_ids[:, None] == ids[None, :]) & (block_ids[:, None] >= 0) | (block_slots[:, None] == slots[None, :])
        scores = low_back(jnp.where(allowed[None], scores, -1e+30))
        row_max = lax.optimization_barrier(jnp.max(scores, axis=-1, keepdims=True))
        expo = jnp.exp(scores - row_max)
        probs = low(expo / lax.optimization_barrier(jnp.sum(expo, axis=-1, keepdims=True)))
        return jnp.einsum('hqk,khd->qhd', probs, value_heads, precision=highest)
    blocked = lax.map(block, (query.reshape(-1, TOK_DEV, HEADS, HEAD), ids.reshape(-1, TOK_DEV), slots.reshape(-1, TOK_DEV)))
    return blocked.reshape(count, D)

def forward(params, inputs, ids, angles):
    w_in, w_out, w_up, w_down, gains = [low(item) for item in params]
    first_normed = low(layer_norm(inputs, gains[:, 0]))
    projected = low_back(matmul(first_normed, w_in))
    query = low(rotate(projected[:, :D], angles))
    keys = low(rotate(projected[:, D:2 * D], angles))
    values = low(projected[:, 2 * D:])
    attended = low_back(low(attend(query, keys, values, ids)))
    middle = inputs + low_back(matmul(attended, w_out))
    second_normed = low(layer_norm(middle, gains[:, 1]))
    gate_up = low_back(matmul(second_normed, w_up))
    hidden = low(jax.nn.gelu(gate_up[:, :FF], approximate=False) * gate_up[:, FF:])
    return middle + matmul(hidden, w_down)

def adam_update(weight, mean, square, grad, rate):
    mean_new = 0.9 * mean + 0.1 * grad
    square_new = 0.999 * square + 0.001 * grad * grad
    step_size = mean_new / (1.0 - 0.9 ** STEP) / (jnp.sqrt(square_new / (1.0 - 0.999 ** STEP)) + 1e-08)
    return (mean_new, square_new, weight - rate * (step_size + 0.01 * weight))

def reference(tokens, slot_ids, cotangent, inproj, outproj, upproj, downproj, norm_gains, inproj_mean, outproj_mean, upproj_mean, downproj_mean, gains_mean, inproj_square, outproj_square, upproj_square, downproj_square, gains_square):
    params = (inproj, outproj, upproj, downproj, norm_gains)

    def one_group(totals, group):
        inputs, grad_out, ids = group
        live = (ids >= 0).astype(jnp.float32)
        angles = rope_angles(positions(ids))
        result, back = jax.vjp(lambda chosen, start: forward(chosen, start, ids, angles), params, inputs.astype(jnp.float32))
        grads, grad_in = back(grad_out.astype(jnp.float32) * live[:, None])
        totals = tuple((total + grad for total, grad in zip(totals, grads)))
        return (totals, (result.astype(jnp.bfloat16), grad_in.astype(jnp.bfloat16)))
    zeros = tuple((jnp.zeros_like(item, dtype=jnp.float32) for item in params))
    totals, (outputs, grads_in) = lax.scan(one_group, zeros, (tokens, cotangent, slot_ids))
    means = (inproj_mean, outproj_mean, upproj_mean, downproj_mean, gains_mean)
    squares = (inproj_square, outproj_square, upproj_square, downproj_square, gains_square)
    updates = [adam_update(params[index], means[index], squares[index], totals[index], rate_list[index]) for index in range(5)]
    return (outputs, grads_in, updates[0][0], updates[0][1], updates[0][2], updates[1][0], updates[1][1], updates[1][2], updates[2][0], updates[2][1], updates[2][2], updates[3][0], updates[3][1], updates[3][2], updates[4][0], updates[4][1], updates[4][2])
```

```python
import jax
import jax.numpy as jnp
from jax import lax
from jax.sharding import Mesh, PartitionSpec as P

D = 1024
HEADS = 16
HEAD = 64
FF = 2624
FF_WIDE = 2688
STEP = 10
SEQ_SLOTS = 9


rope_base = 160000.0
norm_eps = 1e-05
rate_list = (0.1, 0.4, 0.08, 0.05, 0.6)


def layer_norm(values, gain):
    centred = values - jnp.mean(values, axis=-1, keepdims=True)
    spread = jnp.mean(centred * centred, axis=-1, keepdims=True)
    return centred * lax.rsqrt(spread + norm_eps) * gain


def positions(ids):
    live = ids >= 0
    counted = jnp.cumsum(live.astype(jnp.int32)) - 1
    onehot = (
        (ids[:, None] == jnp.arange(SEQ_SLOTS, dtype=jnp.int32)[None, :]) & live[:, None]
    ).astype(jnp.int32)
    counts = jnp.sum(onehot, axis=0)
    starts = jnp.cumsum(counts) - counts
    first = jnp.sum(onehot * starts[None, :], axis=1)
    return jnp.where(live, counted - first, 0)


def rope_angles(where_at):
    half = HEAD // 2
    inverse = rope_base ** (-(jnp.arange(half, dtype=jnp.float32) * 2.0 / HEAD))
    angles = where_at.astype(jnp.float32)[:, None] * inverse[None, :]
    return jnp.concatenate([angles, angles], axis=1)


def rotate(values, angles):
    count = values.shape[0]
    half = HEAD // 2
    heads = values.reshape(count, HEADS, HEAD)
    turned = jnp.concatenate([-heads[..., half:], heads[..., :half]], axis=-1)
    result = heads * jnp.cos(angles)[:, None, :] + turned * jnp.sin(angles)[:, None, :]
    return result.reshape(count, D)


def product(left, right):
    return jnp.dot(left, right, preferred_element_type=jnp.float32)


def contract(left, right):
    return lax.dot_general(
        left, right, (((0,), (0,)), ((), ())), preferred_element_type=jnp.float32
    )


def against(left, right):
    return lax.dot_general(
        left, right, (((1,), (1,)), ((), ())), preferred_element_type=jnp.float32
    )


def split_pairs(values):
    return values.reshape(values.shape[0], HEADS // 2, 2, HEAD).transpose(1, 0, 2, 3)


def join_pairs(values):
    return values.transpose(1, 0, 2, 3).reshape(values.shape[1], D)


def masked_scores(query_pair, key_pair, allowed):
    scores = jnp.einsum(
        "qhd,khd->hqk", query_pair, key_pair, preferred_element_type=jnp.float32
    ) * HEAD ** (-0.5)
    return jnp.where(allowed[None], scores, -1e30)


def attention_forward(query, keys, values, allowed):

    def one_pair(pieces):
        query_pair, key_pair, value_pair = pieces
        scores = masked_scores(query_pair, key_pair, allowed)
        row_max = jnp.max(scores, axis=-1, keepdims=True)
        totals = jnp.sum(jnp.exp(scores - row_max), axis=-1, keepdims=True)
        log_totals = row_max + jnp.log(totals)
        weights = jnp.exp(scores - log_totals).astype(jnp.bfloat16)
        mixed = jnp.einsum("hqk,khd->qhd", weights, value_pair, preferred_element_type=jnp.float32)
        return (mixed, log_totals[..., 0])

    mixed, log_totals = lax.map(
        one_pair, (split_pairs(query), split_pairs(keys), split_pairs(values))
    )
    return (join_pairs(mixed), log_totals)


def attention_backward(query, keys, values, grad_attended, log_totals, allowed):
    scale = HEAD ** (-0.5)

    def one_pair(pieces):
        query_pair, key_pair, value_pair, grad_pair, total_pair = pieces
        scores = masked_scores(query_pair, key_pair, allowed)
        weights = jnp.exp(scores - total_pair[..., None])
        low_weights = weights.astype(jnp.bfloat16)
        grad_values = jnp.einsum(
            "hqk,qhd->khd", low_weights, grad_pair, preferred_element_type=jnp.float32
        )
        grad_weights = jnp.einsum(
            "qhd,khd->hqk", grad_pair, value_pair, preferred_element_type=jnp.float32
        )
        centre = jnp.sum(weights * grad_weights, axis=-1, keepdims=True)
        grad_scores = (weights * (grad_weights - centre)).astype(jnp.bfloat16)
        grad_query = (
            jnp.einsum("hqk,khd->qhd", grad_scores, key_pair, preferred_element_type=jnp.float32)
            * scale
        )
        grad_keys = (
            jnp.einsum("hqk,qhd->khd", grad_scores, query_pair, preferred_element_type=jnp.float32)
            * scale
        )
        return (grad_query, grad_keys, grad_values, centre[..., 0])

    grad_query, grad_keys, grad_values, centre = lax.map(
        one_pair,
        (
            split_pairs(query),
            split_pairs(keys),
            split_pairs(values),
            split_pairs(grad_attended),
            log_totals,
        ),
    )
    return (join_pairs(grad_query), join_pairs(grad_keys), join_pairs(grad_values), centre)


def own_half(array, core):
    half = array.shape[0] // 2
    return lax.dynamic_slice_in_dim(array, core * half, half)


def gather_weight(weight, core):
    return lax.all_gather(
        own_half(weight, core).astype(jnp.bfloat16), ("grp", "core"), axis=0, tiled=True
    )


def reduce_weight(grad):
    share = lax.psum_scatter(
        grad.astype(jnp.bfloat16), ("grp", "core"), scatter_dimension=0, tiled=True
    )
    share = lax.psum(share, "far")
    return lax.all_gather(share, "core", axis=0, tiled=True).astype(jnp.float32)


def spread_halves(array):
    spare = ((0, 0), (0, FF_WIDE - FF))
    return jnp.concatenate([jnp.pad(array[:, :FF], spare), jnp.pad(array[:, FF:], spare)], axis=1)


def joined_halves(array):
    return jnp.concatenate([array[:, :FF], array[:, FF_WIDE : FF_WIDE + FF]], axis=1)


def gated(gate, upward):
    return jax.nn.gelu(gate, approximate=False) * upward


def adam_update(weight, mean, square, grad, rate):
    mean_new = 0.9 * mean + 0.1 * grad
    square_new = 0.999 * square + 0.001 * grad * grad
    step_size = mean_new / (1.0 - 0.9**STEP) / (jnp.sqrt(square_new / (1.0 - 0.999**STEP)) + 1e-08)
    return (mean_new, square_new, weight - rate * (step_size + 0.01 * weight))


def local(
    tokens,
    slot_ids,
    cotangent,
    inproj,
    outproj,
    upproj,
    downproj,
    norm_gains,
    inproj_mean,
    outproj_mean,
    upproj_mean,
    downproj_mean,
    gains_mean,
    inproj_square,
    outproj_square,
    upproj_square,
    downproj_square,
    gains_square,
):
    own_rows = tokens.shape[1]
    own_index = lax.axis_index("grp")
    core = lax.axis_index("core")
    masters = (inproj, outproj, upproj, downproj, norm_gains)
    w_in = gather_weight(inproj, core)
    gains_low = lax.all_gather(norm_gains.astype(jnp.bfloat16), "grp", axis=0, tiled=True)
    w_out = gather_weight(outproj, core)
    w_up = gather_weight(spread_halves(upproj), core)
    w_down = gather_weight(downproj, core)
    w_down = jnp.pad(w_down, ((0, FF_WIDE - FF), (0, 0)))
    gains = gains_low.astype(jnp.float32)
    all_ids = lax.all_gather(slot_ids, "grp", axis=1, tiled=True)[0]
    group_rows = all_ids.shape[0]
    own_ids = slot_ids[0]
    angles = rope_angles(
        lax.dynamic_slice_in_dim(positions(all_ids), own_index * own_rows, own_rows)
    )
    own_slots = own_index * own_rows + jnp.arange(own_rows, dtype=jnp.int32)
    group_slots = jnp.arange(group_rows, dtype=jnp.int32)
    allowed = (own_ids[:, None] == all_ids[None, :]) & (own_ids[:, None] >= 0) | (
        own_slots[:, None] == group_slots[None, :]
    )
    live = (own_ids >= 0).astype(jnp.bfloat16)
    inputs = tokens[0].astype(jnp.float32)
    first_normed = layer_norm(inputs, gains[:, 0]).astype(jnp.bfloat16)
    projected = product(first_normed, w_in)
    query = rotate(projected[:, :D], angles).astype(jnp.bfloat16)
    keys = rotate(projected[:, D : 2 * D], angles).astype(jnp.bfloat16)
    values = projected[:, 2 * D :].astype(jnp.bfloat16)
    keys_all, values_all = (
        lax.all_gather(keys, "grp", axis=0, tiled=True),
        lax.all_gather(values, "grp", axis=0, tiled=True),
    )
    attended, log_totals = attention_forward(query, keys_all, values_all, allowed)
    attended = attended.astype(jnp.bfloat16)
    middle = inputs + product(attended, w_out)
    second_normed = layer_norm(middle, gains[:, 1]).astype(jnp.bfloat16)
    gate_up = product(second_normed, w_up)
    gate = gate_up[:, :FF_WIDE]
    upward = gate_up[:, FF_WIDE:]
    hidden = gated(gate, upward).astype(jnp.bfloat16)
    result = middle + product(hidden, w_down)
    grad_top = cotangent[0] * live[:, None]
    grad_down = contract(hidden, grad_top)[:FF]
    grad_hidden = against(grad_top, w_down)
    _, gate_back = jax.vjp(gated, gate, upward)
    grad_gate, grad_upward = gate_back(grad_hidden)
    grad_gate_up = jnp.concatenate([grad_gate, grad_upward], axis=1).astype(jnp.bfloat16)
    grad_up = contract(second_normed, grad_gate_up)
    grad_second = against(grad_gate_up, w_up)
    _, second_back = jax.vjp(lambda v: layer_norm(v, gains[:, 1]), middle)
    (grad_from_norm,) = second_back(grad_second)
    grad_middle = grad_top.astype(jnp.float32) + grad_from_norm
    grad_branch = grad_middle.astype(jnp.bfloat16)
    grad_outproj = contract(attended, grad_branch)
    grad_attended = against(grad_branch, w_out).astype(jnp.bfloat16)
    grad_query, key_terms, value_terms, centre = attention_backward(
        query, keys_all, values_all, grad_attended, log_totals, allowed
    )
    grad_keys, grad_values = (
        lax.psum_scatter(
            key_terms.astype(jnp.bfloat16), "grp", scatter_dimension=0, tiled=True
        ).astype(jnp.float32),
        lax.psum_scatter(
            value_terms.astype(jnp.bfloat16), "grp", scatter_dimension=0, tiled=True
        ).astype(jnp.float32),
    )
    grad_projected = jnp.concatenate(
        [rotate(grad_query, -angles), rotate(grad_keys, -angles), grad_values], axis=1
    ).astype(jnp.bfloat16)
    grad_in = contract(first_normed, grad_projected)
    grad_first = against(grad_projected, w_in)
    _, first_back = jax.vjp(lambda v: layer_norm(v, gains[:, 0]), inputs)
    (grad_inputs,) = first_back(grad_first)
    input_grad = (grad_middle + grad_inputs).astype(jnp.bfloat16)
    total_in = reduce_weight(grad_in)
    total_out = reduce_weight(grad_outproj)
    total_up = joined_halves(reduce_weight(grad_up))
    total_down = reduce_weight(grad_down)
    low_in = inproj.astype(jnp.bfloat16).astype(jnp.float32)
    low_up = upproj.astype(jnp.bfloat16).astype(jnp.float32)
    low_gains = norm_gains.astype(jnp.bfloat16).astype(jnp.float32)
    total_gains = (
        jnp.stack([jnp.sum(low_in * total_in, axis=1), jnp.sum(low_up * total_up, axis=1)], axis=1)
        / low_gains
    )
    totals = (total_in, total_out, total_up, total_down, total_gains)
    means = (inproj_mean, outproj_mean, upproj_mean, downproj_mean, gains_mean)
    squares = (inproj_square, outproj_square, upproj_square, downproj_square, gains_square)
    updates = [
        adam_update(masters[index], means[index], squares[index], totals[index], rate_list[index])
        for index in range(5)
    ]
    return (
        result.astype(jnp.bfloat16)[None],
        input_grad[None],
        updates[0][0],
        updates[0][1],
        updates[0][2],
        updates[1][0],
        updates[1][1],
        updates[1][2],
        updates[2][0],
        updates[2][1],
        updates[2][2],
        updates[3][0],
        updates[3][1],
        updates[3][2],
        updates[4][0],
        updates[4][1],
        updates[4][2],
    )


def solution(mesh):
    group_size, replicas = mesh.devices.shape
    fine = Mesh(mesh.devices.reshape(group_size, replicas // 2, 2), ("grp", "far", "core"))
    placed = (
        P(("far", "core"), "grp", None),
        P(("far", "core"), "grp"),
        P(("far", "core"), "grp", None),
        P("grp", None),
        P("grp", None),
        P("grp", None),
        P("grp", None),
        P("grp", None),
        P("grp", None),
        P("grp", None),
        P("grp", None),
        P("grp", None),
        P("grp", None),
        P("grp", None),
        P("grp", None),
        P("grp", None),
        P("grp", None),
        P("grp", None),
    )
    return jax.shard_map(
        local,
        mesh=fine,
        in_specs=placed,
        out_specs=(
            P(("far", "core"), "grp", None),
            P(("far", "core"), "grp", None),
            P("grp", None),
            P("grp", None),
            P("grp", None),
            P("grp", None),
            P("grp", None),
            P("grp", None),
            P("grp", None),
            P("grp", None),
            P("grp", None),
            P("grp", None),
            P("grp", None),
            P("grp", None),
            P("grp", None),
            P("grp", None),
            P("grp", None),
        ),
        check_vma=False,
    )
```

```python
import functools

import jax
import jax.numpy as jnp
from jax import lax
from jax.experimental import pallas as pl
from jax.experimental.pallas import tpu as pltpu
from jax.sharding import Mesh, PartitionSpec as P

D = 1024
HEADS = 16
HEAD = 64
FF = 2624
FF_WIDE = 2688
STEP = 10
SEQ_SLOTS = 9
PAIR = 128
STAT_LANE = 16
VMEM_BYTES = 56 * 1024 * 1024


rope_base = 160000.0
norm_eps = 1e-05
rate_list = (0.1, 0.4, 0.08, 0.05, 0.6)


def layer_norm(values, gain):
    centred = values - jnp.mean(values, axis=-1, keepdims=True)
    spread = jnp.mean(centred * centred, axis=-1, keepdims=True)
    return centred * lax.rsqrt(spread + norm_eps) * gain


def positions(ids):
    live = ids >= 0
    counted = jnp.cumsum(live.astype(jnp.int32)) - 1
    onehot = (
        (ids[:, None] == jnp.arange(SEQ_SLOTS, dtype=jnp.int32)[None, :]) & live[:, None]
    ).astype(jnp.int32)
    counts = jnp.sum(onehot, axis=0)
    starts = jnp.cumsum(counts) - counts
    first = jnp.sum(onehot * starts[None, :], axis=1)
    return jnp.where(live, counted - first, 0)


def pair_tables(where_at):
    lane = jnp.arange(PAIR, dtype=jnp.int32)
    order = (lane % (HEAD // 2)).astype(jnp.float32)
    inverse = rope_base ** (-(order * 2.0 / HEAD))
    angles = where_at.astype(jnp.float32)[:, None] * inverse[None, :]
    signs = jnp.where(lane % HEAD < HEAD // 2, -1.0, 1.0)
    return jnp.cos(angles), jnp.sin(angles) * signs[None, :]


def slot_features(ids):
    lane = jnp.arange(PAIR, dtype=jnp.int32)[None, :]
    column = jnp.where(ids < 0, SEQ_SLOTS, ids)[:, None]
    own = lane == column
    query_side = jnp.where((lane <= SEQ_SLOTS) & (~own | (ids < 0)[:, None]), -1e30, 0.0)
    key_side = jnp.where(own | ((lane >= STAT_LANE) & (lane < STAT_LANE + 3)), 1.0, 0.0)
    return query_side.astype(jnp.bfloat16), key_side.astype(jnp.bfloat16)


def turned(values, cos, sin):
    lane = lax.broadcasted_iota(jnp.int32, values.shape, 1)
    half = HEAD // 2
    other = jnp.where(
        lane % HEAD < half, pltpu.roll(values, PAIR - half, 1), pltpu.roll(values, half, 1)
    )
    return values * cos + other * sin


def compiler_params():
    return pltpu.CompilerParams(vmem_limit_bytes=VMEM_BYTES)


def project_kernel(me_ref, x_ref, wq_ref, wk_ref, wv_ref, cos_ref, sin_ref, out_ref):
    weights = jnp.concatenate([wq_ref[...], wk_ref[...], wv_ref[...]], axis=1)
    got = jnp.dot(x_ref[...], weights, preferred_element_type=jnp.float32)
    cos, sin = cos_ref[0], sin_ref[0]
    query = turned(got[:, :PAIR], cos, sin) * HEAD ** (-0.5)
    keys = turned(got[:, PAIR : 2 * PAIR], cos, sin)
    out_ref[0, :, :PAIR] = query.astype(jnp.bfloat16)
    out_ref[0, :, PAIR : 2 * PAIR] = keys.astype(jnp.bfloat16)
    out_ref[0, :, 2 * PAIR :] = got[:, 2 * PAIR :].astype(jnp.bfloat16)


def project(me, first_normed, w_in, cos, sin, pair, group):
    rows = first_normed.shape[0]
    pairs = D // PAIR // group

    def column(part):
        return lambda d, me: (0, part * (D // PAIR) + (me[0] ^ d) * pairs + pair)

    return pl.pallas_call(
        project_kernel,
        grid_spec=pltpu.PrefetchScalarGridSpec(
            num_scalar_prefetch=1,
            grid=(group,),
            in_specs=[
                pl.BlockSpec((rows, D), lambda d, me: (0, 0)),
                pl.BlockSpec((D, PAIR), column(0)),
                pl.BlockSpec((D, PAIR), column(1)),
                pl.BlockSpec((D, PAIR), column(2)),
                pl.BlockSpec((1, rows, PAIR), lambda d, me: (0, 0, 0)),
                pl.BlockSpec((1, rows, PAIR), lambda d, me: (0, 0, 0)),
            ],
            out_specs=pl.BlockSpec((1, rows, 3 * PAIR), lambda d, me: (d, 0, 0)),
        ),
        out_shape=jax.ShapeDtypeStruct((group, rows, 3 * PAIR), jnp.bfloat16),
        compiler_params=compiler_params(),
        name="project",
    )(me, first_normed, w_in, w_in, w_in, cos, sin)


def row_product_kernel(me_ref, x_ref, w_ref, out_ref):
    out_ref[0] = against(x_ref[...], w_ref[...]).astype(jnp.bfloat16)


def row_product(me, left, weight, pair, group):
    rows = left.shape[0]
    pairs = D // PAIR // group
    return pl.pallas_call(
        row_product_kernel,
        grid_spec=pltpu.PrefetchScalarGridSpec(
            num_scalar_prefetch=1,
            grid=(group,),
            in_specs=[
                pl.BlockSpec((rows, D), lambda d, me: (0, 0)),
                pl.BlockSpec((PAIR, D), lambda d, me: ((me[0] ^ d) * pairs + pair, 0)),
            ],
            out_specs=pl.BlockSpec((1, rows, PAIR), lambda d, me: (d, 0, 0)),
        ),
        out_shape=jax.ShapeDtypeStruct((group, rows, PAIR), jnp.bfloat16),
        compiler_params=compiler_params(),
        name="row_product",
    )(me, left, weight)


def place_kernel(me_ref, *refs):
    out_ref = refs[-1]
    for index, ref in enumerate(refs[:-1]):
        out_ref[:, index * PAIR : (index + 1) * PAIR] = ref[0]


def place(me, pieces, parts, group):
    rows = pieces[0].shape[1]
    pairs = len(pieces)
    return pl.pallas_call(
        place_kernel,
        grid_spec=pltpu.PrefetchScalarGridSpec(
            num_scalar_prefetch=1,
            grid=(parts, group),
            in_specs=[pl.BlockSpec((1, rows, PAIR), lambda j, d, me: (d, 0, j))] * pairs,
            out_specs=pl.BlockSpec(
                (rows, pairs * PAIR), lambda j, d, me: (0, j * group + (me[0] ^ d))
            ),
        ),
        out_shape=jax.ShapeDtypeStruct((rows, parts * D), jnp.bfloat16),
        compiler_params=compiler_params(),
        name="place",
    )(me, *pieces)


def swap_heads(pieces, group):
    got = [pieces[0]]
    for step in range(1, group):
        got.append(lax.ppermute(pieces[step], "grp", [(i, i ^ step) for i in range(group)]))
    return jnp.stack(got)


def attend_kernel(q_ref, k_ref, v_ref, qf_ref, kf_ref, own_v_ref, own_f_ref, out_ref, stat_ref, ke):
    @pl.when(pl.program_id(0) == 0)
    def _():
        ke[:, :PAIR] = k_ref[...]
        ke[:, PAIR:] = kf_ref[...]

    query = q_ref[...]
    lane = lax.broadcasted_iota(jnp.int32, query.shape, 1)
    scores = []
    for head in range(2):
        mine = (lane < HEAD) == (head == 0)
        wide = jnp.concatenate([jnp.where(mine, query, 0), qf_ref[...]], axis=1)
        scores.append(against(wide, ke[...]))
    mixed, logs = [], []
    for head in range(2):
        top = jnp.max(scores[head], axis=1, keepdims=True)
        weights = jnp.exp(scores[head] - top)
        total = jnp.sum(weights, axis=1, keepdims=True)
        got = jnp.dot(
            weights.astype(jnp.bfloat16), v_ref[...], preferred_element_type=jnp.float32
        )
        mixed.append(got / total)
        logs.append(top + jnp.log(total))
    dead = own_f_ref[:, SEQ_SLOTS : SEQ_SLOTS + 1].astype(jnp.float32) > 0.5
    result = jnp.where(lane < HEAD, mixed[0], mixed[1]).astype(jnp.bfloat16)
    out_ref[...] = jnp.where(dead, own_v_ref[...], result)
    stat = jnp.where(lane == 0, logs[0], jnp.where(lane == 1, logs[1], 0.0))
    stat_ref[...] = jnp.where(dead, 0.0, stat)


def block_rows(rows):
    return 512 if rows <= 2048 else 256


def attend(qkv, query_side, key_side):
    rows = qkv.shape[0]
    block = block_rows(rows)

    def some(part):
        return pl.BlockSpec((block, PAIR), lambda i: (i, part))

    def whole(part):
        return pl.BlockSpec((rows, PAIR), lambda i: (0, part))

    return pl.pallas_call(
        attend_kernel,
        grid=(rows // block,),
        in_specs=[some(0), whole(1), whole(2), some(0), whole(0), some(2), some(0)],
        out_specs=[some(0), some(0)],
        out_shape=[
            jax.ShapeDtypeStruct((rows, PAIR), jnp.bfloat16),
            jax.ShapeDtypeStruct((rows, PAIR), jnp.float32),
        ],
        scratch_shapes=[pltpu.VMEM((rows, 2 * PAIR), jnp.bfloat16)],
        compiler_params=compiler_params(),
        name="attend",
    )(qkv, qkv, qkv, query_side, key_side, qkv, key_side)


def in_three(column, lane):
    first = column.astype(jnp.bfloat16).astype(jnp.float32)
    second = (column - first).astype(jnp.bfloat16).astype(jnp.float32)
    third = column - first - second
    return jnp.where(
        lane == STAT_LANE,
        first,
        jnp.where(lane == STAT_LANE + 1, second, jnp.where(lane == STAT_LANE + 2, third, 0.0)),
    )


def attend_back_kernel(
    q_ref, k_ref, v_ref, qf_ref, kf_ref, stat_ref, att_ref, grad_ref, cos_ref, sin_ref,
    own_cos_ref, own_sin_ref, dq_ref, dk_ref, dv_ref, ke, ve, kt, dk_sum, dv_sum,
):
    @pl.when(pl.program_id(0) == 0)
    def _():
        ke[:, :PAIR] = k_ref[...]
        ke[:, PAIR:] = kf_ref[...]
        ve[:, :PAIR] = v_ref[...]
        ve[:, PAIR:] = kf_ref[...]
        kt[...] = k_ref[...].T
        dk_sum[...] = jnp.zeros_like(dk_sum)
        dv_sum[...] = jnp.zeros_like(dv_sum)

    query, grad = q_ref[...], grad_ref[...]
    lane = lax.broadcasted_iota(jnp.int32, query.shape, 1)
    both = grad.astype(jnp.float32) * att_ref[...].astype(jnp.float32)
    stat = stat_ref[...]
    query_heads, grad_heads, weights, grad_scores, turned_grads = [], [], [], [], []
    for head in range(2):
        mine = (lane < HEAD) == (head == 0)
        query_head = jnp.where(mine, query, 0)
        grad_head = jnp.where(mine, grad, 0)
        log_total = jnp.sum(jnp.where(lane == head, stat, 0.0), axis=1, keepdims=True)
        centre = jnp.sum(jnp.where(mine, both, 0.0), axis=1, keepdims=True)
        side = (qf_ref[...].astype(jnp.float32) - in_three(log_total, lane)).astype(jnp.bfloat16)
        wide = jnp.concatenate([query_head, side], axis=1)
        weight = jnp.exp(against(ke[...], wide))
        wide_grad = jnp.concatenate(
            [grad_head, (-in_three(centre, lane)).astype(jnp.bfloat16)], axis=1
        )
        grad_score = (weight * against(ve[...], wide_grad)).astype(jnp.bfloat16)
        weights.append(weight.astype(jnp.bfloat16))
        grad_scores.append(grad_score)
        query_heads.append(query_head)
        grad_heads.append(grad_head)
        turned_grads.append(jnp.dot(kt[...], grad_score, preferred_element_type=jnp.float32))
    dv_sum[...] += jnp.dot(
        jnp.concatenate(weights, axis=1),
        jnp.concatenate(grad_heads, axis=0),
        preferred_element_type=jnp.float32,
    )
    dk_sum[...] += jnp.dot(
        jnp.concatenate(grad_scores, axis=1),
        jnp.concatenate(query_heads, axis=0),
        preferred_element_type=jnp.float32,
    )
    row = lax.broadcasted_iota(jnp.int32, turned_grads[0].shape, 0)
    grad_query = jnp.where(row < HEAD, turned_grads[0], turned_grads[1]).T * HEAD ** (-0.5)
    dq_ref[...] = turned(grad_query, own_cos_ref[...], -own_sin_ref[...]).astype(jnp.bfloat16)

    @pl.when(pl.program_id(0) == pl.num_programs(0) - 1)
    def _():
        dk_ref[...] = turned(dk_sum[...], cos_ref[...], -sin_ref[...]).astype(jnp.bfloat16)
        dv_ref[...] = dv_sum[...].astype(jnp.bfloat16)


def attend_back(qkv, query_side, key_side, stat, attended, grad, cos, sin):
    rows = qkv.shape[0]
    block = block_rows(rows)

    def some(part):
        return pl.BlockSpec((block, PAIR), lambda i: (i, part))

    def whole(part):
        return pl.BlockSpec((rows, PAIR), lambda i: (0, part))

    out = jax.ShapeDtypeStruct((rows, PAIR), jnp.bfloat16)
    return pl.pallas_call(
        attend_back_kernel,
        grid=(rows // block,),
        in_specs=[
            some(0), whole(1), whole(2), some(0), whole(0), some(0), some(0), some(0),
            whole(0), whole(0), some(0), some(0),
        ],
        out_specs=[some(0), whole(0), whole(0)],
        out_shape=[out, out, out],
        scratch_shapes=[
            pltpu.VMEM((rows, 2 * PAIR), jnp.bfloat16),
            pltpu.VMEM((rows, 2 * PAIR), jnp.bfloat16),
            pltpu.VMEM((PAIR, rows), jnp.bfloat16),
            pltpu.VMEM((rows, PAIR), jnp.float32),
            pltpu.VMEM((rows, PAIR), jnp.float32),
        ],
        compiler_params=compiler_params(),
        name="attend_back",
    )(qkv, qkv, qkv, query_side, key_side, stat, attended, grad, cos, sin, cos, sin)


def product(left, right):
    return jnp.dot(left, right, preferred_element_type=jnp.float32)


def contract(left, right):
    return lax.dot_general(
        left, right, (((0,), (0,)), ((), ())), preferred_element_type=jnp.float32
    )


def against(left, right):
    return lax.dot_general(
        left, right, (((1,), (1,)), ((), ())), preferred_element_type=jnp.float32
    )


def own_half(array, core):
    half = array.shape[0] // 2
    return lax.dynamic_slice_in_dim(array, core * half, half)


def gather_weight(weight, core):
    return lax.all_gather(
        own_half(weight, core).astype(jnp.bfloat16), ("grp", "core"), axis=0, tiled=True
    )


def exchange(array, axis, mask, size):
    return lax.ppermute(array, axis, [(i, i ^ mask) for i in range(size)])


def pick(array, index, axis):
    return lax.dynamic_index_in_dim(array, index, axis, keepdims=False)


def halved(array, axis, mask, size, dim):
    bit = (lax.axis_index(axis) // mask) % 2
    got = exchange(pick(array, 1 - bit, dim), axis, mask, size)
    kept = pick(array, bit, dim)
    return (kept.astype(jnp.float32) + got.astype(jnp.float32)).astype(jnp.bfloat16)


def doubled(array, axis, mask, size, dim):
    bit = (lax.axis_index(axis) // mask) % 2
    got = exchange(array, axis, mask, size)
    low = jnp.where(bit == 0, array, got)
    high = jnp.where(bit == 0, got, array)
    return jnp.concatenate([low, high], axis=dim)


def scatter_rows(array, order, group):
    bits = group.bit_length() - 1
    rows, columns = array.shape[-2:]
    array = array.reshape((2,) * bits + (rows, columns))
    left = list(range(bits))
    for bit in order:
        place_of = left.index(bit)
        array = halved(array, "grp", 1 << (bits - 1 - bit), group, place_of)
        left.pop(place_of)
    return array


def reduce_weight(left, right, core, group, far):
    columns = right.shape[1] // 2
    theirs = lax.dynamic_slice_in_dim(right, (1 - core) * columns, columns, 1)
    mine = lax.dynamic_slice_in_dim(right, core * columns, columns, 1)
    sent = exchange(contract(left, theirs).astype(jnp.bfloat16), "core", 1, 2)
    share = (contract(left, mine) + sent.astype(jnp.float32)).astype(jnp.bfloat16)
    rows = share.shape[0] // group
    share = share.reshape(group, rows, columns)
    bits = group.bit_length() - 1
    forth = tuple(range(bits))
    share = jnp.concatenate(
        [
            scatter_rows(share[:, : rows // 2], forth, group),
            scatter_rows(share[:, rows // 2 :], forth[::-1], group),
        ],
        axis=0,
    )
    by_rows = rows % (16 * far) == 0
    dim = 0 if by_rows else 1
    masks = []
    mask = 1
    while mask < far:
        size = share.shape[dim]
        if size % 2 == 0 and (by_rows or size % (2 * PAIR) == 0):
            shape = share.shape
            split = (2, shape[0] // 2, shape[1]) if by_rows else (shape[0], 2, shape[1] // 2)
            share = halved(share.reshape(split), "far", mask, far, dim)
            masks.append(mask)
        else:
            got = exchange(share, "far", mask, far)
            share = (share.astype(jnp.float32) + got.astype(jnp.float32)).astype(jnp.bfloat16)
        mask *= 2
    for mask in masks[::-1]:
        share = doubled(share, "far", mask, far, dim)
    return doubled(share, "core", 1, 2, 1).astype(jnp.float32)


def spread_halves(array):
    spare = ((0, 0), (0, FF_WIDE - FF))
    return jnp.concatenate([jnp.pad(array[:, :FF], spare), jnp.pad(array[:, FF:], spare)], axis=1)


def joined_halves(array):
    return jnp.concatenate([array[:, :FF], array[:, FF_WIDE : FF_WIDE + FF]], axis=1)


def gated(gate, upward):
    return jax.nn.gelu(gate, approximate=False) * upward


def adam_update(weight, mean, square, grad, rate):
    mean_new = 0.9 * mean + 0.1 * grad
    square_new = 0.999 * square + 0.001 * grad * grad
    step_size = mean_new / (1.0 - 0.9**STEP) / (jnp.sqrt(square_new / (1.0 - 0.999**STEP)) + 1e-08)
    return (mean_new, square_new, weight - rate * (step_size + 0.01 * weight))


def local(
    group,
    far,
    tokens,
    slot_ids,
    cotangent,
    inproj,
    outproj,
    upproj,
    downproj,
    norm_gains,
    inproj_mean,
    outproj_mean,
    upproj_mean,
    downproj_mean,
    gains_mean,
    inproj_square,
    outproj_square,
    upproj_square,
    downproj_square,
    gains_square,
):
    me = lax.axis_index("grp")
    me_list = me.reshape(1).astype(jnp.int32)
    core = lax.axis_index("core")
    pairs = D // PAIR // group
    masters = (inproj, outproj, upproj, downproj, norm_gains)
    w_in = gather_weight(inproj, core)
    gains_low = lax.all_gather(norm_gains.astype(jnp.bfloat16), "grp", axis=0, tiled=True)
    w_out = gather_weight(outproj, core)
    w_up = gather_weight(spread_halves(upproj), core)
    w_down = gather_weight(downproj, core)
    gains = gains_low.astype(jnp.float32)
    all_ids = lax.all_gather(slot_ids, "grp", axis=1, tiled=True)[0]
    own_rows = tokens.shape[1]
    group_rows = all_ids.shape[0]
    order = me ^ jnp.arange(group, dtype=jnp.int32)
    near_ids = all_ids.reshape(group, own_rows)[order].reshape(group_rows)
    where_at = positions(all_ids).reshape(group, own_rows)[order].reshape(group_rows)
    cos, sin = pair_tables(where_at)
    query_side, key_side = slot_features(near_ids)
    live = (slot_ids[0] >= 0).astype(jnp.bfloat16)
    inputs = tokens[0].astype(jnp.float32)
    first_normed = layer_norm(inputs, gains[:, 0]).astype(jnp.bfloat16)
    cos_near = cos.reshape(group, own_rows, PAIR)
    sin_near = sin.reshape(group, own_rows, PAIR)
    qkv, stats, attended_near, attended_here = [], [], [], []
    for pair in range(pairs):
        pieces = project(me_list, first_normed, w_in, cos_near, sin_near, pair, group)
        qkv.append(swap_heads(pieces, group).reshape(group_rows, 3 * PAIR))
    for pair in range(pairs):
        mixed, stat = attend(qkv[pair], query_side, key_side)
        stats.append(stat)
        attended_near.append(mixed)
        attended_here.append(swap_heads(mixed.reshape(group, own_rows, PAIR), group))
    attended = place(me_list, attended_here, 1, group)
    middle = inputs + product(attended, w_out)
    second_normed = layer_norm(middle, gains[:, 1]).astype(jnp.bfloat16)
    gate_up = product(second_normed, w_up)
    gate = gate_up[:, :FF]
    upward = gate_up[:, FF_WIDE : FF_WIDE + FF]
    hidden = gated(gate, upward).astype(jnp.bfloat16)
    result = middle + product(hidden, w_down)
    grad_top = cotangent[0] * live[:, None]
    grad_hidden = against(grad_top, w_down)
    _, gate_back = jax.vjp(gated, gate, upward)
    grad_gate_up = spread_halves(jnp.concatenate(gate_back(grad_hidden), axis=1)).astype(
        jnp.bfloat16
    )
    grad_second = against(grad_gate_up, w_up)
    _, second_back = jax.vjp(lambda v: layer_norm(v, gains[:, 1]), middle)
    (grad_from_norm,) = second_back(grad_second)
    grad_middle = grad_top.astype(jnp.float32) + grad_from_norm
    grad_branch = grad_middle.astype(jnp.bfloat16)
    total_down = reduce_weight(hidden, grad_top, core, group, far)
    total_up = joined_halves(reduce_weight(second_normed, grad_gate_up, core, group, far))
    pieces_here = []
    for pair in range(pairs):
        sent = row_product(me_list, grad_branch, w_out, pair, group)
        grad_near = swap_heads(sent, group).reshape(group_rows, PAIR)
        grads = attend_back(
            qkv[pair], query_side, key_side, stats[pair], attended_near[pair], grad_near, cos, sin
        )
        joined = jnp.concatenate(grads, axis=1).reshape(group, own_rows, 3 * PAIR)
        pieces_here.append(swap_heads(joined, group))
    total_out = reduce_weight(attended, grad_branch, core, group, far)
    grad_projected = place(me_list, pieces_here, 3, group)
    total_in = reduce_weight(first_normed, grad_projected, core, group, far)
    grad_first = against(grad_projected, w_in)
    _, first_back = jax.vjp(lambda v: layer_norm(v, gains[:, 0]), inputs)
    (grad_inputs,) = first_back(grad_first)
    input_grad = (grad_middle + grad_inputs).astype(jnp.bfloat16)
    low_in = inproj.astype(jnp.bfloat16).astype(jnp.float32)
    low_up = upproj.astype(jnp.bfloat16).astype(jnp.float32)
    low_gains = norm_gains.astype(jnp.bfloat16).astype(jnp.float32)
    total_gains = (
        jnp.stack([jnp.sum(low_in * total_in, axis=1), jnp.sum(low_up * total_up, axis=1)], axis=1)
        / low_gains
    )
    totals = (total_in, total_out, total_up, total_down, total_gains)
    means = (inproj_mean, outproj_mean, upproj_mean, downproj_mean, gains_mean)
    squares = (inproj_square, outproj_square, upproj_square, downproj_square, gains_square)
    updates = [
        adam_update(masters[index], means[index], squares[index], totals[index], rate_list[index])
        for index in range(5)
    ]
    return (
        result.astype(jnp.bfloat16)[None],
        input_grad[None],
        updates[0][0],
        updates[0][1],
        updates[0][2],
        updates[1][0],
        updates[1][1],
        updates[1][2],
        updates[2][0],
        updates[2][1],
        updates[2][2],
        updates[3][0],
        updates[3][1],
        updates[3][2],
        updates[4][0],
        updates[4][1],
        updates[4][2],
    )


def solution(mesh):
    group_size, replicas = mesh.devices.shape
    fine = Mesh(mesh.devices.reshape(group_size, replicas // 2, 2), ("grp", "far", "core"))
    placed = (
        P(("far", "core"), "grp", None),
        P(("far", "core"), "grp"),
        P(("far", "core"), "grp", None),
        P("grp", None),
        P("grp", None),
        P("grp", None),
        P("grp", None),
        P("grp", None),
        P("grp", None),
        P("grp", None),
        P("grp", None),
        P("grp", None),
        P("grp", None),
        P("grp", None),
        P("grp", None),
        P("grp", None),
        P("grp", None),
        P("grp", None),
    )
    return jax.shard_map(
        functools.partial(local, group_size, replicas // 2),
        mesh=fine,
        in_specs=placed,
        out_specs=(
            P(("far", "core"), "grp", None),
            P(("far", "core"), "grp", None),
            P("grp", None),
            P("grp", None),
            P("grp", None),
            P("grp", None),
            P("grp", None),
            P("grp", None),
            P("grp", None),
            P("grp", None),
            P("grp", None),
            P("grp", None),
            P("grp", None),
            P("grp", None),
            P("grp", None),
            P("grp", None),
            P("grp", None),
        ),
        check_vma=False,
    )
```

```python
import functools

import jax
import jax.numpy as jnp
from jax import lax
from jax.experimental import pallas as pl
from jax.experimental.pallas import tpu as pltpu
from jax.sharding import Mesh, PartitionSpec as P

D = 1024
HEADS = 16
HEAD = 64
FF = 2624
FF_WIDE = 2688
STEP = 10
SEQ_SLOTS = 9
PAIR = 128
STAT_LANE = 16
VMEM_BYTES = 56 * 1024 * 1024


rope_base = 160000.0
norm_eps = 1e-05
rate_list = (0.1, 0.4, 0.08, 0.05, 0.6)


def layer_norm(values, gain):
    centred = values - jnp.mean(values, axis=-1, keepdims=True)
    spread = jnp.mean(centred * centred, axis=-1, keepdims=True)
    return centred * lax.rsqrt(spread + norm_eps) * gain


def positions(ids):
    live = ids >= 0
    counted = jnp.cumsum(live.astype(jnp.int32)) - 1
    onehot = (
        (ids[:, None] == jnp.arange(SEQ_SLOTS, dtype=jnp.int32)[None, :]) & live[:, None]
    ).astype(jnp.int32)
    counts = jnp.sum(onehot, axis=0)
    starts = jnp.cumsum(counts) - counts
    first = jnp.sum(onehot * starts[None, :], axis=1)
    return jnp.where(live, counted - first, 0)


def pair_tables(where_at):
    lane = jnp.arange(PAIR, dtype=jnp.int32)
    order = (lane % (HEAD // 2)).astype(jnp.float32)
    inverse = rope_base ** (-(order * 2.0 / HEAD))
    angles = where_at.astype(jnp.float32)[:, None] * inverse[None, :]
    signs = jnp.where(lane % HEAD < HEAD // 2, -1.0, 1.0)
    return jnp.cos(angles), jnp.sin(angles) * signs[None, :]


def slot_features(ids):
    lane = jnp.arange(PAIR, dtype=jnp.int32)[None, :]
    column = jnp.where(ids < 0, SEQ_SLOTS, ids)[:, None]
    own = lane == column
    query_side = jnp.where((lane <= SEQ_SLOTS) & (~own | (ids < 0)[:, None]), -1e30, 0.0)
    key_side = jnp.where(own | ((lane >= STAT_LANE) & (lane < STAT_LANE + 3)), 1.0, 0.0)
    return query_side.astype(jnp.bfloat16), key_side.astype(jnp.bfloat16)


def turned(values, cos, sin):
    lane = lax.broadcasted_iota(jnp.int32, values.shape, 1)
    half = HEAD // 2
    other = jnp.where(
        lane % HEAD < half, pltpu.roll(values, PAIR - half, 1), pltpu.roll(values, half, 1)
    )
    return values * cos + other * sin


def compiler_params():
    return pltpu.CompilerParams(vmem_limit_bytes=VMEM_BYTES)


def project_kernel(me_ref, x_ref, wq_ref, wk_ref, wv_ref, cos_ref, sin_ref, out_ref):
    weights = jnp.concatenate([wq_ref[...], wk_ref[...], wv_ref[...]], axis=1)
    got = jnp.dot(x_ref[...], weights, preferred_element_type=jnp.float32)
    cos, sin = cos_ref[0], sin_ref[0]
    query = turned(got[:, :PAIR], cos, sin) * HEAD ** (-0.5)
    keys = turned(got[:, PAIR : 2 * PAIR], cos, sin)
    out_ref[0, :, :PAIR] = query.astype(jnp.bfloat16)
    out_ref[0, :, PAIR : 2 * PAIR] = keys.astype(jnp.bfloat16)
    out_ref[0, :, 2 * PAIR :] = got[:, 2 * PAIR :].astype(jnp.bfloat16)


def skipping(kernel, before, extra):
    def body(*refs):
        kernel(*refs[:before], *refs[before + extra :])

    return body


def untouched(after):
    return [pl.BlockSpec(memory_space=pl.ANY)] * len(after)


def project(me, first_normed, w_pair, cos, sin, group):
    rows = first_normed.shape[0]

    def column(part):
        return lambda d, me: (0, part * group + (me[0] ^ d))

    return pl.pallas_call(
        project_kernel,
        grid_spec=pltpu.PrefetchScalarGridSpec(
            num_scalar_prefetch=1,
            grid=(group,),
            in_specs=[
                pl.BlockSpec((rows, D), lambda d, me: (0, 0)),
                pl.BlockSpec((D, PAIR), column(0)),
                pl.BlockSpec((D, PAIR), column(1)),
                pl.BlockSpec((D, PAIR), column(2)),
                pl.BlockSpec((1, rows, PAIR), lambda d, me: (0, 0, 0)),
                pl.BlockSpec((1, rows, PAIR), lambda d, me: (0, 0, 0)),
            ],
            out_specs=pl.BlockSpec((1, rows, 3 * PAIR), lambda d, me: (d, 0, 0)),
        ),
        out_shape=jax.ShapeDtypeStruct((group, rows, 3 * PAIR), jnp.bfloat16),
        compiler_params=compiler_params(),
        name="project",
    )(me, first_normed, w_pair, w_pair, w_pair, cos, sin)


def row_product_kernel(me_ref, x_ref, w_ref, out_ref):
    out_ref[0] = against(x_ref[...], w_ref[...]).astype(jnp.bfloat16)


def row_product(me, left, weight, pair, group, after=()):
    rows = left.shape[0]
    pairs = D // PAIR // group
    return pl.pallas_call(
        skipping(row_product_kernel, 3, len(after)),
        grid_spec=pltpu.PrefetchScalarGridSpec(
            num_scalar_prefetch=1,
            grid=(group,),
            in_specs=[
                pl.BlockSpec((rows, D), lambda d, me: (0, 0)),
                pl.BlockSpec((PAIR, D), lambda d, me: ((me[0] ^ d) * pairs + pair, 0)),
                *untouched(after),
            ],
            out_specs=pl.BlockSpec((1, rows, PAIR), lambda d, me: (d, 0, 0)),
        ),
        out_shape=jax.ShapeDtypeStruct((group, rows, PAIR), jnp.bfloat16),
        compiler_params=compiler_params(),
        name="row_product",
    )(me, left, weight, *after)


def run_copies(pairs_of, sems):
    copies = [
        pltpu.make_async_copy(source, target, sems.at[index])
        for index, (source, target) in enumerate(pairs_of)
    ]
    for copy in copies:
        copy.start()
    for copy in copies:
        copy.wait()


def place(me, pieces, parts, group, after=()):
    rows = pieces[0][0].shape[0]
    pairs = len(pieces)
    flat = [piece for near in pieces for piece in near]

    def kernel(me_ref, *refs):
        out_ref, sems = refs[len(flat) + len(after) :]
        moves = []
        for pair in range(pairs):
            for step in range(group):
                owner = me_ref[0] ^ step
                for part in range(parts):
                    column = ((part * group + owner) * pairs + pair) * PAIR
                    moves.append(
                        (
                            refs[pair * group + step].at[:, part * PAIR : (part + 1) * PAIR],
                            out_ref.at[:, pl.ds(pl.multiple_of(column, PAIR), PAIR)],
                        )
                    )
        run_copies(moves, sems)

    return pl.pallas_call(
        kernel,
        in_specs=[pl.BlockSpec(memory_space=pltpu.SMEM)] + untouched(flat) + untouched(after),
        out_specs=pl.BlockSpec(memory_space=pl.ANY),
        out_shape=jax.ShapeDtypeStruct((rows, parts * group * pairs * PAIR), jnp.bfloat16),
        scratch_shapes=[pltpu.SemaphoreType.DMA((len(flat) * parts,))],
        compiler_params=compiler_params(),
        name="place",
    )(me, *flat, *after)


def exchange(array, axis, mask, size):
    return lax.ppermute(array, axis, [(i, i ^ mask) for i in range(size)])


def swap_heads(pieces, group):
    return [pieces[0]] + [exchange(pieces[d], "grp", d, group) for d in range(1, group)]


def gather_rows(half, me_core, group):
    if group != 4:
        return lax.all_gather(half, ("grp", "core"), axis=0, tiled=True)
    rows, columns = half.shape
    middle = rows // 2
    first = exchange(half, "grp", 1, group)
    second = exchange(half, "grp", 2, group)
    upper = exchange(second[:middle], "grp", 1, group)
    lower = exchange(first[middle:], "grp", 2, group)
    got = [half, first, second, upper, lower]
    got += [exchange(piece, "core", 1, 2) for piece in got]

    def kernel(index_ref, *refs):
        out_ref, sems = refs[len(got) :]
        moves = []
        for side in range(2):
            core = index_ref[1] ^ side
            for slot, (step, offset) in enumerate(((0, 0), (1, 0), (2, 0), (3, 0), (3, middle))):
                row = ((index_ref[0] ^ step) * 2 + core) * rows + offset
                source = refs[side * 5 + slot]
                moves.append(
                    (source, out_ref.at[pl.ds(pl.multiple_of(row, middle), source.shape[0])])
                )
        run_copies(moves, sems)

    return pl.pallas_call(
        kernel,
        in_specs=[pl.BlockSpec(memory_space=pltpu.SMEM)] + untouched(got),
        out_specs=pl.BlockSpec(memory_space=pl.ANY),
        out_shape=jax.ShapeDtypeStruct((2 * group * rows, columns), jnp.bfloat16),
        scratch_shapes=[pltpu.SemaphoreType.DMA((len(got),))],
        compiler_params=compiler_params(),
        name="gather_rows",
    )(me_core, *got)


def attend_kernel(q_ref, k_ref, v_ref, qf_ref, kf_ref, own_v_ref, own_f_ref, out_ref, stat_ref, ke):
    @pl.when(pl.program_id(0) == 0)
    def _():
        ke[:, :PAIR] = k_ref[...]
        ke[:, PAIR:] = kf_ref[...]

    query = q_ref[...]
    lane = lax.broadcasted_iota(jnp.int32, query.shape, 1)
    scores = []
    for head in range(2):
        mine = (lane < HEAD) == (head == 0)
        wide = jnp.concatenate([jnp.where(mine, query, 0), qf_ref[...]], axis=1)
        scores.append(against(wide, ke[...]))
    mixed, logs = [], []
    for head in range(2):
        top = jnp.max(scores[head], axis=1, keepdims=True)
        weights = jnp.exp(scores[head] - top)
        total = jnp.sum(weights, axis=1, keepdims=True)
        got = jnp.dot(
            weights.astype(jnp.bfloat16), v_ref[...], preferred_element_type=jnp.float32
        )
        mixed.append(got / total)
        logs.append(top + jnp.log(total))
    dead = own_f_ref[:, SEQ_SLOTS : SEQ_SLOTS + 1].astype(jnp.float32) > 0.5
    result = jnp.where(lane < HEAD, mixed[0], mixed[1]).astype(jnp.bfloat16)
    out_ref[...] = jnp.where(dead, own_v_ref[...], result)
    stat = jnp.where(lane == 0, logs[0], jnp.where(lane == 1, logs[1], 0.0))
    stat_ref[...] = jnp.where(dead, 0.0, stat)


def block_rows(rows):
    return 512 if rows <= 2048 else 256


def attend(qkv, query_side, key_side):
    rows = qkv.shape[0]
    block = block_rows(rows)

    def some(part):
        return pl.BlockSpec((block, PAIR), lambda i: (i, part))

    def whole(part):
        return pl.BlockSpec((rows, PAIR), lambda i: (0, part))

    return pl.pallas_call(
        attend_kernel,
        grid=(rows // block,),
        in_specs=[some(0), whole(1), whole(2), some(0), whole(0), some(2), some(0)],
        out_specs=[some(0), some(0)],
        out_shape=[
            jax.ShapeDtypeStruct((rows, PAIR), jnp.bfloat16),
            jax.ShapeDtypeStruct((rows, PAIR), jnp.float32),
        ],
        scratch_shapes=[pltpu.VMEM((rows, 2 * PAIR), jnp.bfloat16)],
        compiler_params=compiler_params(),
        name="attend",
    )(qkv, qkv, qkv, query_side, key_side, qkv, key_side)


def in_three(column, lane):
    first = column.astype(jnp.bfloat16).astype(jnp.float32)
    second = (column - first).astype(jnp.bfloat16).astype(jnp.float32)
    third = column - first - second
    return jnp.where(
        lane == STAT_LANE,
        first,
        jnp.where(lane == STAT_LANE + 1, second, jnp.where(lane == STAT_LANE + 2, third, 0.0)),
    )


def attend_back_kernel(
    q_ref, k_ref, v_ref, qf_ref, kf_ref, stat_ref, att_ref, grad_ref, cos_ref, sin_ref,
    own_cos_ref, own_sin_ref, out_ref, ke, ve, kt, dk_sum, dv_sum,
):
    @pl.when(pl.program_id(0) == 0)
    def _():
        ke[:, :PAIR] = k_ref[...]
        ke[:, PAIR:] = kf_ref[...]
        ve[:, :PAIR] = v_ref[...]
        ve[:, PAIR:] = kf_ref[...]
        kt[...] = k_ref[...].T
        dk_sum[...] = jnp.zeros_like(dk_sum)
        dv_sum[...] = jnp.zeros_like(dv_sum)

    query, grad = q_ref[...], grad_ref[...]
    lane = lax.broadcasted_iota(jnp.int32, query.shape, 1)
    both = grad.astype(jnp.float32) * att_ref[...].astype(jnp.float32)
    stat = stat_ref[...]
    query_heads, grad_heads, weights, grad_scores, turned_grads = [], [], [], [], []
    for head in range(2):
        mine = (lane < HEAD) == (head == 0)
        query_head = jnp.where(mine, query, 0)
        grad_head = jnp.where(mine, grad, 0)
        log_total = jnp.sum(jnp.where(lane == head, stat, 0.0), axis=1, keepdims=True)
        centre = jnp.sum(jnp.where(mine, both, 0.0), axis=1, keepdims=True)
        side = (qf_ref[...].astype(jnp.float32) - in_three(log_total, lane)).astype(jnp.bfloat16)
        wide = jnp.concatenate([query_head, side], axis=1)
        weight = jnp.exp(against(ke[...], wide))
        wide_grad = jnp.concatenate(
            [grad_head, (-in_three(centre, lane)).astype(jnp.bfloat16)], axis=1
        )
        grad_score = (weight * against(ve[...], wide_grad)).astype(jnp.bfloat16)
        weights.append(weight.astype(jnp.bfloat16))
        grad_scores.append(grad_score)
        query_heads.append(query_head)
        grad_heads.append(grad_head)
        turned_grads.append(jnp.dot(kt[...], grad_score, preferred_element_type=jnp.float32))
    dv_sum[...] += jnp.dot(
        jnp.concatenate(weights, axis=1),
        jnp.concatenate(grad_heads, axis=0),
        preferred_element_type=jnp.float32,
    )
    dk_sum[...] += jnp.dot(
        jnp.concatenate(grad_scores, axis=1),
        jnp.concatenate(query_heads, axis=0),
        preferred_element_type=jnp.float32,
    )
    row = lax.broadcasted_iota(jnp.int32, turned_grads[0].shape, 0)
    grad_query = jnp.where(row < HEAD, turned_grads[0], turned_grads[1]).T * HEAD ** (-0.5)
    block = query.shape[0]
    own = pl.ds(pl.multiple_of(pl.program_id(0) * block, block), block)
    out_ref[own, :PAIR] = turned(grad_query, own_cos_ref[...], -own_sin_ref[...]).astype(
        jnp.bfloat16
    )

    @pl.when(pl.program_id(0) == pl.num_programs(0) - 1)
    def _():
        out_ref[:, PAIR : 2 * PAIR] = turned(dk_sum[...], cos_ref[...], -sin_ref[...]).astype(
            jnp.bfloat16
        )
        out_ref[:, 2 * PAIR :] = dv_sum[...].astype(jnp.bfloat16)


def attend_back(qkv, query_side, key_side, stat, attended, grad, cos, sin, after=()):
    rows = qkv.shape[0]
    block = block_rows(rows)

    def some(part):
        return pl.BlockSpec((block, PAIR), lambda i: (i, part))

    def whole(part):
        return pl.BlockSpec((rows, PAIR), lambda i: (0, part))

    return pl.pallas_call(
        skipping(attend_back_kernel, 12, len(after)),
        grid=(rows // block,),
        in_specs=[
            some(0), whole(1), whole(2), some(0), whole(0), some(0), some(0), some(0),
            whole(0), whole(0), some(0), some(0), *untouched(after),
        ],
        out_specs=pl.BlockSpec((rows, 3 * PAIR), lambda i: (0, 0)),
        out_shape=jax.ShapeDtypeStruct((rows, 3 * PAIR), jnp.bfloat16),
        scratch_shapes=[
            pltpu.VMEM((rows, 2 * PAIR), jnp.bfloat16),
            pltpu.VMEM((rows, 2 * PAIR), jnp.bfloat16),
            pltpu.VMEM((PAIR, rows), jnp.bfloat16),
            pltpu.VMEM((rows, PAIR), jnp.float32),
            pltpu.VMEM((rows, PAIR), jnp.float32),
        ],
        compiler_params=compiler_params(),
        name="attend_back",
    )(qkv, qkv, qkv, query_side, key_side, stat, attended, grad, cos, sin, cos, sin, *after)


def product(left, right):
    return jnp.dot(left, right, preferred_element_type=jnp.float32)


def contract(left, right):
    return lax.dot_general(
        left, right, (((0,), (0,)), ((), ())), preferred_element_type=jnp.float32
    )


def against(left, right):
    return lax.dot_general(
        left, right, (((1,), (1,)), ((), ())), preferred_element_type=jnp.float32
    )


def own_half(array, core):
    half = array.shape[0] // 2
    return lax.dynamic_slice_in_dim(array, core * half, half)


def gather_weight(weight, core):
    return lax.all_gather(
        own_half(weight, core).astype(jnp.bfloat16), ("grp", "core"), axis=0, tiled=True
    )


def pick(array, index, axis):
    return lax.dynamic_index_in_dim(array, index, axis, keepdims=False)


def added(*terms):
    return sum(term.astype(jnp.float32) for term in terms).astype(jnp.bfloat16)


def halved(array, mask, group, dim):
    bit = (lax.axis_index("grp") // mask) % 2
    got = exchange(pick(array, 1 - bit, dim), "grp", mask, group)
    return added(pick(array, bit, dim), got)


def core_sum(left, right, core):
    columns = right.shape[1] // 2
    theirs = lax.dynamic_slice_in_dim(right, (1 - core) * columns, columns, 1)
    mine = lax.dynamic_slice_in_dim(right, core * columns, columns, 1)
    sent = exchange(contract(left, theirs).astype(jnp.bfloat16), "core", 1, 2)
    return (contract(left, mine) + sent.astype(jnp.float32)).astype(jnp.bfloat16)


def group_first(share, group):
    rows, columns = share.shape[0] // group, share.shape[1]
    if group != 4:
        return (lax.psum_scatter(share, "grp", scatter_dimension=0, tiled=True),)
    share = share.reshape(2, 2, rows, columns)
    return (
        halved(share[:, :, : rows // 2], 2, group, 0),
        halved(share[:, :, rows // 2 :], 1, group, 1),
    )


def group_second(halves, group):
    if group != 4:
        return halves[0]
    return jnp.concatenate([halved(halves[0], 1, group, 0), halved(halves[1], 2, group, 0)], axis=0)


def far_scatter(share, far):
    if far > 4:
        return lax.psum(share, "far")
    rows, columns = share.shape
    own = lax.axis_index("far")
    if rows % (16 * far) == 0:
        chunk = rows // far
        pieces = [lax.dynamic_slice_in_dim(share, (own ^ d) * chunk, chunk, 0) for d in range(far)]
    else:
        chunk = columns // far
        pieces = [lax.dynamic_slice_in_dim(share, (own ^ d) * chunk, chunk, 1) for d in range(far)]
    return added(pieces[0], *[exchange(pieces[d], "far", d, far) for d in range(1, far)])


def far_gather(chunk, rows, far):
    if far > 4:
        return chunk
    pieces = [chunk] + [exchange(chunk, "far", d, far) for d in range(1, far)]
    own = lax.axis_index("far")
    mask = 1
    while mask < far:
        swap = (own // mask) % 2 == 1
        pieces = [jnp.where(swap, pieces[j ^ mask], pieces[j]) for j in range(far)]
        mask *= 2
    return jnp.concatenate(pieces, axis=0 if rows % (16 * far) == 0 else 1)


def finished(chunk, rows, core, far):
    share = far_gather(chunk, rows, far)
    other = exchange(share, "core", 1, 2)
    low = jnp.where(core == 0, share, other)
    high = jnp.where(core == 0, other, share)
    return jnp.concatenate([low, high], axis=1).astype(jnp.float32)


def pair_columns(weight, pair, pairs):
    blocks = range(pair, weight.shape[1] // PAIR, pairs)
    return jnp.concatenate([weight[:, j * PAIR : (j + 1) * PAIR] for j in blocks], axis=1)


def merged_columns(parts):
    pairs = len(parts)
    blocks = range(pairs * parts[0].shape[1] // PAIR)
    return jnp.concatenate(
        [parts[j % pairs][:, j // pairs * PAIR : (j // pairs + 1) * PAIR] for j in blocks], axis=1
    )


def spread_halves(array):
    spare = ((0, 0), (0, FF_WIDE - FF))
    return jnp.concatenate([jnp.pad(array[:, :FF], spare), jnp.pad(array[:, FF:], spare)], axis=1)


def joined_halves(array):
    return jnp.concatenate([array[:, :FF], array[:, FF_WIDE : FF_WIDE + FF]], axis=1)


def gated(gate, upward):
    return jax.nn.gelu(gate, approximate=False) * upward


def adam_update(weight, mean, square, grad, rate):
    mean_new = 0.9 * mean + 0.1 * grad
    square_new = 0.999 * square + 0.001 * grad * grad
    step_size = mean_new / (1.0 - 0.9**STEP) / (jnp.sqrt(square_new / (1.0 - 0.999**STEP)) + 1e-08)
    return (mean_new, square_new, weight - rate * (step_size + 0.01 * weight))


def local(
    group,
    far,
    tokens,
    slot_ids,
    cotangent,
    inproj,
    outproj,
    upproj,
    downproj,
    norm_gains,
    inproj_mean,
    outproj_mean,
    upproj_mean,
    downproj_mean,
    gains_mean,
    inproj_square,
    outproj_square,
    upproj_square,
    downproj_square,
    gains_square,
):
    me = lax.axis_index("grp")
    core = lax.axis_index("core")
    me_list = me.reshape(1).astype(jnp.int32)
    me_core = jnp.stack([me, core]).astype(jnp.int32)
    pairs = D // PAIR // group
    masters = (inproj, outproj, upproj, downproj, norm_gains)
    own_rows = tokens.shape[1]
    own_gains = norm_gains.shape[0]
    w_pairs = [
        gather_rows(
            own_half(pair_columns(inproj, pair, pairs), core).astype(jnp.bfloat16), me_core, group
        )
        for pair in range(pairs)
    ]
    w_up = gather_weight(spread_halves(upproj), core)
    w_down = gather_weight(downproj, core)
    w_out = gather_rows(own_half(outproj, core).astype(jnp.bfloat16), me_core, group)
    packed = jnp.concatenate([norm_gains[:, 0], norm_gains[:, 1], slot_ids[0].astype(jnp.float32)])
    packed = lax.all_gather(packed.astype(jnp.bfloat16), "grp", axis=0, tiled=False)
    gain_one = packed[:, :own_gains].reshape(D).astype(jnp.float32)
    gain_two = packed[:, own_gains : 2 * own_gains].reshape(D).astype(jnp.float32)
    all_ids = packed[:, 2 * own_gains :].astype(jnp.int32).reshape(group * own_rows)
    group_rows = all_ids.shape[0]
    order = me ^ jnp.arange(group, dtype=jnp.int32)
    near_ids = all_ids.reshape(group, own_rows)[order].reshape(group_rows)
    where_at = positions(all_ids).reshape(group, own_rows)[order].reshape(group_rows)
    cos, sin = pair_tables(where_at)
    query_side, key_side = slot_features(near_ids)
    live = (slot_ids[0] >= 0).astype(jnp.bfloat16)
    inputs = tokens[0].astype(jnp.float32)
    first_normed = layer_norm(inputs, gain_one).astype(jnp.bfloat16)
    cos_near = cos.reshape(group, own_rows, PAIR)
    sin_near = sin.reshape(group, own_rows, PAIR)
    qkv, stats, attended_near, attended_here = [], [], [], []
    for pair in range(pairs):
        pieces = project(me_list, first_normed, w_pairs[pair], cos_near, sin_near, group)
        qkv.append(jnp.concatenate(swap_heads(pieces, group), axis=0))
    for pair in range(pairs):
        mixed, stat = attend(qkv[pair], query_side, key_side)
        stats.append(stat)
        attended_near.append(mixed)
        attended_here.append(swap_heads(mixed.reshape(group, own_rows, PAIR), group))
    attended = place(me_list, attended_here, 1, group)
    middle = inputs + product(attended, w_out)
    second_normed = layer_norm(middle, gain_two).astype(jnp.bfloat16)
    gate_up = product(second_normed, w_up)
    gate = gate_up[:, :FF]
    upward = gate_up[:, FF_WIDE : FF_WIDE + FF]
    hidden = gated(gate, upward).astype(jnp.bfloat16)
    result = middle + product(hidden, w_down)
    grad_top = cotangent[0] * live[:, None]
    grad_hidden = against(grad_top, w_down)
    _, gate_back = jax.vjp(gated, gate, upward)
    grad_gate_up = spread_halves(jnp.concatenate(gate_back(grad_hidden), axis=1)).astype(
        jnp.bfloat16
    )
    grad_second = against(grad_gate_up, w_up)
    _, second_back = jax.vjp(lambda v: layer_norm(v, gain_two), middle)
    (grad_from_norm,) = second_back(grad_second)
    grad_middle = grad_top.astype(jnp.float32) + grad_from_norm
    grad_branch = grad_middle.astype(jnp.bfloat16)
    down_rows, up_rows, out_rows = downproj.shape[0], upproj.shape[0], outproj.shape[0]
    down_share = core_sum(hidden, grad_top, core)
    up_share = core_sum(second_normed, grad_gate_up, core)
    grad_near = []
    for pair in range(pairs):
        sent = row_product(
            me_list, grad_branch, w_out, pair, group, (down_share,) if pair == 0 else ()
        )
        grad_near.append(jnp.concatenate(swap_heads(sent, group), axis=0))
    down_halves = group_first(down_share, group)
    out_share = core_sum(attended, grad_branch, core)
    waits = [(*down_halves, up_share)]
    down_half = group_second(down_halves, group)
    up_halves = group_first(up_share, group)
    waits.append((down_half, *up_halves, out_share))
    grads_here = []
    for pair in range(pairs):
        grads = attend_back(
            qkv[pair], query_side, key_side, stats[pair], attended_near[pair], grad_near[pair],
            cos, sin, waits[pair],
        )
        grads_here.append(swap_heads(grads.reshape(group, own_rows, 3 * PAIR), group))
    up_half = group_second(up_halves, group)
    down_chunk = far_scatter(down_half, far)
    out_halves = group_first(out_share, group)
    waits = [(down_chunk, *out_halves), ()]
    in_shares, grad_first = [], 0.0
    for pair in range(pairs):
        grad_projected = place(me_list, [grads_here[pair]], 3, group, waits[pair])
        in_shares.append(core_sum(first_normed, grad_projected, core))
        grad_first = grad_first + against(grad_projected, w_pairs[pair])
    up_chunk = far_scatter(up_half, far)
    out_chunk = far_scatter(group_second(out_halves, group), far)
    in_chunks = [
        far_scatter(group_second(group_first(share, group), group), far) for share in in_shares
    ]
    total_down = finished(down_chunk, down_rows, core, far)
    total_up = joined_halves(finished(up_chunk, up_rows, core, far))
    total_out = finished(out_chunk, out_rows, core, far)
    total_in = merged_columns([finished(chunk, inproj.shape[0], core, far) for chunk in in_chunks])
    _, first_back = jax.vjp(lambda v: layer_norm(v, gain_one), inputs)
    (grad_inputs,) = first_back(grad_first)
    input_grad = (grad_middle + grad_inputs).astype(jnp.bfloat16)
    low_in = inproj.astype(jnp.bfloat16).astype(jnp.float32)
    low_up = upproj.astype(jnp.bfloat16).astype(jnp.float32)
    low_gains = norm_gains.astype(jnp.bfloat16).astype(jnp.float32)
    total_gains = (
        jnp.stack([jnp.sum(low_in * total_in, axis=1), jnp.sum(low_up * total_up, axis=1)], axis=1)
        / low_gains
    )
    totals = (total_in, total_out, total_up, total_down, total_gains)
    means = (inproj_mean, outproj_mean, upproj_mean, downproj_mean, gains_mean)
    squares = (inproj_square, outproj_square, upproj_square, downproj_square, gains_square)
    updates = [
        adam_update(masters[index], means[index], squares[index], totals[index], rate_list[index])
        for index in range(5)
    ]
    return (
        result.astype(jnp.bfloat16)[None],
        input_grad[None],
        updates[0][0],
        updates[0][1],
        updates[0][2],
        updates[1][0],
        updates[1][1],
        updates[1][2],
        updates[2][0],
        updates[2][1],
        updates[2][2],
        updates[3][0],
        updates[3][1],
        updates[3][2],
        updates[4][0],
        updates[4][1],
        updates[4][2],
    )


def solution(mesh):
    group_size, replicas = mesh.devices.shape
    fine = Mesh(mesh.devices.reshape(group_size, replicas // 2, 2), ("grp", "far", "core"))
    placed = (
        P(("far", "core"), "grp", None),
        P(("far", "core"), "grp"),
        P(("far", "core"), "grp", None),
        P("grp", None),
        P("grp", None),
        P("grp", None),
        P("grp", None),
        P("grp", None),
        P("grp", None),
        P("grp", None),
        P("grp", None),
        P("grp", None),
        P("grp", None),
        P("grp", None),
        P("grp", None),
        P("grp", None),
        P("grp", None),
        P("grp", None),
    )
    return jax.shard_map(
        functools.partial(local, group_size, replicas // 2),
        mesh=fine,
        in_specs=placed,
        out_specs=(
            P(("far", "core"), "grp", None),
            P(("far", "core"), "grp", None),
            P("grp", None),
            P("grp", None),
            P("grp", None),
            P("grp", None),
            P("grp", None),
            P("grp", None),
            P("grp", None),
            P("grp", None),
            P("grp", None),
            P("grp", None),
            P("grp", None),
            P("grp", None),
            P("grp", None),
            P("grp", None),
            P("grp", None),
        ),
        check_vma=False,
    )
```

```python
import functools

import jax
import jax.numpy as jnp
from jax import lax
from jax.experimental import pallas as pl
from jax.experimental.pallas import tpu as pltpu
from jax.sharding import Mesh, PartitionSpec as P

D = 1024
HEADS = 16
HEAD = 64
FF = 2624
FF_WIDE = 2688
STEP = 10
SEQ_SLOTS = 9
PAIR = 128
STAT_LANE = 16
VMEM_BYTES = 56 * 1024 * 1024


rope_base = 160000.0
norm_eps = 1e-05
rate_list = (0.1, 0.4, 0.08, 0.05, 0.6)


def layer_norm(values, gain):
    centred = values - jnp.mean(values, axis=-1, keepdims=True)
    spread = jnp.mean(centred * centred, axis=-1, keepdims=True)
    return centred * lax.rsqrt(spread + norm_eps) * gain


def positions(ids):
    live = ids >= 0
    counted = jnp.cumsum(live.astype(jnp.int32)) - 1
    onehot = (
        (ids[:, None] == jnp.arange(SEQ_SLOTS, dtype=jnp.int32)[None, :]) & live[:, None]
    ).astype(jnp.int32)
    counts = jnp.sum(onehot, axis=0)
    starts = jnp.cumsum(counts) - counts
    first = jnp.sum(onehot * starts[None, :], axis=1)
    return jnp.where(live, counted - first, 0)


def pair_tables(where_at):
    lane = jnp.arange(PAIR, dtype=jnp.int32)
    order = (lane % (HEAD // 2)).astype(jnp.float32)
    inverse = rope_base ** (-(order * 2.0 / HEAD))
    angles = where_at.astype(jnp.float32)[:, None] * inverse[None, :]
    signs = jnp.where(lane % HEAD < HEAD // 2, -1.0, 1.0)
    return jnp.cos(angles), jnp.sin(angles) * signs[None, :]


def slot_features(ids):
    lane = jnp.arange(PAIR, dtype=jnp.int32)[None, :]
    column = jnp.where(ids < 0, SEQ_SLOTS, ids)[:, None]
    own = lane == column
    query_side = jnp.where((lane <= SEQ_SLOTS) & (~own | (ids < 0)[:, None]), -1e30, 0.0)
    key_side = jnp.where(own | ((lane >= STAT_LANE) & (lane < STAT_LANE + 3)), 1.0, 0.0)
    return query_side.astype(jnp.bfloat16), key_side.astype(jnp.bfloat16)


def turned(values, cos, sin):
    lane = lax.broadcasted_iota(jnp.int32, values.shape, 1)
    half = HEAD // 2
    other = jnp.where(
        lane % HEAD < half, pltpu.roll(values, PAIR - half, 1), pltpu.roll(values, half, 1)
    )
    return values * cos + other * sin


def compiler_params():
    return pltpu.CompilerParams(vmem_limit_bytes=VMEM_BYTES)


def lower_kernel(pairs, group, core_ref, w_ref, out_ref):
    for pair in range(pairs):
        for owner in range(group):
            for part in range(3):
                source = ((part * group + owner) * pairs + pair) * PAIR
                target = ((pair * group + owner) * 3 + part) * PAIR
                out_ref[:, target : target + PAIR] = w_ref[:, source : source + PAIR].astype(
                    jnp.bfloat16
                )


def lower_half(core, weight, group):
    rows, columns = weight.shape[0] // 2, weight.shape[1]
    return pl.pallas_call(
        functools.partial(lower_kernel, D // PAIR // group, group),
        grid_spec=pltpu.PrefetchScalarGridSpec(
            num_scalar_prefetch=1,
            grid=(1,),
            in_specs=[pl.BlockSpec((rows, columns), lambda i, core: (core[0], 0))],
            out_specs=pl.BlockSpec((rows, columns), lambda i, core: (0, 0)),
        ),
        out_shape=jax.ShapeDtypeStruct((rows, columns), jnp.bfloat16),
        compiler_params=compiler_params(),
        name="lower_half",
    )(core, weight)


def project_kernel(me_ref, x_ref, w_ref, cos_ref, sin_ref, out_ref):
    got = jnp.dot(x_ref[...], w_ref[...], preferred_element_type=jnp.float32)
    cos, sin = cos_ref[0], sin_ref[0]
    query = turned(got[:, :PAIR], cos, sin) * HEAD ** (-0.5)
    keys = turned(got[:, PAIR : 2 * PAIR], cos, sin)
    out_ref[0, :, :PAIR] = query.astype(jnp.bfloat16)
    out_ref[0, :, PAIR : 2 * PAIR] = keys.astype(jnp.bfloat16)
    out_ref[0, :, 2 * PAIR :] = got[:, 2 * PAIR :].astype(jnp.bfloat16)


def skipping(kernel, before, extra):
    def body(*refs):
        kernel(*refs[:before], *refs[before + extra :])

    return body


def untouched(after):
    return [pl.BlockSpec(memory_space=pl.ANY)] * len(after)


def project(me, first_normed, w_in, cos, sin, pair, group):
    rows = first_normed.shape[0]
    return pl.pallas_call(
        project_kernel,
        grid_spec=pltpu.PrefetchScalarGridSpec(
            num_scalar_prefetch=1,
            grid=(group,),
            in_specs=[
                pl.BlockSpec((rows, D), lambda d, me: (0, 0)),
                pl.BlockSpec((D, 3 * PAIR), lambda d, me: (0, pair * group + (me[0] ^ d))),
                pl.BlockSpec((1, rows, PAIR), lambda d, me: (0, 0, 0)),
                pl.BlockSpec((1, rows, PAIR), lambda d, me: (0, 0, 0)),
            ],
            out_specs=pl.BlockSpec((1, rows, 3 * PAIR), lambda d, me: (d, 0, 0)),
        ),
        out_shape=jax.ShapeDtypeStruct((group, rows, 3 * PAIR), jnp.bfloat16),
        compiler_params=compiler_params(),
        name="project",
    )(me, first_normed, w_in, cos, sin)


def row_product_kernel(me_ref, x_ref, w_ref, out_ref):
    out_ref[0] = against(x_ref[...], w_ref[...]).astype(jnp.bfloat16)


def row_product(me, left, weight, pair, group, after=()):
    rows = left.shape[0]
    pairs = D // PAIR // group
    return pl.pallas_call(
        skipping(row_product_kernel, 3, len(after)),
        grid_spec=pltpu.PrefetchScalarGridSpec(
            num_scalar_prefetch=1,
            grid=(group,),
            in_specs=[
                pl.BlockSpec((rows, D), lambda d, me: (0, 0)),
                pl.BlockSpec((PAIR, D), lambda d, me: ((me[0] ^ d) * pairs + pair, 0)),
                *untouched(after),
            ],
            out_specs=pl.BlockSpec((1, rows, PAIR), lambda d, me: (d, 0, 0)),
        ),
        out_shape=jax.ShapeDtypeStruct((group, rows, PAIR), jnp.bfloat16),
        compiler_params=compiler_params(),
        name="row_product",
    )(me, left, weight, *after)


def place(me, pieces, group, after=()):
    rows, width = pieces[0][0].shape
    pairs = len(pieces)
    flat = [piece for near in pieces for piece in near]

    def kernel(me_ref, *refs):
        out_ref = refs[-1]
        for step in range(group):

            @pl.when(pl.program_id(0) == step)
            def _():
                for pair in range(pairs):
                    out_ref[:, pair * width : (pair + 1) * width] = refs[pair * group + step][...]

    return pl.pallas_call(
        kernel,
        grid_spec=pltpu.PrefetchScalarGridSpec(
            num_scalar_prefetch=1,
            grid=(group,),
            in_specs=[pl.BlockSpec((rows, width), lambda d, me: (0, 0))] * len(flat)
            + untouched(after),
            out_specs=pl.BlockSpec((rows, pairs * width), lambda d, me: (0, me[0] ^ d)),
        ),
        out_shape=jax.ShapeDtypeStruct((rows, group * pairs * width), jnp.bfloat16),
        compiler_params=compiler_params(),
        name="place",
    )(me, *flat, *after)


def exchange(array, axis, mask, size):
    return lax.ppermute(array, axis, [(i, i ^ mask) for i in range(size)])


def swap_heads(pieces, group):
    return [pieces[0]] + [exchange(pieces[d], "grp", d, group) for d in range(1, group)]


def attend_kernel(q_ref, k_ref, v_ref, qf_ref, kf_ref, own_v_ref, own_f_ref, out_ref, stat_ref, ke):
    @pl.when(pl.program_id(0) == 0)
    def _():
        ke[:, :PAIR] = k_ref[...]
        ke[:, PAIR:] = kf_ref[...]

    query = q_ref[...]
    lane = lax.broadcasted_iota(jnp.int32, query.shape, 1)
    scores = []
    for head in range(2):
        mine = (lane < HEAD) == (head == 0)
        wide = jnp.concatenate([jnp.where(mine, query, 0), qf_ref[...]], axis=1)
        scores.append(against(wide, ke[...]))
    mixed, logs = [], []
    for head in range(2):
        top = jnp.max(scores[head], axis=1, keepdims=True)
        weights = jnp.exp(scores[head] - top)
        total = jnp.sum(weights, axis=1, keepdims=True)
        got = jnp.dot(
            weights.astype(jnp.bfloat16), v_ref[...], preferred_element_type=jnp.float32
        )
        mixed.append(got / total)
        logs.append(top + jnp.log(total))
    dead = own_f_ref[:, SEQ_SLOTS : SEQ_SLOTS + 1].astype(jnp.float32) > 0.5
    result = jnp.where(lane < HEAD, mixed[0], mixed[1]).astype(jnp.bfloat16)
    out_ref[...] = jnp.where(dead, own_v_ref[...], result)
    stat = jnp.where(lane == 0, logs[0], jnp.where(lane == 1, logs[1], 0.0))
    stat_ref[...] = jnp.where(dead, 0.0, stat)


def block_rows(rows):
    return 512 if rows <= 2048 else 256


def attend(qkv, query_side, key_side):
    rows = qkv.shape[0]
    block = block_rows(rows)

    def some(part):
        return pl.BlockSpec((block, PAIR), lambda i: (i, part))

    def whole(part):
        return pl.BlockSpec((rows, PAIR), lambda i: (0, part))

    return pl.pallas_call(
        attend_kernel,
        grid=(rows // block,),
        in_specs=[some(0), whole(1), whole(2), some(0), whole(0), some(2), some(0)],
        out_specs=[some(0), some(0)],
        out_shape=[
            jax.ShapeDtypeStruct((rows, PAIR), jnp.bfloat16),
            jax.ShapeDtypeStruct((rows, PAIR), jnp.float32),
        ],
        scratch_shapes=[pltpu.VMEM((rows, 2 * PAIR), jnp.bfloat16)],
        compiler_params=compiler_params(),
        name="attend",
    )(qkv, qkv, qkv, query_side, key_side, qkv, key_side)


def in_three(column, lane):
    first = column.astype(jnp.bfloat16).astype(jnp.float32)
    second = (column - first).astype(jnp.bfloat16).astype(jnp.float32)
    third = column - first - second
    return jnp.where(
        lane == STAT_LANE,
        first,
        jnp.where(lane == STAT_LANE + 1, second, jnp.where(lane == STAT_LANE + 2, third, 0.0)),
    )


def attend_back_kernel(
    q_ref, k_ref, v_ref, qf_ref, kf_ref, stat_ref, att_ref, grad_ref, cos_ref, sin_ref,
    own_cos_ref, own_sin_ref, out_ref, ke, ve, kt, dk_sum, dv_sum,
):
    @pl.when(pl.program_id(0) == 0)
    def _():
        ke[:, :PAIR] = k_ref[...]
        ke[:, PAIR:] = kf_ref[...]
        ve[:, :PAIR] = v_ref[...]
        ve[:, PAIR:] = kf_ref[...]
        kt[...] = k_ref[...].T
        dk_sum[...] = jnp.zeros_like(dk_sum)
        dv_sum[...] = jnp.zeros_like(dv_sum)

    query, grad = q_ref[...], grad_ref[...]
    lane = lax.broadcasted_iota(jnp.int32, query.shape, 1)
    both = grad.astype(jnp.float32) * att_ref[...].astype(jnp.float32)
    stat = stat_ref[...]
    query_heads, grad_heads, weights, grad_scores, turned_grads = [], [], [], [], []
    for head in range(2):
        mine = (lane < HEAD) == (head == 0)
        query_head = jnp.where(mine, query, 0)
        grad_head = jnp.where(mine, grad, 0)
        log_total = jnp.sum(jnp.where(lane == head, stat, 0.0), axis=1, keepdims=True)
        centre = jnp.sum(jnp.where(mine, both, 0.0), axis=1, keepdims=True)
        side = (qf_ref[...].astype(jnp.float32) - in_three(log_total, lane)).astype(jnp.bfloat16)
        wide = jnp.concatenate([query_head, side], axis=1)
        weight = jnp.exp(against(ke[...], wide))
        wide_grad = jnp.concatenate(
            [grad_head, (-in_three(centre, lane)).astype(jnp.bfloat16)], axis=1
        )
        grad_score = (weight * against(ve[...], wide_grad)).astype(jnp.bfloat16)
        weights.append(weight.astype(jnp.bfloat16))
        grad_scores.append(grad_score)
        query_heads.append(query_head)
        grad_heads.append(grad_head)
        turned_grads.append(jnp.dot(kt[...], grad_score, preferred_element_type=jnp.float32))
    dv_sum[...] += jnp.dot(
        jnp.concatenate(weights, axis=1),
        jnp.concatenate(grad_heads, axis=0),
        preferred_element_type=jnp.float32,
    )
    dk_sum[...] += jnp.dot(
        jnp.concatenate(grad_scores, axis=1),
        jnp.concatenate(query_heads, axis=0),
        preferred_element_type=jnp.float32,
    )
    row = lax.broadcasted_iota(jnp.int32, turned_grads[0].shape, 0)
    grad_query = jnp.where(row < HEAD, turned_grads[0], turned_grads[1]).T * HEAD ** (-0.5)
    block = query.shape[0]
    own = pl.ds(pl.multiple_of(pl.program_id(0) * block, block), block)
    out_ref[own, :PAIR] = turned(grad_query, own_cos_ref[...], -own_sin_ref[...]).astype(
        jnp.bfloat16
    )

    @pl.when(pl.program_id(0) == pl.num_programs(0) - 1)
    def _():
        out_ref[:, PAIR : 2 * PAIR] = turned(dk_sum[...], cos_ref[...], -sin_ref[...]).astype(
            jnp.bfloat16
        )
        out_ref[:, 2 * PAIR :] = dv_sum[...].astype(jnp.bfloat16)


def attend_back(qkv, query_side, key_side, stat, attended, grad, cos, sin, after=()):
    rows = qkv.shape[0]
    block = block_rows(rows)

    def some(part):
        return pl.BlockSpec((block, PAIR), lambda i: (i, part))

    def whole(part):
        return pl.BlockSpec((rows, PAIR), lambda i: (0, part))

    return pl.pallas_call(
        skipping(attend_back_kernel, 12, len(after)),
        grid=(rows // block,),
        in_specs=[
            some(0), whole(1), whole(2), some(0), whole(0), some(0), some(0), some(0),
            whole(0), whole(0), some(0), some(0), *untouched(after),
        ],
        out_specs=pl.BlockSpec((rows, 3 * PAIR), lambda i: (0, 0)),
        out_shape=jax.ShapeDtypeStruct((rows, 3 * PAIR), jnp.bfloat16),
        scratch_shapes=[
            pltpu.VMEM((rows, 2 * PAIR), jnp.bfloat16),
            pltpu.VMEM((rows, 2 * PAIR), jnp.bfloat16),
            pltpu.VMEM((PAIR, rows), jnp.bfloat16),
            pltpu.VMEM((rows, PAIR), jnp.float32),
            pltpu.VMEM((rows, PAIR), jnp.float32),
        ],
        compiler_params=compiler_params(),
        name="attend_back",
    )(qkv, qkv, qkv, query_side, key_side, stat, attended, grad, cos, sin, cos, sin, *after)


def product(left, right):
    return jnp.dot(left, right, preferred_element_type=jnp.float32)


def contract(left, right):
    return lax.dot_general(
        left, right, (((0,), (0,)), ((), ())), preferred_element_type=jnp.float32
    )


def against(left, right):
    return lax.dot_general(
        left, right, (((1,), (1,)), ((), ())), preferred_element_type=jnp.float32
    )


def own_half(array, core):
    half = array.shape[0] // 2
    return lax.dynamic_slice_in_dim(array, core * half, half)


def gather_weight(weight, core):
    return lax.all_gather(
        own_half(weight, core).astype(jnp.bfloat16), ("grp", "core"), axis=0, tiled=True
    )


def pick(array, index, axis):
    return lax.dynamic_index_in_dim(array, index, axis, keepdims=False)


def added(*terms):
    return sum(term.astype(jnp.float32) for term in terms).astype(jnp.bfloat16)


def delayed(value, after):
    return lax.optimization_barrier((value, after))[0]


def halved(array, mask, group, dim):
    bit = (lax.axis_index("grp") // mask) % 2
    got = exchange(pick(array, 1 - bit, dim), "grp", mask, group)
    return added(pick(array, bit, dim), got)


def core_theirs(left, right, core):
    columns = right.shape[1] // 2
    theirs = lax.dynamic_slice_in_dim(right, (1 - core) * columns, columns, 1)
    return contract(left, theirs).astype(jnp.bfloat16)


def core_mine(left, right, core, sent):
    columns = right.shape[1] // 2
    mine = lax.dynamic_slice_in_dim(right, core * columns, columns, 1)
    got = exchange(sent, "core", 1, 2)
    return (contract(left, mine) + got.astype(jnp.float32)).astype(jnp.bfloat16)


def group_first(share, group):
    rows, columns = share.shape[0] // group, share.shape[1]
    if group != 4:
        return (lax.psum_scatter(share, "grp", scatter_dimension=0, tiled=True),)
    share = share.reshape(2, 2, rows, columns)
    return (
        halved(share[:, :, : rows // 2], 2, group, 0),
        halved(share[:, :, rows // 2 :], 1, group, 1),
    )


def group_second(halves, group):
    if group != 4:
        return halves[0]
    return jnp.concatenate([halved(halves[0], 1, group, 0), halved(halves[1], 2, group, 0)], axis=0)


def far_masks(far):
    return [1 << bit for bit in range(far.bit_length() - 1)]


def far_scatter(share, far, waits=((), ())):
    if far > 4:
        return lax.psum(share, "far")
    for mask, after in zip(far_masks(far), waits):
        bit = (lax.axis_index("far") // mask) % 2
        rows = share.shape[0] // 2
        got = exchange(
            lax.dynamic_slice_in_dim(share, (1 - bit) * rows, rows, 0), "far", mask, far
        )
        kept = lax.dynamic_slice_in_dim(share, bit * rows, rows, 0)
        share = added(delayed(kept, after), got)
    return share


def doubled(array, axis, mask, size, dim, after):
    bit = (lax.axis_index(axis) // mask) % 2
    got = exchange(array, axis, mask, size)
    array = delayed(array, after)
    low = jnp.where(bit == 0, array, got)
    high = jnp.where(bit == 0, got, array)
    return jnp.concatenate([low, high], axis=dim)


def spread(share, far, waits=((), ())):
    if far <= 4:
        for mask, after in zip(far_masks(far)[::-1], waits):
            share = doubled(share, "far", mask, far, 0, after)
    return share


def merged_columns(parts, group):
    pairs = len(parts)
    blocks = []
    for part in range(3):
        for owner in range(group):
            for pair in range(pairs):
                column = (owner * 3 + part) * PAIR
                blocks.append(parts[pair][:, column : column + PAIR])
    return jnp.concatenate(blocks, axis=1)


def spread_halves(array):
    spare = ((0, 0), (0, FF_WIDE - FF))
    return jnp.concatenate([jnp.pad(array[:, :FF], spare), jnp.pad(array[:, FF:], spare)], axis=1)


def gated(gate, upward):
    return jax.nn.gelu(gate, approximate=False) * upward


def adam_update(weight, mean, square, grad, rate):
    mean_new = 0.9 * mean + 0.1 * grad
    square_new = 0.999 * square + 0.001 * grad * grad
    step_size = mean_new / (1.0 - 0.9**STEP) / (jnp.sqrt(square_new / (1.0 - 0.999**STEP)) + 1e-08)
    return (mean_new, square_new, weight - rate * (step_size + 0.01 * weight))


def local(
    group,
    far,
    tokens,
    slot_ids,
    cotangent,
    inproj,
    outproj,
    upproj,
    downproj,
    norm_gains,
    inproj_mean,
    outproj_mean,
    upproj_mean,
    downproj_mean,
    gains_mean,
    inproj_square,
    outproj_square,
    upproj_square,
    downproj_square,
    gains_square,
):
    me = lax.axis_index("grp")
    core = lax.axis_index("core")
    me_list = me.reshape(1).astype(jnp.int32)
    core_list = core.reshape(1).astype(jnp.int32)
    pairs = D // PAIR // group
    masters = (inproj, outproj, upproj, downproj, norm_gains)
    own_rows = tokens.shape[1]
    own_gains = norm_gains.shape[0]
    both = ("grp", "core")
    w_in = lax.all_gather(lower_half(core_list, inproj, group), both, axis=0, tiled=True)
    w_outup = gather_weight(jnp.concatenate([outproj, spread_halves(upproj)], axis=1), core)
    w_down = gather_weight(downproj, core)
    w_out, w_up = w_outup[:, :D], w_outup[:, D:]
    packed = jnp.concatenate([norm_gains[:, 0], norm_gains[:, 1], slot_ids[0].astype(jnp.float32)])
    packed = lax.all_gather(packed.astype(jnp.bfloat16), "grp", axis=0, tiled=False)
    gain_one = packed[:, :own_gains].reshape(D).astype(jnp.float32)
    gain_two = packed[:, own_gains : 2 * own_gains].reshape(D).astype(jnp.float32)
    all_ids = packed[:, 2 * own_gains :].astype(jnp.int32).reshape(group * own_rows)
    group_rows = all_ids.shape[0]
    order = me ^ jnp.arange(group, dtype=jnp.int32)
    near_ids = all_ids.reshape(group, own_rows)[order].reshape(group_rows)
    where_at = positions(all_ids).reshape(group, own_rows)[order].reshape(group_rows)
    cos, sin = pair_tables(where_at)
    query_side, key_side = slot_features(near_ids)
    live = (slot_ids[0] >= 0).astype(jnp.bfloat16)
    inputs = tokens[0].astype(jnp.float32)
    first_normed = layer_norm(inputs, gain_one).astype(jnp.bfloat16)
    cos_near = cos.reshape(group, own_rows, PAIR)
    sin_near = sin.reshape(group, own_rows, PAIR)
    qkv, stats, attended_near, attended_here = [], [], [], []
    for pair in range(pairs):
        pieces = project(me_list, first_normed, w_in, cos_near, sin_near, pair, group)
        qkv.append(jnp.concatenate(swap_heads(pieces, group), axis=0))
    for pair in range(pairs):
        mixed, stat = attend(qkv[pair], query_side, key_side)
        stats.append(stat)
        attended_near.append(mixed)
        attended_here.append(swap_heads(mixed.reshape(group, own_rows, PAIR), group))
    attended = place(me_list, attended_here, group)
    middle = inputs + product(attended, w_out)
    second_normed = layer_norm(middle, gain_two).astype(jnp.bfloat16)
    gate_up = product(second_normed, w_up)
    gate = gate_up[:, :FF]
    upward = gate_up[:, FF_WIDE : FF_WIDE + FF]
    hidden = gated(gate, upward).astype(jnp.bfloat16)
    result = middle + product(hidden, w_down)
    grad_top = cotangent[0] * live[:, None]
    grad_hidden = against(grad_top, w_down)
    _, gate_back = jax.vjp(gated, gate, upward)
    grad_gate_up = spread_halves(jnp.concatenate(gate_back(grad_hidden), axis=1)).astype(
        jnp.bfloat16
    )
    grad_down = contract(hidden, grad_top).astype(jnp.bfloat16)
    up_theirs = core_theirs(second_normed, grad_gate_up, core)
    grad_gate_up, up_theirs, grad_down = lax.optimization_barrier(
        (grad_gate_up, up_theirs, grad_down)
    )
    grad_second = against(grad_gate_up, w_up)
    _, second_back = jax.vjp(lambda v: layer_norm(v, gain_two), middle)
    (grad_from_norm,) = second_back(grad_second)
    grad_middle = grad_top.astype(jnp.float32) + grad_from_norm
    grad_branch = grad_middle.astype(jnp.bfloat16)
    down_share = lax.psum_scatter(grad_down, both, scatter_dimension=0, tiled=True)
    grad_near = []
    for pair in range(pairs):
        after = (up_theirs, grad_down) if pair == 0 else (sent,)
        sent = row_product(me_list, grad_branch, w_outup, pair, group, after)
        grad_near.append(jnp.concatenate(swap_heads(sent, group), axis=0))
    out_theirs = core_theirs(attended, grad_branch, core)
    up_share = jnp.concatenate(
        [
            core_mine(second_normed, grad_gate_up, core, up_theirs),
            core_mine(attended, grad_branch, core, out_theirs),
        ],
        axis=1,
    )
    up_halves = group_first(up_share, group)
    up_half = group_second(up_halves, group)
    waits = [(up_share,), up_halves]
    grads_here = []
    for pair in range(pairs):
        grads = attend_back(
            qkv[pair], query_side, key_side, stats[pair], attended_near[pair], grad_near[pair],
            cos, sin, waits[pair],
        )
        grads_here.append(swap_heads(grads.reshape(group, own_rows, 3 * PAIR), group))
    grads_placed, in_theirs, grad_first = [], [], 0.0
    for pair in range(pairs):
        after = (up_half,) if pair == 0 else (in_theirs[0],)
        placed = place(me_list, [grads_here[pair]], group, after)
        grads_placed.append(placed)
        in_theirs.append(core_theirs(first_normed, placed, core))
    in_shares = [
        core_mine(first_normed, grads_placed[pair], core, in_theirs[pair]) for pair in range(pairs)
    ]
    in_firsts = [delayed(group_first(share, group), in_theirs[-1]) for share in in_shares]
    in_halves = [group_second(first, group) for first in in_firsts]
    in_chunks = [far_scatter(half, far) for half in in_halves]
    for pair in range(pairs):
        width = 3 * PAIR * group
        part = w_in[:, pair * width : (pair + 1) * width]
        grad_first = grad_first + against(grads_placed[pair], part)
    up_chunk = far_scatter(up_half, far, (in_theirs[-1], in_shares[-1]))
    up_chunk = spread(up_chunk, far, (in_firsts[-1], in_halves[-1]))
    total_up = doubled(up_chunk, "core", 1, 2, 1, in_chunks[-1]).astype(jnp.float32)
    wide = up_chunk.shape[1]
    total_out = jnp.concatenate([total_up[:, FF_WIDE:wide], total_up[:, wide + FF_WIDE :]], axis=1)
    total_up = jnp.concatenate(
        [total_up[:, :FF], total_up[:, wide : wide + FF]], axis=1
    )
    down_share = lax.psum(delayed(down_share, in_theirs[0]), "far")
    total_down = doubled(
        delayed(down_share, in_halves[-1]), "core", 1, 2, 0, in_chunks[-1]
    ).astype(jnp.float32)
    total_in = merged_columns(
        [doubled(spread(chunk, far), "core", 1, 2, 1, ()) for chunk in in_chunks], group
    ).astype(jnp.float32)
    _, first_back = jax.vjp(lambda v: layer_norm(v, gain_one), inputs)
    (grad_inputs,) = first_back(grad_first)
    input_grad = (grad_middle + grad_inputs).astype(jnp.bfloat16)
    low_in = inproj.astype(jnp.bfloat16).astype(jnp.float32)
    low_up = upproj.astype(jnp.bfloat16).astype(jnp.float32)
    low_gains = norm_gains.astype(jnp.bfloat16).astype(jnp.float32)
    total_gains = (
        jnp.stack([jnp.sum(low_in * total_in, axis=1), jnp.sum(low_up * total_up, axis=1)], axis=1)
        / low_gains
    )
    totals = (total_in, total_out, total_up, total_down, total_gains)
    means = (inproj_mean, outproj_mean, upproj_mean, downproj_mean, gains_mean)
    squares = (inproj_square, outproj_square, upproj_square, downproj_square, gains_square)
    updates = [
        adam_update(masters[index], means[index], squares[index], totals[index], rate_list[index])
        for index in range(5)
    ]
    return (
        result.astype(jnp.bfloat16)[None],
        input_grad[None],
        updates[0][0],
        updates[0][1],
        updates[0][2],
        updates[1][0],
        updates[1][1],
        updates[1][2],
        updates[2][0],
        updates[2][1],
        updates[2][2],
        updates[3][0],
        updates[3][1],
        updates[3][2],
        updates[4][0],
        updates[4][1],
        updates[4][2],
    )


def solution(mesh):
    group_size, replicas = mesh.devices.shape
    fine = Mesh(mesh.devices.reshape(group_size, replicas // 2, 2), ("grp", "far", "core"))
    placed = (
        P(("far", "core"), "grp", None),
        P(("far", "core"), "grp"),
        P(("far", "core"), "grp", None),
        P("grp", None),
        P("grp", None),
        P("grp", None),
        P("grp", None),
        P("grp", None),
        P("grp", None),
        P("grp", None),
        P("grp", None),
        P("grp", None),
        P("grp", None),
        P("grp", None),
        P("grp", None),
        P("grp", None),
        P("grp", None),
        P("grp", None),
    )
    return jax.shard_map(
        functools.partial(local, group_size, replicas // 2),
        mesh=fine,
        in_specs=placed,
        out_specs=(
            P(("far", "core"), "grp", None),
            P(("far", "core"), "grp", None),
            P("grp", None),
            P("grp", None),
            P("grp", None),
            P("grp", None),
            P("grp", None),
            P("grp", None),
            P("grp", None),
            P("grp", None),
            P("grp", None),
            P("grp", None),
            P("grp", None),
            P("grp", None),
            P("grp", None),
            P("grp", None),
            P("grp", None),
        ),
        check_vma=False,
    )
```

```python
import functools

import jax
import jax.numpy as jnp
from jax import lax
from jax.experimental import pallas as pl
from jax.experimental.pallas import tpu as pltpu
from jax.sharding import Mesh, PartitionSpec as P

D = 1024
HEADS = 16
HEAD = 64
FF = 2624
FF_WIDE = 2688
STEP = 10
SEQ_SLOTS = 9
PAIR = 128
STAT_LANE = 16
VMEM_BYTES = 56 * 1024 * 1024


rope_base = 160000.0
norm_eps = 1e-05
rate_list = (0.1, 0.4, 0.08, 0.05, 0.6)


def layer_norm(values, gain):
    centred = values - jnp.mean(values, axis=-1, keepdims=True)
    spread = jnp.mean(centred * centred, axis=-1, keepdims=True)
    return centred * lax.rsqrt(spread + norm_eps) * gain


def positions(ids):
    live = ids >= 0
    counted = jnp.cumsum(live.astype(jnp.int32)) - 1
    onehot = (
        (ids[:, None] == jnp.arange(SEQ_SLOTS, dtype=jnp.int32)[None, :]) & live[:, None]
    ).astype(jnp.int32)
    counts = jnp.sum(onehot, axis=0)
    starts = jnp.cumsum(counts) - counts
    first = jnp.sum(onehot * starts[None, :], axis=1)
    return jnp.where(live, counted - first, 0)


def pair_tables(where_at):
    lane = jnp.arange(PAIR, dtype=jnp.int32)
    order = (lane % (HEAD // 2)).astype(jnp.float32)
    inverse = rope_base ** (-(order * 2.0 / HEAD))
    angles = where_at.astype(jnp.float32)[:, None] * inverse[None, :]
    signs = jnp.where(lane % HEAD < HEAD // 2, -1.0, 1.0)
    return jnp.cos(angles), jnp.sin(angles) * signs[None, :]


def slot_features(ids):
    lane = jnp.arange(PAIR, dtype=jnp.int32)[None, :]
    column = jnp.where(ids < 0, SEQ_SLOTS, ids)[:, None]
    own = lane == column
    query_side = jnp.where((lane <= SEQ_SLOTS) & (~own | (ids < 0)[:, None]), -1e30, 0.0)
    key_side = jnp.where(own | ((lane >= STAT_LANE) & (lane < STAT_LANE + 3)), 1.0, 0.0)
    return query_side.astype(jnp.bfloat16), key_side.astype(jnp.bfloat16)


def turned(values, cos, sin):
    lane = lax.broadcasted_iota(jnp.int32, values.shape, 1)
    half = HEAD // 2
    other = jnp.where(
        lane % HEAD < half, pltpu.roll(values, PAIR - half, 1), pltpu.roll(values, half, 1)
    )
    return values * cos + other * sin


def compiler_params():
    return pltpu.CompilerParams(vmem_limit_bytes=VMEM_BYTES)


def lower_kernel(pairs, group, core_ref, w_ref, out_ref):
    for pair in range(pairs):
        for owner in range(group):
            for part in range(3):
                source = ((part * group + owner) * pairs + pair) * PAIR
                target = ((pair * group + owner) * 3 + part) * PAIR
                out_ref[:, target : target + PAIR] = w_ref[:, source : source + PAIR].astype(
                    jnp.bfloat16
                )


def lower_half(core, weight, group):
    rows, columns = weight.shape[0] // 2, weight.shape[1]
    return pl.pallas_call(
        functools.partial(lower_kernel, D // PAIR // group, group),
        grid_spec=pltpu.PrefetchScalarGridSpec(
            num_scalar_prefetch=1,
            grid=(1,),
            in_specs=[pl.BlockSpec((rows, columns), lambda i, core: (core[0], 0))],
            out_specs=pl.BlockSpec((rows, columns), lambda i, core: (0, 0)),
        ),
        out_shape=jax.ShapeDtypeStruct((rows, columns), jnp.bfloat16),
        compiler_params=compiler_params(),
        name="lower_half",
    )(core, weight)


def project_kernel(me_ref, x_ref, w_ref, cos_ref, sin_ref, out_ref):
    got = jnp.dot(x_ref[...], w_ref[...], preferred_element_type=jnp.float32)
    cos, sin = cos_ref[0], sin_ref[0]
    query = turned(got[:, :PAIR], cos, sin) * HEAD ** (-0.5)
    keys = turned(got[:, PAIR : 2 * PAIR], cos, sin)
    out_ref[0, :, :PAIR] = query.astype(jnp.bfloat16)
    out_ref[0, :, PAIR : 2 * PAIR] = keys.astype(jnp.bfloat16)
    out_ref[0, :, 2 * PAIR :] = got[:, 2 * PAIR :].astype(jnp.bfloat16)


def skipping(kernel, before, extra):
    def body(*refs):
        kernel(*refs[:before], *refs[before + extra :])

    return body


def untouched(after):
    return [pl.BlockSpec(memory_space=pl.ANY)] * len(after)


def project(me, first_normed, w_in, cos, sin, pair, group, after=()):
    rows = first_normed.shape[0]
    return pl.pallas_call(
        skipping(project_kernel, 5, len(after)),
        grid_spec=pltpu.PrefetchScalarGridSpec(
            num_scalar_prefetch=1,
            grid=(group,),
            in_specs=[
                pl.BlockSpec((rows, D), lambda d, me: (0, 0)),
                pl.BlockSpec((D, 3 * PAIR), lambda d, me: (0, pair * group + (me[0] ^ d))),
                pl.BlockSpec((1, rows, PAIR), lambda d, me: (0, 0, 0)),
                pl.BlockSpec((1, rows, PAIR), lambda d, me: (0, 0, 0)),
                *untouched(after),
            ],
            out_specs=pl.BlockSpec((1, rows, 3 * PAIR), lambda d, me: (d, 0, 0)),
        ),
        out_shape=jax.ShapeDtypeStruct((group, rows, 3 * PAIR), jnp.bfloat16),
        compiler_params=compiler_params(),
        name="project",
    )(me, first_normed, w_in, cos, sin, *after)


def row_product_kernel(me_ref, x_ref, w_ref, out_ref):
    out_ref[0] = against(x_ref[...], w_ref[...]).astype(jnp.bfloat16)


def row_product(me, left, weight, group, after=()):
    rows = left.shape[0]
    wide = D // group
    return pl.pallas_call(
        skipping(row_product_kernel, 3, len(after)),
        grid_spec=pltpu.PrefetchScalarGridSpec(
            num_scalar_prefetch=1,
            grid=(group,),
            in_specs=[
                pl.BlockSpec((rows, D), lambda d, me: (0, 0)),
                pl.BlockSpec((wide, D), lambda d, me: (me[0] ^ d, 0)),
                *untouched(after),
            ],
            out_specs=pl.BlockSpec((1, rows, wide), lambda d, me: (d, 0, 0)),
        ),
        out_shape=jax.ShapeDtypeStruct((group, rows, wide), jnp.bfloat16),
        compiler_params=compiler_params(),
        name="row_product",
    )(me, left, weight, *after)


def place(me, pieces, group, after=()):
    rows, width = pieces[0][0].shape
    pairs = len(pieces)
    flat = [piece for near in pieces for piece in near]

    def kernel(me_ref, *refs):
        out_ref = refs[-1]
        for step in range(group):

            @pl.when(pl.program_id(0) == step)
            def _():
                for pair in range(pairs):
                    out_ref[:, pair * width : (pair + 1) * width] = refs[pair * group + step][...]

    return pl.pallas_call(
        kernel,
        grid_spec=pltpu.PrefetchScalarGridSpec(
            num_scalar_prefetch=1,
            grid=(group,),
            in_specs=[pl.BlockSpec((rows, width), lambda d, me: (0, 0))] * len(flat)
            + untouched(after),
            out_specs=pl.BlockSpec((rows, pairs * width), lambda d, me: (0, me[0] ^ d)),
        ),
        out_shape=jax.ShapeDtypeStruct((rows, group * pairs * width), jnp.bfloat16),
        compiler_params=compiler_params(),
        name="place",
    )(me, *flat, *after)


def exchange(array, axis, mask, size):
    return lax.ppermute(array, axis, [(i, i ^ mask) for i in range(size)])


def swap_heads(pieces, group):
    return [pieces[0]] + [exchange(pieces[d], "grp", d, group) for d in range(1, group)]


def assemble_kernel(me_ref, own_ref, other_ref, out_ref):
    @pl.when(pl.program_id(1) == 0)
    def _():
        out_ref[...] = own_ref[0]

    @pl.when(pl.program_id(1) == 1)
    def _():
        out_ref[...] = other_ref[0]


def near_parts(part, group):
    return jnp.stack([part] + [exchange(part, "grp", d, group) for d in range(1, group)])


def gather_direct(own, me_core, group, by_rows):
    other = exchange(own, "core", 1, 2)
    rows, columns = own.shape[1:]
    if by_rows:
        shape = (2 * group * rows, columns)
        target = lambda d, side, me: ((me[0] ^ d) * 2 + (me[1] ^ side), 0)
    else:
        shape = (group * rows, 2 * columns)
        target = lambda d, side, me: (me[0] ^ d, me[1] ^ side)
    return pl.pallas_call(
        assemble_kernel,
        grid_spec=pltpu.PrefetchScalarGridSpec(
            num_scalar_prefetch=1,
            grid=(group, 2),
            in_specs=[pl.BlockSpec((1, rows, columns), lambda d, side, me: (d, 0, 0))] * 2,
            out_specs=pl.BlockSpec((rows, columns), target),
        ),
        out_shape=jax.ShapeDtypeStruct(shape, jnp.bfloat16),
        compiler_params=compiler_params(),
        name="assemble",
    )(me_core, own, other)


def attend_kernel(q_ref, k_ref, v_ref, qf_ref, kf_ref, own_v_ref, own_f_ref, out_ref, stat_ref, ke):
    @pl.when(pl.program_id(0) == 0)
    def _():
        ke[:, :PAIR] = k_ref[...]
        ke[:, PAIR:] = kf_ref[...]

    query = q_ref[...]
    lane = lax.broadcasted_iota(jnp.int32, query.shape, 1)
    scores = []
    for head in range(2):
        mine = (lane < HEAD) == (head == 0)
        wide = jnp.concatenate([jnp.where(mine, query, 0), qf_ref[...]], axis=1)
        scores.append(against(wide, ke[...]))
    mixed, logs = [], []
    for head in range(2):
        top = jnp.max(scores[head], axis=1, keepdims=True)
        weights = jnp.exp(scores[head] - top)
        total = jnp.sum(weights, axis=1, keepdims=True)
        got = jnp.dot(
            weights.astype(jnp.bfloat16), v_ref[...], preferred_element_type=jnp.float32
        )
        mixed.append(got / total)
        logs.append(top + jnp.log(total))
    dead = own_f_ref[:, SEQ_SLOTS : SEQ_SLOTS + 1].astype(jnp.float32) > 0.5
    result = jnp.where(lane < HEAD, mixed[0], mixed[1]).astype(jnp.bfloat16)
    out_ref[...] = jnp.where(dead, own_v_ref[...], result)
    stat = jnp.where(lane == 0, logs[0], jnp.where(lane == 1, logs[1], 0.0))
    stat_ref[...] = jnp.where(dead, 0.0, stat)


def block_rows(rows):
    return 512 if rows <= 2048 else 256


def attend(qkv, query_side, key_side, after=()):
    rows = qkv.shape[0]
    block = block_rows(rows)

    def some(part):
        return pl.BlockSpec((block, PAIR), lambda i: (i, part))

    def whole(part):
        return pl.BlockSpec((rows, PAIR), lambda i: (0, part))

    return pl.pallas_call(
        skipping(attend_kernel, 7, len(after)),
        grid=(rows // block,),
        in_specs=[
            some(0), whole(1), whole(2), some(0), whole(0), some(2), some(0), *untouched(after),
        ],
        out_specs=[some(0), some(0)],
        out_shape=[
            jax.ShapeDtypeStruct((rows, PAIR), jnp.bfloat16),
            jax.ShapeDtypeStruct((rows, PAIR), jnp.float32),
        ],
        scratch_shapes=[pltpu.VMEM((rows, 2 * PAIR), jnp.bfloat16)],
        compiler_params=compiler_params(),
        name="attend",
    )(qkv, qkv, qkv, query_side, key_side, qkv, key_side, *after)


def in_three(column, lane):
    first = column.astype(jnp.bfloat16).astype(jnp.float32)
    second = (column - first).astype(jnp.bfloat16).astype(jnp.float32)
    third = column - first - second
    return jnp.where(
        lane == STAT_LANE,
        first,
        jnp.where(lane == STAT_LANE + 1, second, jnp.where(lane == STAT_LANE + 2, third, 0.0)),
    )


def attend_back_kernel(
    q_ref, k_ref, v_ref, qf_ref, kf_ref, stat_ref, att_ref, grad_ref, cos_ref, sin_ref,
    own_cos_ref, own_sin_ref, out_ref, ke, ve, kt, dk_sum, dv_sum,
):
    @pl.when(pl.program_id(0) == 0)
    def _():
        ke[:, :PAIR] = k_ref[...]
        ke[:, PAIR:] = kf_ref[...]
        ve[:, :PAIR] = v_ref[...]
        ve[:, PAIR:] = kf_ref[...]
        kt[...] = k_ref[...].T
        dk_sum[...] = jnp.zeros_like(dk_sum)
        dv_sum[...] = jnp.zeros_like(dv_sum)

    query, grad = q_ref[...], grad_ref[...]
    lane = lax.broadcasted_iota(jnp.int32, query.shape, 1)
    both = grad.astype(jnp.float32) * att_ref[...].astype(jnp.float32)
    stat = stat_ref[...]
    query_heads, grad_heads, weights, grad_scores, turned_grads = [], [], [], [], []
    for head in range(2):
        mine = (lane < HEAD) == (head == 0)
        query_head = jnp.where(mine, query, 0)
        grad_head = jnp.where(mine, grad, 0)
        log_total = jnp.sum(jnp.where(lane == head, stat, 0.0), axis=1, keepdims=True)
        centre = jnp.sum(jnp.where(mine, both, 0.0), axis=1, keepdims=True)
        side = (qf_ref[...].astype(jnp.float32) - in_three(log_total, lane)).astype(jnp.bfloat16)
        wide = jnp.concatenate([query_head, side], axis=1)
        weight = jnp.exp(against(ke[...], wide))
        wide_grad = jnp.concatenate(
            [grad_head, (-in_three(centre, lane)).astype(jnp.bfloat16)], axis=1
        )
        grad_score = (weight * against(ve[...], wide_grad)).astype(jnp.bfloat16)
        weights.append(weight.astype(jnp.bfloat16))
        grad_scores.append(grad_score)
        query_heads.append(query_head)
        grad_heads.append(grad_head)
        turned_grads.append(jnp.dot(kt[...], grad_score, preferred_element_type=jnp.float32))
    dv_sum[...] += jnp.dot(
        jnp.concatenate(weights, axis=1),
        jnp.concatenate(grad_heads, axis=0),
        preferred_element_type=jnp.float32,
    )
    dk_sum[...] += jnp.dot(
        jnp.concatenate(grad_scores, axis=1),
        jnp.concatenate(query_heads, axis=0),
        preferred_element_type=jnp.float32,
    )
    row = lax.broadcasted_iota(jnp.int32, turned_grads[0].shape, 0)
    grad_query = jnp.where(row < HEAD, turned_grads[0], turned_grads[1]).T * HEAD ** (-0.5)
    block = query.shape[0]
    own = pl.ds(pl.multiple_of(pl.program_id(0) * block, block), block)
    out_ref[own, :PAIR] = turned(grad_query, own_cos_ref[...], -own_sin_ref[...]).astype(
        jnp.bfloat16
    )

    @pl.when(pl.program_id(0) == pl.num_programs(0) - 1)
    def _():
        out_ref[:, PAIR : 2 * PAIR] = turned(dk_sum[...], cos_ref[...], -sin_ref[...]).astype(
            jnp.bfloat16
        )
        out_ref[:, 2 * PAIR :] = dv_sum[...].astype(jnp.bfloat16)


def attend_back(qkv, query_side, key_side, stat, attended, grad, cos, sin, pair, after=()):
    rows = qkv.shape[0]
    block = block_rows(rows)

    def some(part):
        return pl.BlockSpec((block, PAIR), lambda i: (i, part))

    def whole(part):
        return pl.BlockSpec((rows, PAIR), lambda i: (0, part))

    return pl.pallas_call(
        skipping(attend_back_kernel, 12, len(after)),
        grid=(rows // block,),
        in_specs=[
            some(0), whole(1), whole(2), some(0), whole(0), some(0), some(0), some(pair),
            whole(0), whole(0), some(0), some(0), *untouched(after),
        ],
        out_specs=pl.BlockSpec((rows, 3 * PAIR), lambda i: (0, 0)),
        out_shape=jax.ShapeDtypeStruct((rows, 3 * PAIR), jnp.bfloat16),
        scratch_shapes=[
            pltpu.VMEM((rows, 2 * PAIR), jnp.bfloat16),
            pltpu.VMEM((rows, 2 * PAIR), jnp.bfloat16),
            pltpu.VMEM((PAIR, rows), jnp.bfloat16),
            pltpu.VMEM((rows, PAIR), jnp.float32),
            pltpu.VMEM((rows, PAIR), jnp.float32),
        ],
        compiler_params=compiler_params(),
        name="attend_back",
    )(qkv, qkv, qkv, query_side, key_side, stat, attended, grad, cos, sin, cos, sin, *after)


def product(left, right):
    return jnp.dot(left, right, preferred_element_type=jnp.float32)


def contract(left, right):
    return lax.dot_general(
        left, right, (((0,), (0,)), ((), ())), preferred_element_type=jnp.float32
    )


def against(left, right):
    return lax.dot_general(
        left, right, (((1,), (1,)), ((), ())), preferred_element_type=jnp.float32
    )


def own_half(array, core):
    half = array.shape[0] // 2
    return lax.dynamic_slice_in_dim(array, core * half, half)


def gather_weight(weight, core):
    return lax.all_gather(
        own_half(weight, core).astype(jnp.bfloat16), ("grp", "core"), axis=0, tiled=True
    )


def pick(array, index, axis):
    return lax.dynamic_index_in_dim(array, index, axis, keepdims=False)


def added(*terms):
    return sum(term.astype(jnp.float32) for term in terms).astype(jnp.bfloat16)


def delayed(value, after):
    return lax.optimization_barrier((value, after))[0]


def halved(array, mask, group, dim, after=()):
    bit = (lax.axis_index("grp") // mask) % 2
    got = exchange(pick(array, 1 - bit, dim), "grp", mask, group)
    return added(delayed(pick(array, bit, dim), after), got)


def core_theirs(left, right, core):
    columns = right.shape[1] // 2
    theirs = lax.dynamic_slice_in_dim(right, (1 - core) * columns, columns, 1)
    return contract(left, theirs).astype(jnp.bfloat16)


def core_mine(left, right, core, sent):
    columns = right.shape[1] // 2
    mine = lax.dynamic_slice_in_dim(right, core * columns, columns, 1)
    got = exchange(sent, "core", 1, 2)
    return (contract(left, mine) + got.astype(jnp.float32)).astype(jnp.bfloat16)


def group_first(share, group):
    rows, columns = share.shape[0] // group, share.shape[1]
    if group != 4:
        return (lax.psum_scatter(share, "grp", scatter_dimension=0, tiled=True),)
    share = share.reshape(2, 2, rows, columns)
    return (
        halved(share[:, :, : rows // 2], 2, group, 0),
        halved(share[:, :, rows // 2 :], 1, group, 1),
    )


def group_second(halves, group, after=()):
    if group != 4:
        return halves[0]
    return jnp.concatenate(
        [halved(halves[0], 1, group, 0, after), halved(halves[1], 2, group, 0, after)], axis=0
    )


def far_masks(far):
    return [1 << bit for bit in range(far.bit_length() - 1)]


def far_scatter(share, far, waits=((), ())):
    if far > 4:
        return lax.psum(share, "far")
    for mask, after in zip(far_masks(far), waits):
        bit = (lax.axis_index("far") // mask) % 2
        rows = share.shape[0] // 2
        got = exchange(
            lax.dynamic_slice_in_dim(share, (1 - bit) * rows, rows, 0), "far", mask, far
        )
        kept = lax.dynamic_slice_in_dim(share, bit * rows, rows, 0)
        share = added(delayed(kept, after), got)
    return share


def doubled(array, axis, mask, size, dim, after):
    bit = (lax.axis_index(axis) // mask) % 2
    got = exchange(array, axis, mask, size)
    array = delayed(array, after)
    low = jnp.where(bit == 0, array, got)
    high = jnp.where(bit == 0, got, array)
    return jnp.concatenate([low, high], axis=dim)


def spread(share, far, waits=((), ())):
    if far <= 4:
        for mask, after in zip(far_masks(far)[::-1], waits):
            share = doubled(share, "far", mask, far, 0, after)
    return share


def merged_columns(total, pairs, group):
    half = 3 * PAIR * group // 2
    blocks = []
    for part in range(3):
        for owner in range(group):
            for pair in range(pairs):
                side, within = divmod((owner * 3 + part) * PAIR, half)
                column = (side * pairs + pair) * half + within
                blocks.append(total[:, column : column + PAIR])
    return jnp.concatenate(blocks, axis=1)


def spread_halves(array):
    spare = ((0, 0), (0, FF_WIDE - FF))
    return jnp.concatenate([jnp.pad(array[:, :FF], spare), jnp.pad(array[:, FF:], spare)], axis=1)


def gated(gate, upward):
    return jax.nn.gelu(gate, approximate=False) * upward


def adam_update(weight, mean, square, grad, rate):
    mean_new = 0.9 * mean + 0.1 * grad
    square_new = 0.999 * square + 0.001 * grad * grad
    step_size = mean_new / (1.0 - 0.9**STEP) / (jnp.sqrt(square_new / (1.0 - 0.999**STEP)) + 1e-08)
    return (mean_new, square_new, weight - rate * (step_size + 0.01 * weight))


def local(
    group,
    far,
    tokens,
    slot_ids,
    cotangent,
    inproj,
    outproj,
    upproj,
    downproj,
    norm_gains,
    inproj_mean,
    outproj_mean,
    upproj_mean,
    downproj_mean,
    gains_mean,
    inproj_square,
    outproj_square,
    upproj_square,
    downproj_square,
    gains_square,
):
    me = lax.axis_index("grp")
    core = lax.axis_index("core")
    me_list = me.reshape(1).astype(jnp.int32)
    core_list = core.reshape(1).astype(jnp.int32)
    pairs = D // PAIR // group
    masters = (inproj, outproj, upproj, downproj, norm_gains)
    own_rows = tokens.shape[1]
    own_gains = norm_gains.shape[0]
    both = ("grp", "core")
    w_in = lax.all_gather(lower_half(core_list, inproj, group), both, axis=0, tiled=True)
    me_core = jnp.stack([me, core]).astype(jnp.int32)
    near_out = near_parts(own_half(outproj, core).astype(jnp.bfloat16), group)
    w_out = gather_direct(near_out, me_core, group, True)
    w_up = gather_weight(spread_halves(upproj), core)
    packed = jnp.concatenate([norm_gains[:, 0], norm_gains[:, 1], slot_ids[0].astype(jnp.float32)])
    packed = lax.all_gather(packed.astype(jnp.bfloat16), "grp", axis=0, tiled=False)
    gain_one = packed[:, :own_gains].reshape(D).astype(jnp.float32)
    gain_two = packed[:, own_gains : 2 * own_gains].reshape(D).astype(jnp.float32)
    all_ids = packed[:, 2 * own_gains :].astype(jnp.int32).reshape(group * own_rows)
    group_rows = all_ids.shape[0]
    order = me ^ jnp.arange(group, dtype=jnp.int32)
    near_ids = all_ids.reshape(group, own_rows)[order].reshape(group_rows)
    where_at = positions(all_ids).reshape(group, own_rows)[order].reshape(group_rows)
    cos, sin = pair_tables(where_at)
    query_side, key_side = slot_features(near_ids)
    live = (slot_ids[0] >= 0).astype(jnp.bfloat16)
    inputs = tokens[0].astype(jnp.float32)
    first_normed = layer_norm(inputs, gain_one).astype(jnp.bfloat16)
    cos_near = cos.reshape(group, own_rows, PAIR)
    sin_near = sin.reshape(group, own_rows, PAIR)
    qkv, stats, attended_near, attended_here, first_sent = [], [], [], [], []
    for pair in range(pairs):
        after = (near_out,) if pair == 0 else (first_sent[0],)
        pieces = project(me_list, first_normed, w_in, cos_near, sin_near, pair, group, after)
        first_sent.append(pieces)
        qkv.append(jnp.concatenate(swap_heads(pieces, group), axis=0))
    for pair in range(pairs):
        mixed, stat = attend(qkv[pair], query_side, key_side, [qkv[-1]] + stats[-1:])
        stats.append(stat)
        attended_near.append(mixed)
        attended_here.append(swap_heads(mixed.reshape(group, own_rows, PAIR), group))
    low_down = lax.dynamic_slice_in_dim(downproj, core * (D // 2), D // 2, 1).astype(jnp.bfloat16)
    w_down = gather_direct(near_parts(delayed(low_down, qkv[-1]), group), me_core, group, False)
    attended = place(me_list, attended_here, group)
    middle = inputs + product(attended, w_out)
    second_normed = layer_norm(middle, gain_two).astype(jnp.bfloat16)
    gate_up = product(second_normed, w_up)
    gate = gate_up[:, :FF]
    upward = gate_up[:, FF_WIDE : FF_WIDE + FF]
    hidden = gated(gate, upward).astype(jnp.bfloat16)
    result = middle + product(hidden, w_down)
    grad_top = cotangent[0] * live[:, None]
    grad_down = contract(hidden, grad_top).astype(jnp.bfloat16)
    grad_hidden = against(delayed(grad_top, grad_down), w_down)
    _, gate_back = jax.vjp(gated, gate, upward)
    grad_gate_up = spread_halves(jnp.concatenate(gate_back(grad_hidden), axis=1)).astype(
        jnp.bfloat16
    )
    down_share = lax.psum_scatter(grad_down, both, scatter_dimension=0, tiled=True)
    up_theirs = core_theirs(second_normed, grad_gate_up, core)
    grad_gate_up, up_theirs = lax.optimization_barrier((grad_gate_up, up_theirs))
    grad_second = against(grad_gate_up, w_up)
    _, second_back = jax.vjp(lambda v: layer_norm(v, gain_two), middle)
    (grad_from_norm,) = second_back(grad_second)
    grad_middle = grad_top.astype(jnp.float32) + grad_from_norm
    grad_branch = grad_middle.astype(jnp.bfloat16)
    sent = row_product(me_list, grad_branch, w_out, group, (up_theirs,))
    grad_near = jnp.concatenate(swap_heads(sent, group), axis=0)
    out_theirs = core_theirs(attended, delayed(grad_branch, sent), core)
    up_share = jnp.concatenate(
        [
            core_mine(second_normed, grad_gate_up, core, up_theirs),
            core_mine(attended, grad_branch, core, out_theirs),
        ],
        axis=1,
    )
    up_halves = group_first(delayed(up_share, grad_near), group)
    up_half = group_second(up_halves, group)
    grads_here, grads_near = [], [up_share, down_share]
    for pair in range(pairs):
        grads = attend_back(
            qkv[pair], query_side, key_side, stats[pair], attended_near[pair], grad_near,
            cos, sin, pair, grads_near,
        )
        grads_near = [grads, *up_halves]
        grads_here.append(swap_heads(grads.reshape(group, own_rows, 3 * PAIR), group))
    down_share = lax.psum(down_share, "far")
    grads_placed, in_theirs, grad_first = [], [], 0.0
    for pair in range(pairs):
        after = (up_half,) if pair == 0 else (in_theirs[0], down_share)
        placed = place(me_list, [grads_here[pair]], group, after)
        grads_placed.append(placed)
        in_theirs.append(core_theirs(first_normed, placed, core))
    in_share = jnp.concatenate(
        [
            core_mine(first_normed, grads_placed[pair], core, in_theirs[pair])
            for pair in range(pairs)
        ],
        axis=1,
    )
    in_first = group_first(in_share, group)
    in_half = group_second(in_first, group)
    in_chunk = far_scatter(in_half, far)
    for pair in range(pairs):
        width = 3 * PAIR * group
        part = w_in[:, pair * width : (pair + 1) * width]
        grad_first = grad_first + against(grads_placed[pair], part)
    up_chunk = far_scatter(up_half, far, (in_theirs[-1], in_share))
    up_chunk = spread(up_chunk, far, (in_first, in_half))
    total_up = doubled(up_chunk, "core", 1, 2, 1, in_chunk).astype(jnp.float32)
    wide = up_chunk.shape[1]
    total_out = jnp.concatenate([total_up[:, FF_WIDE:wide], total_up[:, wide + FF_WIDE :]], axis=1)
    total_up = jnp.concatenate([total_up[:, :FF], total_up[:, wide : wide + FF]], axis=1)
    total_down = doubled(
        delayed(down_share, in_share), "core", 1, 2, 0, in_half
    ).astype(jnp.float32)
    total_in = merged_columns(doubled(spread(in_chunk, far), "core", 1, 2, 1, ()), pairs, group)
    total_in = total_in.astype(jnp.float32)
    _, first_back = jax.vjp(lambda v: layer_norm(v, gain_one), inputs)
    (grad_inputs,) = first_back(grad_first)
    input_grad = (grad_middle + grad_inputs).astype(jnp.bfloat16)
    low_in = inproj.astype(jnp.bfloat16).astype(jnp.float32)
    low_up = upproj.astype(jnp.bfloat16).astype(jnp.float32)
    low_gains = norm_gains.astype(jnp.bfloat16).astype(jnp.float32)
    total_gains = (
        jnp.stack([jnp.sum(low_in * total_in, axis=1), jnp.sum(low_up * total_up, axis=1)], axis=1)
        / low_gains
    )
    totals = (total_in, total_out, total_up, total_down, total_gains)
    means = (inproj_mean, outproj_mean, upproj_mean, downproj_mean, gains_mean)
    squares = (inproj_square, outproj_square, upproj_square, downproj_square, gains_square)
    updates = [
        adam_update(masters[index], means[index], squares[index], totals[index], rate_list[index])
        for index in range(5)
    ]
    return (
        result.astype(jnp.bfloat16)[None],
        input_grad[None],
        updates[0][0],
        updates[0][1],
        updates[0][2],
        updates[1][0],
        updates[1][1],
        updates[1][2],
        updates[2][0],
        updates[2][1],
        updates[2][2],
        updates[3][0],
        updates[3][1],
        updates[3][2],
        updates[4][0],
        updates[4][1],
        updates[4][2],
    )


def solution(mesh):
    group_size, replicas = mesh.devices.shape
    fine = Mesh(mesh.devices.reshape(group_size, replicas // 2, 2), ("grp", "far", "core"))
    placed = (
        P(("far", "core"), "grp", None),
        P(("far", "core"), "grp"),
        P(("far", "core"), "grp", None),
        P("grp", None),
        P("grp", None),
        P("grp", None),
        P("grp", None),
        P("grp", None),
        P("grp", None),
        P("grp", None),
        P("grp", None),
        P("grp", None),
        P("grp", None),
        P("grp", None),
        P("grp", None),
        P("grp", None),
        P("grp", None),
        P("grp", None),
    )
    return jax.shard_map(
        functools.partial(local, group_size, replicas // 2),
        mesh=fine,
        in_specs=placed,
        out_specs=(
            P(("far", "core"), "grp", None),
            P(("far", "core"), "grp", None),
            P("grp", None),
            P("grp", None),
            P("grp", None),
            P("grp", None),
            P("grp", None),
            P("grp", None),
            P("grp", None),
            P("grp", None),
            P("grp", None),
            P("grp", None),
            P("grp", None),
            P("grp", None),
            P("grp", None),
            P("grp", None),
            P("grp", None),
        ),
        check_vma=False,
    )
```

```python
import functools

import jax
import jax.numpy as jnp
from jax import lax
from jax.experimental import pallas as pl
from jax.experimental.pallas import tpu as pltpu
from jax.sharding import Mesh, PartitionSpec as P

D = 1024
HEADS = 16
HEAD = 64
FF = 2624
FF_WIDE = 2688
STEP = 10
SEQ_SLOTS = 9
PAIR = 128
STAT_LANE = 16
VMEM_BYTES = 56 * 1024 * 1024


rope_base = 160000.0
norm_eps = 1e-05
rate_list = (0.1, 0.4, 0.08, 0.05, 0.6)


def layer_norm(values, gain):
    centred = values - jnp.mean(values, axis=-1, keepdims=True)
    spread = jnp.mean(centred * centred, axis=-1, keepdims=True)
    return centred * lax.rsqrt(spread + norm_eps) * gain


def positions(ids):
    live = ids >= 0
    counted = jnp.cumsum(live.astype(jnp.int32)) - 1
    onehot = (
        (ids[:, None] == jnp.arange(SEQ_SLOTS, dtype=jnp.int32)[None, :]) & live[:, None]
    ).astype(jnp.int32)
    counts = jnp.sum(onehot, axis=0)
    starts = jnp.cumsum(counts) - counts
    first = jnp.sum(onehot * starts[None, :], axis=1)
    return jnp.where(live, counted - first, 0)


def pair_tables(where_at):
    lane = jnp.arange(PAIR, dtype=jnp.int32)
    order = (lane % (HEAD // 2)).astype(jnp.float32)
    inverse = rope_base ** (-(order * 2.0 / HEAD))
    angles = where_at.astype(jnp.float32)[:, None] * inverse[None, :]
    signs = jnp.where(lane % HEAD < HEAD // 2, -1.0, 1.0)
    return jnp.cos(angles), jnp.sin(angles) * signs[None, :]


def slot_features(ids):
    lane = jnp.arange(PAIR, dtype=jnp.int32)[None, :]
    column = jnp.where(ids < 0, SEQ_SLOTS, ids)[:, None]
    own = lane == column
    query_side = jnp.where((lane <= SEQ_SLOTS) & (~own | (ids < 0)[:, None]), -1e30, 0.0)
    key_side = jnp.where(own | ((lane >= STAT_LANE) & (lane < STAT_LANE + 3)), 1.0, 0.0)
    return query_side.astype(jnp.bfloat16), key_side.astype(jnp.bfloat16)


def turned(values, cos, sin):
    lane = lax.broadcasted_iota(jnp.int32, values.shape, 1)
    half = HEAD // 2
    other = jnp.where(
        lane % HEAD < half, pltpu.roll(values, PAIR - half, 1), pltpu.roll(values, half, 1)
    )
    return values * cos + other * sin


def compiler_params():
    return pltpu.CompilerParams(vmem_limit_bytes=VMEM_BYTES)


def lower_kernel(pairs, group, core_ref, w_ref, out_ref):
    for pair in range(pairs):
        for owner in range(group):
            for part in range(3):
                source = ((part * group + owner) * pairs + pair) * PAIR
                target = ((pair * group + owner) * 3 + part) * PAIR
                out_ref[:, target : target + PAIR] = w_ref[:, source : source + PAIR].astype(
                    jnp.bfloat16
                )


def lower_half(core, weight, group):
    rows, columns = weight.shape[0] // 2, weight.shape[1]
    return pl.pallas_call(
        functools.partial(lower_kernel, D // PAIR // group, group),
        grid_spec=pltpu.PrefetchScalarGridSpec(
            num_scalar_prefetch=1,
            grid=(1,),
            in_specs=[pl.BlockSpec((rows, columns), lambda i, core: (core[0], 0))],
            out_specs=pl.BlockSpec((rows, columns), lambda i, core: (0, 0)),
        ),
        out_shape=jax.ShapeDtypeStruct((rows, columns), jnp.bfloat16),
        compiler_params=compiler_params(),
        name="lower_half",
    )(core, weight)


def project_kernel(me_ref, x_ref, w_ref, cos_ref, sin_ref, out_ref):
    got = jnp.dot(x_ref[...], w_ref[...], preferred_element_type=jnp.float32)
    cos, sin = cos_ref[0], sin_ref[0]
    query = turned(got[:, :PAIR], cos, sin) * HEAD ** (-0.5)
    keys = turned(got[:, PAIR : 2 * PAIR], cos, sin)
    out_ref[0, :, :PAIR] = query.astype(jnp.bfloat16)
    out_ref[0, :, PAIR : 2 * PAIR] = keys.astype(jnp.bfloat16)
    out_ref[0, :, 2 * PAIR :] = got[:, 2 * PAIR :].astype(jnp.bfloat16)


def skipping(kernel, before, extra):
    def body(*refs):
        kernel(*refs[:before], *refs[before + extra :])

    return body


def untouched(after):
    return [pl.BlockSpec(memory_space=pl.ANY)] * len(after)


def project(me, first_normed, w_in, cos, sin, pair, group, after=()):
    rows = first_normed.shape[0]
    return pl.pallas_call(
        skipping(project_kernel, 5, len(after)),
        grid_spec=pltpu.PrefetchScalarGridSpec(
            num_scalar_prefetch=1,
            grid=(group,),
            in_specs=[
                pl.BlockSpec((rows, D), lambda d, me: (0, 0)),
                pl.BlockSpec((D, 3 * PAIR), lambda d, me: (0, pair * group + (me[0] ^ d))),
                pl.BlockSpec((1, rows, PAIR), lambda d, me: (0, 0, 0)),
                pl.BlockSpec((1, rows, PAIR), lambda d, me: (0, 0, 0)),
                *untouched(after),
            ],
            out_specs=pl.BlockSpec((1, rows, 3 * PAIR), lambda d, me: (d, 0, 0)),
        ),
        out_shape=jax.ShapeDtypeStruct((group, rows, 3 * PAIR), jnp.bfloat16),
        compiler_params=compiler_params(),
        name="project",
    )(me, first_normed, w_in, cos, sin, *after)


def row_product_kernel(me_ref, x_ref, w_ref, out_ref):
    out_ref[0] = against(x_ref[...], w_ref[...]).astype(jnp.bfloat16)


def row_product(me, left, weight, group, after=()):
    rows = left.shape[0]
    wide = D // group
    return pl.pallas_call(
        skipping(row_product_kernel, 3, len(after)),
        grid_spec=pltpu.PrefetchScalarGridSpec(
            num_scalar_prefetch=1,
            grid=(group,),
            in_specs=[
                pl.BlockSpec((rows, D), lambda d, me: (0, 0)),
                pl.BlockSpec((wide, D), lambda d, me: (me[0] ^ d, 0)),
                *untouched(after),
            ],
            out_specs=pl.BlockSpec((1, rows, wide), lambda d, me: (d, 0, 0)),
        ),
        out_shape=jax.ShapeDtypeStruct((group, rows, wide), jnp.bfloat16),
        compiler_params=compiler_params(),
        name="row_product",
    )(me, left, weight, *after)


def place(me, pieces, group, after=()):
    rows, width = pieces[0][0].shape
    pairs = len(pieces)
    flat = [piece for near in pieces for piece in near]

    def kernel(me_ref, *refs):
        out_ref = refs[-1]
        for step in range(group):

            @pl.when(pl.program_id(0) == step)
            def _():
                for pair in range(pairs):
                    out_ref[:, pair * width : (pair + 1) * width] = refs[pair * group + step][...]

    return pl.pallas_call(
        kernel,
        grid_spec=pltpu.PrefetchScalarGridSpec(
            num_scalar_prefetch=1,
            grid=(group,),
            in_specs=[pl.BlockSpec((rows, width), lambda d, me: (0, 0))] * len(flat)
            + untouched(after),
            out_specs=pl.BlockSpec((rows, pairs * width), lambda d, me: (0, me[0] ^ d)),
        ),
        out_shape=jax.ShapeDtypeStruct((rows, group * pairs * width), jnp.bfloat16),
        compiler_params=compiler_params(),
        name="place",
    )(me, *flat, *after)


def exchange(array, axis, mask, size):
    return lax.ppermute(array, axis, [(i, i ^ mask) for i in range(size)])


def swap_heads(pieces, group):
    return [pieces[0]] + [exchange(pieces[d], "grp", d, group) for d in range(1, group)]


def assemble_kernel(me_ref, own_ref, other_ref, out_ref):
    @pl.when(pl.program_id(1) == 0)
    def _():
        out_ref[...] = own_ref[0]

    @pl.when(pl.program_id(1) == 1)
    def _():
        out_ref[...] = other_ref[0]


def near_first(part, group):
    steps = (1, 2) if group == 4 else range(1, group)
    return [exchange(part, "grp", d, group) for d in steps]


def near_second(part, near, group, after, later):
    if group == 4:
        rows = part.shape[0] // 2
        first, second = delayed(tuple(near), after)
        upper = exchange(second[:rows], "grp", 1, group)
        lower = exchange(first[rows:], "grp", 2, group)
        near = [first, second, jnp.concatenate([upper, lower], axis=0)]
    return jnp.stack([delayed(part, later), *near])


def gather_direct(own, me_core, group, by_rows):
    other = exchange(own, "core", 1, 2)
    rows, columns = own.shape[1:]
    if by_rows:
        shape = (2 * group * rows, columns)
        target = lambda d, side, me: ((me[0] ^ d) * 2 + (me[1] ^ side), 0)
    else:
        shape = (group * rows, 2 * columns)
        target = lambda d, side, me: (me[0] ^ d, me[1] ^ side)
    return pl.pallas_call(
        assemble_kernel,
        grid_spec=pltpu.PrefetchScalarGridSpec(
            num_scalar_prefetch=1,
            grid=(group, 2),
            in_specs=[pl.BlockSpec((1, rows, columns), lambda d, side, me: (d, 0, 0))] * 2,
            out_specs=pl.BlockSpec((rows, columns), target),
        ),
        out_shape=jax.ShapeDtypeStruct(shape, jnp.bfloat16),
        compiler_params=compiler_params(),
        name="assemble",
    )(me_core, own, other)


def update_kernel(rate, w_ref, m_ref, s_ref, grad_ref, mean_ref, square_ref, new_ref):
    mean, square, new = adam_update(
        w_ref[...], m_ref[...], s_ref[...], grad_ref[...].astype(jnp.float32), rate
    )
    mean_ref[...] = mean
    square_ref[...] = square
    new_ref[...] = new


def update_after(weight, mean, square, grad, rate, after):
    rows, columns = weight.shape
    block = pl.BlockSpec((32, columns), lambda i: (i, 0))
    return pl.pallas_call(
        skipping(functools.partial(update_kernel, rate), 4, len(after)),
        grid=(rows // 32,),
        in_specs=[block] * 4 + untouched(after),
        out_specs=[block] * 3,
        out_shape=[jax.ShapeDtypeStruct(weight.shape, jnp.float32)] * 3,
        compiler_params=compiler_params(),
        name="update_inproj",
    )(weight, mean, square, grad, *after)


def attend_kernel(q_ref, k_ref, v_ref, qf_ref, kf_ref, own_v_ref, own_f_ref, out_ref, stat_ref, ke):
    @pl.when(pl.program_id(0) == 0)
    def _():
        ke[:, :PAIR] = k_ref[...]
        ke[:, PAIR:] = kf_ref[...]

    query = q_ref[...]
    lane = lax.broadcasted_iota(jnp.int32, query.shape, 1)
    scores = []
    for head in range(2):
        mine = (lane < HEAD) == (head == 0)
        wide = jnp.concatenate([jnp.where(mine, query, 0), qf_ref[...]], axis=1)
        scores.append(against(wide, ke[...]))
    mixed, logs = [], []
    for head in range(2):
        top = jnp.max(scores[head], axis=1, keepdims=True)
        weights = jnp.exp(scores[head] - top)
        total = jnp.sum(weights, axis=1, keepdims=True)
        got = jnp.dot(
            weights.astype(jnp.bfloat16), v_ref[...], preferred_element_type=jnp.float32
        )
        mixed.append(got / total)
        logs.append(top + jnp.log(total))
    dead = own_f_ref[:, SEQ_SLOTS : SEQ_SLOTS + 1].astype(jnp.float32) > 0.5
    result = jnp.where(lane < HEAD, mixed[0], mixed[1]).astype(jnp.bfloat16)
    out_ref[...] = jnp.where(dead, own_v_ref[...], result)
    stat = jnp.where(lane == 0, logs[0], jnp.where(lane == 1, logs[1], 0.0))
    stat_ref[...] = jnp.where(dead, 0.0, stat)


def block_rows(rows):
    return 512 if rows <= 2048 else 256


def attend(qkv, query_side, key_side, after=()):
    rows = qkv.shape[0]
    block = block_rows(rows)

    def some(part):
        return pl.BlockSpec((block, PAIR), lambda i: (i, part))

    def whole(part):
        return pl.BlockSpec((rows, PAIR), lambda i: (0, part))

    return pl.pallas_call(
        skipping(attend_kernel, 7, len(after)),
        grid=(rows // block,),
        in_specs=[
            some(0), whole(1), whole(2), some(0), whole(0), some(2), some(0), *untouched(after),
        ],
        out_specs=[some(0), some(0)],
        out_shape=[
            jax.ShapeDtypeStruct((rows, PAIR), jnp.bfloat16),
            jax.ShapeDtypeStruct((rows, PAIR), jnp.float32),
        ],
        scratch_shapes=[pltpu.VMEM((rows, 2 * PAIR), jnp.bfloat16)],
        compiler_params=compiler_params(),
        name="attend",
    )(qkv, qkv, qkv, query_side, key_side, qkv, key_side, *after)


def in_three(column, lane):
    first = column.astype(jnp.bfloat16).astype(jnp.float32)
    second = (column - first).astype(jnp.bfloat16).astype(jnp.float32)
    third = column - first - second
    return jnp.where(
        lane == STAT_LANE,
        first,
        jnp.where(lane == STAT_LANE + 1, second, jnp.where(lane == STAT_LANE + 2, third, 0.0)),
    )


def attend_back_kernel(
    q_ref, k_ref, v_ref, qf_ref, kf_ref, stat_ref, att_ref, grad_ref, cos_ref, sin_ref,
    own_cos_ref, own_sin_ref, out_ref, ke, ve, kt, dk_sum, dv_sum,
):
    @pl.when(pl.program_id(0) == 0)
    def _():
        ke[:, :PAIR] = k_ref[...]
        ke[:, PAIR:] = kf_ref[...]
        ve[:, :PAIR] = v_ref[...]
        ve[:, PAIR:] = kf_ref[...]
        kt[...] = k_ref[...].T
        dk_sum[...] = jnp.zeros_like(dk_sum)
        dv_sum[...] = jnp.zeros_like(dv_sum)

    query, grad = q_ref[...], grad_ref[...]
    lane = lax.broadcasted_iota(jnp.int32, query.shape, 1)
    both = grad.astype(jnp.float32) * att_ref[...].astype(jnp.float32)
    stat = stat_ref[...]
    query_heads, grad_heads, weights, grad_scores, turned_grads = [], [], [], [], []
    for head in range(2):
        mine = (lane < HEAD) == (head == 0)
        query_head = jnp.where(mine, query, 0)
        grad_head = jnp.where(mine, grad, 0)
        log_total = jnp.sum(jnp.where(lane == head, stat, 0.0), axis=1, keepdims=True)
        centre = jnp.sum(jnp.where(mine, both, 0.0), axis=1, keepdims=True)
        side = (qf_ref[...].astype(jnp.float32) - in_three(log_total, lane)).astype(jnp.bfloat16)
        wide = jnp.concatenate([query_head, side], axis=1)
        weight = jnp.exp(against(ke[...], wide))
        wide_grad = jnp.concatenate(
            [grad_head, (-in_three(centre, lane)).astype(jnp.bfloat16)], axis=1
        )
        grad_score = (weight * against(ve[...], wide_grad)).astype(jnp.bfloat16)
        weights.append(weight.astype(jnp.bfloat16))
        grad_scores.append(grad_score)
        query_heads.append(query_head)
        grad_heads.append(grad_head)
        turned_grads.append(jnp.dot(kt[...], grad_score, preferred_element_type=jnp.float32))
    dv_sum[...] += jnp.dot(
        jnp.concatenate(weights, axis=1),
        jnp.concatenate(grad_heads, axis=0),
        preferred_element_type=jnp.float32,
    )
    dk_sum[...] += jnp.dot(
        jnp.concatenate(grad_scores, axis=1),
        jnp.concatenate(query_heads, axis=0),
        preferred_element_type=jnp.float32,
    )
    row = lax.broadcasted_iota(jnp.int32, turned_grads[0].shape, 0)
    grad_query = jnp.where(row < HEAD, turned_grads[0], turned_grads[1]).T * HEAD ** (-0.5)
    block = query.shape[0]
    own = pl.ds(pl.multiple_of(pl.program_id(0) * block, block), block)
    out_ref[own, :PAIR] = turned(grad_query, own_cos_ref[...], -own_sin_ref[...]).astype(
        jnp.bfloat16
    )

    @pl.when(pl.program_id(0) == pl.num_programs(0) - 1)
    def _():
        out_ref[:, PAIR : 2 * PAIR] = turned(dk_sum[...], cos_ref[...], -sin_ref[...]).astype(
            jnp.bfloat16
        )
        out_ref[:, 2 * PAIR :] = dv_sum[...].astype(jnp.bfloat16)


def attend_back(qkv, query_side, key_side, stat, attended, grad, cos, sin, pair, after=()):
    rows = qkv.shape[0]
    block = block_rows(rows)

    def some(part):
        return pl.BlockSpec((block, PAIR), lambda i: (i, part))

    def whole(part):
        return pl.BlockSpec((rows, PAIR), lambda i: (0, part))

    return pl.pallas_call(
        skipping(attend_back_kernel, 12, len(after)),
        grid=(rows // block,),
        in_specs=[
            some(0), whole(1), whole(2), some(0), whole(0), some(0), some(0), some(pair),
            whole(0), whole(0), some(0), some(0), *untouched(after),
        ],
        out_specs=pl.BlockSpec((rows, 3 * PAIR), lambda i: (0, 0)),
        out_shape=jax.ShapeDtypeStruct((rows, 3 * PAIR), jnp.bfloat16),
        scratch_shapes=[
            pltpu.VMEM((rows, 2 * PAIR), jnp.bfloat16),
            pltpu.VMEM((rows, 2 * PAIR), jnp.bfloat16),
            pltpu.VMEM((PAIR, rows), jnp.bfloat16),
            pltpu.VMEM((rows, PAIR), jnp.float32),
            pltpu.VMEM((rows, PAIR), jnp.float32),
        ],
        compiler_params=compiler_params(),
        name="attend_back",
    )(qkv, qkv, qkv, query_side, key_side, stat, attended, grad, cos, sin, cos, sin, *after)


def product(left, right):
    return jnp.dot(left, right, preferred_element_type=jnp.float32)


def contract(left, right):
    return lax.dot_general(
        left, right, (((0,), (0,)), ((), ())), preferred_element_type=jnp.float32
    )


def against(left, right):
    return lax.dot_general(
        left, right, (((1,), (1,)), ((), ())), preferred_element_type=jnp.float32
    )


def own_half(array, core):
    half = array.shape[0] // 2
    return lax.dynamic_slice_in_dim(array, core * half, half)


def gather_weight(weight, core):
    return lax.all_gather(
        own_half(weight, core).astype(jnp.bfloat16), ("grp", "core"), axis=0, tiled=True
    )


def pick(array, index, axis):
    return lax.dynamic_index_in_dim(array, index, axis, keepdims=False)


def added(*terms):
    return sum(term.astype(jnp.float32) for term in terms).astype(jnp.bfloat16)


def delayed(value, after):
    return lax.optimization_barrier((value, after))[0]


def halved(array, mask, group, dim, after=()):
    bit = (lax.axis_index("grp") // mask) % 2
    got = exchange(pick(array, 1 - bit, dim), "grp", mask, group)
    return added(delayed(pick(array, bit, dim), after), got)


def core_theirs(left, right, core):
    columns = right.shape[1] // 2
    theirs = lax.dynamic_slice_in_dim(right, (1 - core) * columns, columns, 1)
    return contract(left, theirs).astype(jnp.bfloat16)


def core_mine(left, right, core, sent):
    columns = right.shape[1] // 2
    mine = lax.dynamic_slice_in_dim(right, core * columns, columns, 1)
    got = exchange(sent, "core", 1, 2)
    return (contract(left, mine) + got.astype(jnp.float32)).astype(jnp.bfloat16)


def group_first(share, group, after=()):
    rows, columns = share.shape[0] // group, share.shape[1]
    if group != 4:
        return (lax.psum_scatter(share, "grp", scatter_dimension=0, tiled=True),)
    share = share.reshape(2, 2, rows, columns)
    return (
        halved(share[:, :, : rows // 2], 2, group, 0, after),
        halved(share[:, :, rows // 2 :], 1, group, 1, after),
    )


def group_second(halves, group, after=()):
    if group != 4:
        return halves[0]
    return jnp.concatenate(
        [halved(halves[0], 1, group, 0, after), halved(halves[1], 2, group, 0, after)], axis=0
    )


def far_masks(far):
    return [1 << bit for bit in range(far.bit_length() - 1)]


def far_scatter(share, far, waits=((), ())):
    if far > 4:
        return [lax.psum(share, "far")]
    stages = [share]
    for mask, after in zip(far_masks(far), waits):
        share = stages[-1]
        bit = (lax.axis_index("far") // mask) % 2
        rows = share.shape[0] // 2
        got = exchange(
            lax.dynamic_slice_in_dim(share, (1 - bit) * rows, rows, 0), "far", mask, far
        )
        kept = lax.dynamic_slice_in_dim(share, bit * rows, rows, 0)
        stages.append(added(delayed(kept, after), got))
    return stages


def doubled(array, axis, mask, size, dim, after):
    bit = (lax.axis_index(axis) // mask) % 2
    got = exchange(array, axis, mask, size)
    array = delayed(array, after)
    low = jnp.where(bit == 0, array, got)
    high = jnp.where(bit == 0, got, array)
    return jnp.concatenate([low, high], axis=dim)


def spread(share, far, waits=((), ())):
    if far <= 4:
        for mask, after in zip(far_masks(far)[::-1], waits):
            share = doubled(share, "far", mask, far, 0, after)
    return share


def merged_columns(total, pairs, group):
    half = 3 * PAIR * group // 2
    blocks = []
    for part in range(3):
        for owner in range(group):
            for pair in range(pairs):
                side, within = divmod((owner * 3 + part) * PAIR, half)
                column = (side * pairs + pair) * half + within
                blocks.append(total[:, column : column + PAIR])
    return jnp.concatenate(blocks, axis=1)


def spread_halves(array):
    spare = ((0, 0), (0, FF_WIDE - FF))
    return jnp.concatenate([jnp.pad(array[:, :FF], spare), jnp.pad(array[:, FF:], spare)], axis=1)


def gated(gate, upward):
    return jax.nn.gelu(gate, approximate=False) * upward


def adam_update(weight, mean, square, grad, rate):
    mean_new = 0.9 * mean + 0.1 * grad
    square_new = 0.999 * square + 0.001 * grad * grad
    step_size = mean_new / (1.0 - 0.9**STEP) / (jnp.sqrt(square_new / (1.0 - 0.999**STEP)) + 1e-08)
    return (mean_new, square_new, weight - rate * (step_size + 0.01 * weight))


def local(
    group,
    far,
    tokens,
    slot_ids,
    cotangent,
    inproj,
    outproj,
    upproj,
    downproj,
    norm_gains,
    inproj_mean,
    outproj_mean,
    upproj_mean,
    downproj_mean,
    gains_mean,
    inproj_square,
    outproj_square,
    upproj_square,
    downproj_square,
    gains_square,
):
    me = lax.axis_index("grp")
    core = lax.axis_index("core")
    me_list = me.reshape(1).astype(jnp.int32)
    core_list = core.reshape(1).astype(jnp.int32)
    pairs = D // PAIR // group
    masters = (inproj, outproj, upproj, downproj, norm_gains)
    own_rows = tokens.shape[1]
    own_gains = norm_gains.shape[0]
    both = ("grp", "core")
    w_in = lax.all_gather(lower_half(core_list, inproj, group), both, axis=0, tiled=True)
    me_core = jnp.stack([me, core]).astype(jnp.int32)
    w_outup = gather_weight(jnp.concatenate([outproj, spread_halves(upproj)], axis=1), core)
    w_out, w_up = w_outup[:, :D], w_outup[:, D:]
    packed = jnp.concatenate([norm_gains[:, 0], norm_gains[:, 1], slot_ids[0].astype(jnp.float32)])
    packed = lax.all_gather(packed.astype(jnp.bfloat16), "grp", axis=0, tiled=False)
    gain_one = packed[:, :own_gains].reshape(D).astype(jnp.float32)
    gain_two = packed[:, own_gains : 2 * own_gains].reshape(D).astype(jnp.float32)
    all_ids = packed[:, 2 * own_gains :].astype(jnp.int32).reshape(group * own_rows)
    group_rows = all_ids.shape[0]
    order = me ^ jnp.arange(group, dtype=jnp.int32)
    near_ids = all_ids.reshape(group, own_rows)[order].reshape(group_rows)
    where_at = positions(all_ids).reshape(group, own_rows)[order].reshape(group_rows)
    cos, sin = pair_tables(where_at)
    query_side, key_side = slot_features(near_ids)
    live = (slot_ids[0] >= 0).astype(jnp.bfloat16)
    inputs = tokens[0].astype(jnp.float32)
    first_normed = layer_norm(inputs, gain_one).astype(jnp.bfloat16)
    cos_near = cos.reshape(group, own_rows, PAIR)
    sin_near = sin.reshape(group, own_rows, PAIR)
    qkv, stats, attended_near, attended_here, first_sent = [], [], [], [], []
    for pair in range(pairs):
        after = first_sent[:1]
        pieces = project(me_list, first_normed, w_in, cos_near, sin_near, pair, group, after)
        first_sent.append(pieces)
        qkv.append(swap_heads(pieces, group))
    low_down = lax.dynamic_slice_in_dim(downproj, core * (D // 2), D // 2, 1).astype(jnp.bfloat16)
    for pair in range(pairs):
        qkv[pair] = jnp.concatenate([delayed(qkv[pair][0], stats[-1:]), *qkv[pair][1:]], axis=0)
        if pair == pairs - 1:
            low_down = delayed(low_down, qkv[pair])
            near_down = near_first(low_down, group)
        mixed, stat = attend(qkv[pair], query_side, key_side)
        stats.append(stat)
        attended_near.append(mixed)
        mixed = delayed(mixed, attended_here[:1])
        attended_here.append(swap_heads(mixed.reshape(group, own_rows, PAIR), group))
    attended = place(me_list, attended_here, group)
    near_down = near_second(low_down, near_down, group, stats[-1], attended)
    w_down = gather_direct(near_down, me_core, group, False)
    middle = inputs + product(attended, w_out)
    second_normed = layer_norm(middle, gain_two).astype(jnp.bfloat16)
    gate_up = product(second_normed, w_up)
    gate = gate_up[:, :FF]
    upward = gate_up[:, FF_WIDE : FF_WIDE + FF]
    hidden = gated(gate, upward).astype(jnp.bfloat16)
    result = middle + product(hidden, w_down)
    grad_top = cotangent[0] * live[:, None]
    grad_down = contract(hidden, grad_top).astype(jnp.bfloat16)
    grad_hidden = against(delayed(grad_top, grad_down), w_down)
    _, gate_back = jax.vjp(gated, gate, upward)
    grad_gate_up = spread_halves(jnp.concatenate(gate_back(grad_hidden), axis=1)).astype(
        jnp.bfloat16
    )
    down_share = lax.psum_scatter(grad_down, both, scatter_dimension=0, tiled=True)
    up_theirs = core_theirs(second_normed, grad_gate_up, core)
    grad_gate_up, up_theirs = lax.optimization_barrier((grad_gate_up, up_theirs))
    grad_second = against(grad_gate_up, w_up)
    _, second_back = jax.vjp(lambda v: layer_norm(v, gain_two), middle)
    (grad_from_norm,) = second_back(grad_second)
    grad_middle = grad_top.astype(jnp.float32) + grad_from_norm
    grad_branch = grad_middle.astype(jnp.bfloat16)
    sent = row_product(me_list, grad_branch, w_outup, group, (up_theirs,))
    grad_near = jnp.concatenate(swap_heads(sent, group), axis=0)
    out_theirs = core_theirs(attended, delayed(grad_branch, sent), core)
    up_share = jnp.concatenate(
        [
            core_mine(second_normed, grad_gate_up, core, up_theirs),
            core_mine(attended, grad_branch, core, out_theirs),
        ],
        axis=1,
    )
    grads_here, grads_near = [], [up_share]
    for pair in range(pairs):
        grads = attend_back(
            qkv[pair], query_side, key_side, stats[pair], attended_near[pair], grad_near,
            cos, sin, pair, grads_near,
        )
        if pair == 0:
            up_halves = group_first(delayed(up_share, grad_near), group, grads)
            grads_near = [grads, down_share, *up_halves]
        if pair == pairs - 1:
            up_half = group_second(up_halves, group, grads)
        if pair > 0:
            grads = delayed(grads, grads_here[0])
        grads_here.append(swap_heads(grads.reshape(group, own_rows, 3 * PAIR), group))
    down_share = lax.psum(down_share, "far")
    grads_placed, in_theirs, grad_first = [], [], 0.0
    for pair in range(pairs):
        after = (up_half,) if pair == 0 else (in_theirs[0],)
        placed = place(me_list, [grads_here[pair]], group, after)
        grads_placed.append(placed)
        in_theirs.append(core_theirs(first_normed, placed, core))
    in_share = jnp.concatenate(
        [
            core_mine(first_normed, grads_placed[pair], core, in_theirs[pair])
            for pair in range(pairs)
        ],
        axis=1,
    )
    in_first = group_first(in_share, group)
    in_half = group_second(in_first, group)
    in_stages = far_scatter(in_half, far)
    in_chunk, in_early = in_stages[-1], in_stages[min(1, len(in_stages) - 1)]
    for pair in range(pairs):
        width = 3 * PAIR * group
        part = w_in[:, pair * width : (pair + 1) * width]
        grad_first = grad_first + against(grads_placed[pair], part)
    up_chunk = far_scatter(up_half, far, (in_theirs[-1], in_share))[-1]
    up_chunk = spread(up_chunk, far, (in_first, in_half))
    up_final = doubled(up_chunk, "core", 1, 2, 1, in_early)
    total_up = up_final.astype(jnp.float32)
    wide = up_chunk.shape[1]
    total_out = jnp.concatenate([total_up[:, FF_WIDE:wide], total_up[:, wide + FF_WIDE :]], axis=1)
    total_up = jnp.concatenate([total_up[:, :FF], total_up[:, wide : wide + FF]], axis=1)
    total_down = doubled(
        delayed(down_share, in_first), "core", 1, 2, 0, in_early
    ).astype(jnp.float32)
    _, first_back = jax.vjp(lambda v: layer_norm(v, gain_one), inputs)
    (grad_inputs,) = first_back(grad_first)
    input_grad = (grad_middle + grad_inputs).astype(jnp.bfloat16)
    means = (inproj_mean, outproj_mean, upproj_mean, downproj_mean, gains_mean)
    squares = (inproj_square, outproj_square, upproj_square, downproj_square, gains_square)

    def update(index, total):
        return adam_update(masters[index], means[index], squares[index], total, rate_list[index])

    updates = [None, update(1, total_out), update(2, total_up), update(3, total_down), None]
    in_share = doubled(spread(in_chunk, far, ((), ())), "core", 1, 2, 1, ())
    low_total = merged_columns(in_share, pairs, group)
    total_in = low_total.astype(jnp.float32)
    low_in = inproj.astype(jnp.bfloat16).astype(jnp.float32)
    low_up = upproj.astype(jnp.bfloat16).astype(jnp.float32)
    low_gains = norm_gains.astype(jnp.bfloat16).astype(jnp.float32)
    total_gains = (
        jnp.stack([jnp.sum(low_in * total_in, axis=1), jnp.sum(low_up * total_up, axis=1)], axis=1)
        / low_gains
    )
    updates[0] = update_after(
        inproj, inproj_mean, inproj_square, low_total, rate_list[0],
        [updates[index][2] for index in (1, 2, 3)],
    )
    updates[4] = update(4, total_gains)
    return (
        result.astype(jnp.bfloat16)[None],
        input_grad[None],
        updates[0][0],
        updates[0][1],
        updates[0][2],
        updates[1][0],
        updates[1][1],
        updates[1][2],
        updates[2][0],
        updates[2][1],
        updates[2][2],
        updates[3][0],
        updates[3][1],
        updates[3][2],
        updates[4][0],
        updates[4][1],
        updates[4][2],
    )


def solution(mesh):
    group_size, replicas = mesh.devices.shape
    fine = Mesh(mesh.devices.reshape(group_size, replicas // 2, 2), ("grp", "far", "core"))
    placed = (
        P(("far", "core"), "grp", None),
        P(("far", "core"), "grp"),
        P(("far", "core"), "grp", None),
        P("grp", None),
        P("grp", None),
        P("grp", None),
        P("grp", None),
        P("grp", None),
        P("grp", None),
        P("grp", None),
        P("grp", None),
        P("grp", None),
        P("grp", None),
        P("grp", None),
        P("grp", None),
        P("grp", None),
        P("grp", None),
        P("grp", None),
    )
    return jax.shard_map(
        functools.partial(local, group_size, replicas // 2),
        mesh=fine,
        in_specs=placed,
        out_specs=(
            P(("far", "core"), "grp", None),
            P(("far", "core"), "grp", None),
            P("grp", None),
            P("grp", None),
            P("grp", None),
            P("grp", None),
            P("grp", None),
            P("grp", None),
            P("grp", None),
            P("grp", None),
            P("grp", None),
            P("grp", None),
            P("grp", None),
            P("grp", None),
            P("grp", None),
            P("grp", None),
            P("grp", None),
        ),
        check_vma=False,
    )
```

```python
import functools

import jax
import jax.numpy as jnp
from jax import lax
from jax.experimental import pallas as pl
from jax.experimental.pallas import tpu as pltpu
from jax.sharding import Mesh, PartitionSpec as P

D = 1024
HEADS = 16
HEAD = 64
FF = 2624
FF_WIDE = 2688
STEP = 10
SEQ_SLOTS = 9
PAIR = 128
STAT_LANE = 16
VMEM_BYTES = 56 * 1024 * 1024


rope_base = 160000.0
norm_eps = 1e-05
rate_list = (0.1, 0.4, 0.08, 0.05, 0.6)


def layer_norm(values, gain):
    centred = values - jnp.mean(values, axis=-1, keepdims=True)
    spread = jnp.mean(centred * centred, axis=-1, keepdims=True)
    return centred * lax.rsqrt(spread + norm_eps) * gain


def positions(ids):
    live = ids >= 0
    counted = jnp.cumsum(live.astype(jnp.int32)) - 1
    onehot = (
        (ids[:, None] == jnp.arange(SEQ_SLOTS, dtype=jnp.int32)[None, :]) & live[:, None]
    ).astype(jnp.int32)
    counts = jnp.sum(onehot, axis=0)
    starts = jnp.cumsum(counts) - counts
    first = jnp.sum(onehot * starts[None, :], axis=1)
    return jnp.where(live, counted - first, 0)


def pair_tables(where_at):
    lane = jnp.arange(PAIR, dtype=jnp.int32)
    order = (lane % (HEAD // 2)).astype(jnp.float32)
    inverse = rope_base ** (-(order * 2.0 / HEAD))
    angles = where_at.astype(jnp.float32)[:, None] * inverse[None, :]
    signs = jnp.where(lane % HEAD < HEAD // 2, -1.0, 1.0)
    return jnp.cos(angles), jnp.sin(angles) * signs[None, :]


def slot_features(ids):
    lane = jnp.arange(PAIR, dtype=jnp.int32)[None, :]
    column = jnp.where(ids < 0, SEQ_SLOTS, ids)[:, None]
    own = lane == column
    query_side = jnp.where((lane <= SEQ_SLOTS) & (~own | (ids < 0)[:, None]), -1e30, 0.0)
    key_side = jnp.where(own | ((lane >= STAT_LANE) & (lane < STAT_LANE + 3)), 1.0, 0.0)
    return query_side.astype(jnp.bfloat16), key_side.astype(jnp.bfloat16)


def turned(values, cos, sin):
    lane = lax.broadcasted_iota(jnp.int32, values.shape, 1)
    half = HEAD // 2
    other = jnp.where(
        lane % HEAD < half, pltpu.roll(values, PAIR - half, 1), pltpu.roll(values, half, 1)
    )
    return values * cos + other * sin


def compiler_params():
    return pltpu.CompilerParams(vmem_limit_bytes=VMEM_BYTES)


def lower_kernel(pairs, group, core_ref, w_ref, out_ref):
    for pair in range(pairs):
        for owner in range(group):
            for part in range(3):
                source = ((part * group + owner) * pairs + pair) * PAIR
                target = ((pair * group + owner) * 3 + part) * PAIR
                out_ref[:, target : target + PAIR] = w_ref[:, source : source + PAIR].astype(
                    jnp.bfloat16
                )


def lower_half(core, weight, group):
    rows, columns = weight.shape[0] // 2, weight.shape[1]
    return pl.pallas_call(
        functools.partial(lower_kernel, D // PAIR // group, group),
        grid_spec=pltpu.PrefetchScalarGridSpec(
            num_scalar_prefetch=1,
            grid=(1,),
            in_specs=[pl.BlockSpec((rows, columns), lambda i, core: (core[0], 0))],
            out_specs=pl.BlockSpec((rows, columns), lambda i, core: (0, 0)),
        ),
        out_shape=jax.ShapeDtypeStruct((rows, columns), jnp.bfloat16),
        compiler_params=compiler_params(),
        name="lower_half",
    )(core, weight)


def project_kernel(me_ref, x_ref, w_ref, cos_ref, sin_ref, out_ref):
    got = jnp.dot(x_ref[...], w_ref[...], preferred_element_type=jnp.float32)
    cos, sin = cos_ref[0], sin_ref[0]
    query = turned(got[:, :PAIR], cos, sin) * HEAD ** (-0.5)
    keys = turned(got[:, PAIR : 2 * PAIR], cos, sin)
    out_ref[0, :, :PAIR] = query.astype(jnp.bfloat16)
    out_ref[0, :, PAIR : 2 * PAIR] = keys.astype(jnp.bfloat16)
    out_ref[0, :, 2 * PAIR :] = got[:, 2 * PAIR :].astype(jnp.bfloat16)


def skipping(kernel, before, extra):
    def body(*refs):
        kernel(*refs[:before], *refs[before + extra :])

    return body


def untouched(after):
    return [pl.BlockSpec(memory_space=pl.ANY)] * len(after)


def project(me, first_normed, w_in, cos, sin, pair, group, after=()):
    rows = first_normed.shape[0]
    return pl.pallas_call(
        skipping(project_kernel, 5, len(after)),
        grid_spec=pltpu.PrefetchScalarGridSpec(
            num_scalar_prefetch=1,
            grid=(group,),
            in_specs=[
                pl.BlockSpec((rows, D), lambda d, me: (0, 0)),
                pl.BlockSpec((D, 3 * PAIR), lambda d, me: (0, pair * group + (me[0] ^ d))),
                pl.BlockSpec((1, rows, PAIR), lambda d, me: (0, 0, 0)),
                pl.BlockSpec((1, rows, PAIR), lambda d, me: (0, 0, 0)),
                *untouched(after),
            ],
            out_specs=pl.BlockSpec((1, rows, 3 * PAIR), lambda d, me: (d, 0, 0)),
        ),
        out_shape=jax.ShapeDtypeStruct((group, rows, 3 * PAIR), jnp.bfloat16),
        compiler_params=compiler_params(),
        name="project",
    )(me, first_normed, w_in, cos, sin, *after)


def row_product_kernel(me_ref, x_ref, w_ref, out_ref):
    out_ref[0] = against(x_ref[...], w_ref[...]).astype(jnp.bfloat16)


def row_product(me, left, weight, group, after=()):
    rows = left.shape[0]
    wide = D // group
    return pl.pallas_call(
        skipping(row_product_kernel, 3, len(after)),
        grid_spec=pltpu.PrefetchScalarGridSpec(
            num_scalar_prefetch=1,
            grid=(group,),
            in_specs=[
                pl.BlockSpec((rows, D), lambda d, me: (0, 0)),
                pl.BlockSpec((wide, D), lambda d, me: (me[0] ^ d, 0)),
                *untouched(after),
            ],
            out_specs=pl.BlockSpec((1, rows, wide), lambda d, me: (d, 0, 0)),
        ),
        out_shape=jax.ShapeDtypeStruct((group, rows, wide), jnp.bfloat16),
        compiler_params=compiler_params(),
        name="row_product",
    )(me, left, weight, *after)


def place(me, pieces, group, after=()):
    rows, width = pieces[0][0].shape
    pairs = len(pieces)
    flat = [piece for near in pieces for piece in near]

    def kernel(me_ref, *refs):
        out_ref = refs[-1]
        for step in range(group):

            @pl.when(pl.program_id(0) == step)
            def _():
                for pair in range(pairs):
                    out_ref[:, pair * width : (pair + 1) * width] = refs[pair * group + step][...]

    return pl.pallas_call(
        kernel,
        grid_spec=pltpu.PrefetchScalarGridSpec(
            num_scalar_prefetch=1,
            grid=(group,),
            in_specs=[pl.BlockSpec((rows, width), lambda d, me: (0, 0))] * len(flat)
            + untouched(after),
            out_specs=pl.BlockSpec((rows, pairs * width), lambda d, me: (0, me[0] ^ d)),
        ),
        out_shape=jax.ShapeDtypeStruct((rows, group * pairs * width), jnp.bfloat16),
        compiler_params=compiler_params(),
        name="place",
    )(me, *flat, *after)


def exchange(array, axis, mask, size):
    return lax.ppermute(array, axis, [(i, i ^ mask) for i in range(size)])


def swap_heads(pieces, group):
    return [pieces[0]] + [exchange(pieces[d], "grp", d, group) for d in range(1, group)]


def assemble_kernel(me_ref, own_ref, other_ref, out_ref):
    @pl.when(pl.program_id(1) == 0)
    def _():
        out_ref[...] = own_ref[0]

    @pl.when(pl.program_id(1) == 1)
    def _():
        out_ref[...] = other_ref[0]


def near_parts(part, group):
    if group != 4:
        return jnp.stack([part] + [exchange(part, "grp", d, group) for d in range(1, group)])
    rows = part.shape[0] // 2
    first, second = [exchange(part, "grp", d, group) for d in (1, 2)]
    upper = exchange(second[:rows], "grp", 1, group)
    lower = exchange(first[rows:], "grp", 2, group)
    return jnp.stack([part, first, second, jnp.concatenate([upper, lower], axis=0)])


def gather_direct(own, me_core, group, by_rows):
    other = exchange(own, "core", 1, 2)
    rows, columns = own.shape[1:]
    if by_rows:
        shape = (2 * group * rows, columns)
        target = lambda d, side, me: ((me[0] ^ d) * 2 + (me[1] ^ side), 0)
    else:
        shape = (group * rows, 2 * columns)
        target = lambda d, side, me: (me[0] ^ d, me[1] ^ side)
    return pl.pallas_call(
        assemble_kernel,
        grid_spec=pltpu.PrefetchScalarGridSpec(
            num_scalar_prefetch=1,
            grid=(group, 2),
            in_specs=[pl.BlockSpec((1, rows, columns), lambda d, side, me: (d, 0, 0))] * 2,
            out_specs=pl.BlockSpec((rows, columns), target),
        ),
        out_shape=jax.ShapeDtypeStruct(shape, jnp.bfloat16),
        compiler_params=compiler_params(),
        name="assemble",
    )(me_core, own, other)


def merge_kernel(pairs, group, core_ref, own_ref, other_ref, out_ref):
    low, high = [], []
    half = 3 * PAIR * group // 2
    first = core_ref[0] == 0
    for part in range(3):
        for owner in range(group):
            for pair in range(pairs):
                side, within = divmod((owner * 3 + part) * PAIR, half)
                source = pl.ds(pair * half + within, PAIR)
                target = ((part * group + owner) * pairs + pair) * PAIR
                own, other = own_ref[:, source], other_ref[:, source]
                chosen = jnp.where(first, own, other) if side == 0 else jnp.where(first, other, own)
                out_ref[:, target : target + PAIR] = chosen


def merged_columns(core, own, other, pairs, group, after):
    rows, columns = own.shape
    block = pl.BlockSpec((rows, columns), lambda i, core: (0, 0))
    return pl.pallas_call(
        skipping(functools.partial(merge_kernel, pairs, group), 3, len(after)),
        grid_spec=pltpu.PrefetchScalarGridSpec(
            num_scalar_prefetch=1,
            grid=(1,),
            in_specs=[block, block, *untouched(after)],
            out_specs=pl.BlockSpec((rows, 2 * columns), lambda i, core: (0, 0)),
        ),
        out_shape=jax.ShapeDtypeStruct((rows, 2 * columns), jnp.bfloat16),
        compiler_params=compiler_params(),
        name="merge",
    )(core, own, other, *after)


def attend_kernel(q_ref, k_ref, v_ref, qf_ref, kf_ref, own_v_ref, own_f_ref, out_ref, stat_ref, ke):
    @pl.when(pl.program_id(0) == 0)
    def _():
        ke[:, :PAIR] = k_ref[...]
        ke[:, PAIR:] = kf_ref[...]

    query = q_ref[...]
    lane = lax.broadcasted_iota(jnp.int32, query.shape, 1)
    scores = []
    for head in range(2):
        mine = (lane < HEAD) == (head == 0)
        wide = jnp.concatenate([jnp.where(mine, query, 0), qf_ref[...]], axis=1)
        scores.append(against(wide, ke[...]))
    mixed, logs = [], []
    for head in range(2):
        top = jnp.max(scores[head], axis=1, keepdims=True)
        weights = jnp.exp(scores[head] - top)
        total = jnp.sum(weights, axis=1, keepdims=True)
        got = jnp.dot(
            weights.astype(jnp.bfloat16), v_ref[...], preferred_element_type=jnp.float32
        )
        mixed.append(got / total)
        logs.append(top + jnp.log(total))
    dead = own_f_ref[:, SEQ_SLOTS : SEQ_SLOTS + 1].astype(jnp.float32) > 0.5
    result = jnp.where(lane < HEAD, mixed[0], mixed[1]).astype(jnp.bfloat16)
    out_ref[...] = jnp.where(dead, own_v_ref[...], result)
    stat = jnp.where(lane == 0, logs[0], jnp.where(lane == 1, logs[1], 0.0))
    stat_ref[...] = jnp.where(dead, 0.0, stat)


def block_rows(rows):
    return 512 if rows <= 2048 else 256


def attend(qkv, query_side, key_side, after=()):
    rows = qkv.shape[0]
    block = block_rows(rows)

    def some(part):
        return pl.BlockSpec((block, PAIR), lambda i: (i, part))

    def whole(part):
        return pl.BlockSpec((rows, PAIR), lambda i: (0, part))

    return pl.pallas_call(
        skipping(attend_kernel, 7, len(after)),
        grid=(rows // block,),
        in_specs=[
            some(0), whole(1), whole(2), some(0), whole(0), some(2), some(0), *untouched(after),
        ],
        out_specs=[some(0), some(0)],
        out_shape=[
            jax.ShapeDtypeStruct((rows, PAIR), jnp.bfloat16),
            jax.ShapeDtypeStruct((rows, PAIR), jnp.float32),
        ],
        scratch_shapes=[pltpu.VMEM((rows, 2 * PAIR), jnp.bfloat16)],
        compiler_params=compiler_params(),
        name="attend",
    )(qkv, qkv, qkv, query_side, key_side, qkv, key_side, *after)


def in_three(column, lane):
    first = column.astype(jnp.bfloat16).astype(jnp.float32)
    second = (column - first).astype(jnp.bfloat16).astype(jnp.float32)
    third = column - first - second
    return jnp.where(
        lane == STAT_LANE,
        first,
        jnp.where(lane == STAT_LANE + 1, second, jnp.where(lane == STAT_LANE + 2, third, 0.0)),
    )


def attend_back_kernel(
    q_ref, k_ref, v_ref, qf_ref, kf_ref, stat_ref, att_ref, grad_ref, cos_ref, sin_ref,
    own_cos_ref, own_sin_ref, out_ref, ke, ve, kt, dk_sum, dv_sum,
):
    @pl.when(pl.program_id(0) == 0)
    def _():
        ke[:, :PAIR] = k_ref[...]
        ke[:, PAIR:] = kf_ref[...]
        ve[:, :PAIR] = v_ref[...]
        ve[:, PAIR:] = kf_ref[...]
        kt[...] = k_ref[...].T
        dk_sum[...] = jnp.zeros_like(dk_sum)
        dv_sum[...] = jnp.zeros_like(dv_sum)

    query, grad = q_ref[...], grad_ref[...]
    lane = lax.broadcasted_iota(jnp.int32, query.shape, 1)
    both = grad.astype(jnp.float32) * att_ref[...].astype(jnp.float32)
    stat = stat_ref[...]
    query_heads, grad_heads, weights, grad_scores, turned_grads = [], [], [], [], []
    for head in range(2):
        mine = (lane < HEAD) == (head == 0)
        query_head = jnp.where(mine, query, 0)
        grad_head = jnp.where(mine, grad, 0)
        log_total = jnp.sum(jnp.where(lane == head, stat, 0.0), axis=1, keepdims=True)
        centre = jnp.sum(jnp.where(mine, both, 0.0), axis=1, keepdims=True)
        side = (qf_ref[...].astype(jnp.float32) - in_three(log_total, lane)).astype(jnp.bfloat16)
        wide = jnp.concatenate([query_head, side], axis=1)
        weight = jnp.exp(against(ke[...], wide))
        wide_grad = jnp.concatenate(
            [grad_head, (-in_three(centre, lane)).astype(jnp.bfloat16)], axis=1
        )
        grad_score = (weight * against(ve[...], wide_grad)).astype(jnp.bfloat16)
        weights.append(weight.astype(jnp.bfloat16))
        grad_scores.append(grad_score)
        query_heads.append(query_head)
        grad_heads.append(grad_head)
        turned_grads.append(jnp.dot(kt[...], grad_score, preferred_element_type=jnp.float32))
    dv_sum[...] += jnp.dot(
        jnp.concatenate(weights, axis=1),
        jnp.concatenate(grad_heads, axis=0),
        preferred_element_type=jnp.float32,
    )
    dk_sum[...] += jnp.dot(
        jnp.concatenate(grad_scores, axis=1),
        jnp.concatenate(query_heads, axis=0),
        preferred_element_type=jnp.float32,
    )
    row = lax.broadcasted_iota(jnp.int32, turned_grads[0].shape, 0)
    grad_query = jnp.where(row < HEAD, turned_grads[0], turned_grads[1]).T * HEAD ** (-0.5)
    block = query.shape[0]
    own = pl.ds(pl.multiple_of(pl.program_id(0) * block, block), block)
    out_ref[own, :PAIR] = turned(grad_query, own_cos_ref[...], -own_sin_ref[...]).astype(
        jnp.bfloat16
    )

    @pl.when(pl.program_id(0) == pl.num_programs(0) - 1)
    def _():
        out_ref[:, PAIR : 2 * PAIR] = turned(dk_sum[...], cos_ref[...], -sin_ref[...]).astype(
            jnp.bfloat16
        )
        out_ref[:, 2 * PAIR :] = dv_sum[...].astype(jnp.bfloat16)


def attend_back(qkv, query_side, key_side, stat, attended, grad, cos, sin, pair, after=()):
    rows = qkv.shape[0]
    block = block_rows(rows)

    def some(part):
        return pl.BlockSpec((block, PAIR), lambda i: (i, part))

    def whole(part):
        return pl.BlockSpec((rows, PAIR), lambda i: (0, part))

    return pl.pallas_call(
        skipping(attend_back_kernel, 12, len(after)),
        grid=(rows // block,),
        in_specs=[
            some(0), whole(1), whole(2), some(0), whole(0), some(0), some(0), some(pair),
            whole(0), whole(0), some(0), some(0), *untouched(after),
        ],
        out_specs=pl.BlockSpec((rows, 3 * PAIR), lambda i: (0, 0)),
        out_shape=jax.ShapeDtypeStruct((rows, 3 * PAIR), jnp.bfloat16),
        scratch_shapes=[
            pltpu.VMEM((rows, 2 * PAIR), jnp.bfloat16),
            pltpu.VMEM((rows, 2 * PAIR), jnp.bfloat16),
            pltpu.VMEM((PAIR, rows), jnp.bfloat16),
            pltpu.VMEM((rows, PAIR), jnp.float32),
            pltpu.VMEM((rows, PAIR), jnp.float32),
        ],
        compiler_params=compiler_params(),
        name="attend_back",
    )(qkv, qkv, qkv, query_side, key_side, stat, attended, grad, cos, sin, cos, sin, *after)


def product(left, right):
    return jnp.dot(left, right, preferred_element_type=jnp.float32)


def contract(left, right):
    return lax.dot_general(
        left, right, (((0,), (0,)), ((), ())), preferred_element_type=jnp.float32
    )


def against(left, right):
    return lax.dot_general(
        left, right, (((1,), (1,)), ((), ())), preferred_element_type=jnp.float32
    )


def own_half(array, core):
    half = array.shape[0] // 2
    return lax.dynamic_slice_in_dim(array, core * half, half)


def gather_weight(weight, core):
    return lax.all_gather(
        own_half(weight, core).astype(jnp.bfloat16), ("grp", "core"), axis=0, tiled=True
    )


def pick(array, index, axis):
    return lax.dynamic_index_in_dim(array, index, axis, keepdims=False)


def added(*terms):
    return sum(term.astype(jnp.float32) for term in terms).astype(jnp.bfloat16)


def delayed(value, after):
    return lax.optimization_barrier((value, after))[0]


def halved(array, mask, group, dim, after=()):
    bit = (lax.axis_index("grp") // mask) % 2
    got = exchange(pick(array, 1 - bit, dim), "grp", mask, group)
    return added(delayed(pick(array, bit, dim), after), got)


def core_theirs(left, right, core):
    columns = right.shape[1] // 2
    theirs = lax.dynamic_slice_in_dim(right, (1 - core) * columns, columns, 1)
    return contract(left, theirs).astype(jnp.bfloat16)


def core_mine(left, right, core, sent):
    columns = right.shape[1] // 2
    mine = lax.dynamic_slice_in_dim(right, core * columns, columns, 1)
    got = exchange(sent, "core", 1, 2)
    return (contract(left, mine) + got.astype(jnp.float32)).astype(jnp.bfloat16)


def group_first(share, group, after=()):
    rows, columns = share.shape[0] // group, share.shape[1]
    if group != 4:
        return (lax.psum_scatter(share, "grp", scatter_dimension=0, tiled=True),)
    share = share.reshape(2, 2, rows, columns)
    return (
        halved(share[:, :, : rows // 2], 2, group, 0, after),
        halved(share[:, :, rows // 2 :], 1, group, 1, after),
    )


def group_second(halves, group, after=()):
    if group != 4:
        return halves[0]
    return jnp.concatenate(
        [halved(halves[0], 1, group, 0, after), halved(halves[1], 2, group, 0, after)], axis=0
    )


def far_masks(far):
    return [1 << bit for bit in range(far.bit_length() - 1)]


def far_scatter(share, far, waits=((), ()), dim=0):
    if far > 4:
        return [lax.psum(share, "far")]
    stages = [share]
    for mask, after in zip(far_masks(far), waits):
        share = stages[-1]
        bit = (lax.axis_index("far") // mask) % 2
        size = share.shape[dim] // 2
        got = exchange(
            lax.dynamic_slice_in_dim(share, (1 - bit) * size, size, dim), "far", mask, far
        )
        kept = lax.dynamic_slice_in_dim(share, bit * size, size, dim)
        stages.append(added(delayed(kept, after), got))
    return stages


def doubled(array, axis, mask, size, dim, after):
    bit = (lax.axis_index(axis) // mask) % 2
    got = exchange(array, axis, mask, size)
    array = delayed(array, after)
    low = jnp.where(bit == 0, array, got)
    high = jnp.where(bit == 0, got, array)
    return jnp.concatenate([low, high], axis=dim)


def spread(share, far, waits=((), ()), dim=0):
    if far <= 4:
        for mask, after in zip(far_masks(far)[::-1], waits):
            share = doubled(share, "far", mask, far, dim, after)
    return share


def spread_halves(array):
    spare = ((0, 0), (0, FF_WIDE - FF))
    return jnp.concatenate([jnp.pad(array[:, :FF], spare), jnp.pad(array[:, FF:], spare)], axis=1)


def gated(gate, upward):
    return jax.nn.gelu(gate, approximate=False) * upward


def adam_update(weight, mean, square, grad, rate):
    mean_new = 0.9 * mean + 0.1 * grad
    square_new = 0.999 * square + 0.001 * grad * grad
    step_size = mean_new / (1.0 - 0.9**STEP) / (jnp.sqrt(square_new / (1.0 - 0.999**STEP)) + 1e-08)
    return (mean_new, square_new, weight - rate * (step_size + 0.01 * weight))


def local(
    group,
    far,
    tokens,
    slot_ids,
    cotangent,
    inproj,
    outproj,
    upproj,
    downproj,
    norm_gains,
    inproj_mean,
    outproj_mean,
    upproj_mean,
    downproj_mean,
    gains_mean,
    inproj_square,
    outproj_square,
    upproj_square,
    downproj_square,
    gains_square,
):
    me = lax.axis_index("grp")
    core = lax.axis_index("core")
    me_list = me.reshape(1).astype(jnp.int32)
    core_list = core.reshape(1).astype(jnp.int32)
    pairs = D // PAIR // group
    masters = (inproj, outproj, upproj, downproj, norm_gains)
    own_rows = tokens.shape[1]
    own_gains = norm_gains.shape[0]
    both = ("grp", "core")
    w_in = lax.all_gather(lower_half(core_list, inproj, group), both, axis=0, tiled=True)
    me_core = jnp.stack([me, core]).astype(jnp.int32)
    w_outup = gather_weight(jnp.concatenate([outproj, spread_halves(upproj)], axis=1), core)
    w_out, w_up = w_outup[:, :D], w_outup[:, D:]
    packed = jnp.concatenate([norm_gains[:, 0], norm_gains[:, 1], slot_ids[0].astype(jnp.float32)])
    packed = lax.all_gather(packed.astype(jnp.bfloat16), "grp", axis=0, tiled=False)
    gain_one = packed[:, :own_gains].reshape(D).astype(jnp.float32)
    gain_two = packed[:, own_gains : 2 * own_gains].reshape(D).astype(jnp.float32)
    all_ids = packed[:, 2 * own_gains :].astype(jnp.int32).reshape(group * own_rows)
    group_rows = all_ids.shape[0]
    order = me ^ jnp.arange(group, dtype=jnp.int32)
    near_ids = all_ids.reshape(group, own_rows)[order].reshape(group_rows)
    where_at = positions(all_ids).reshape(group, own_rows)[order].reshape(group_rows)
    cos, sin = pair_tables(where_at)
    query_side, key_side = slot_features(near_ids)
    live = (slot_ids[0] >= 0).astype(jnp.bfloat16)
    inputs = tokens[0].astype(jnp.float32)
    first_normed = layer_norm(inputs, gain_one).astype(jnp.bfloat16)
    cos_near = cos.reshape(group, own_rows, PAIR)
    sin_near = sin.reshape(group, own_rows, PAIR)
    shares = 2 * far if far <= 4 else 2
    place_of = core * far + lax.axis_index("far") if far <= 4 else core
    low_down = lax.dynamic_slice_in_dim(
        downproj, place_of * (D // shares), D // shares, 1
    ).astype(jnp.bfloat16)
    near_down = near_parts(low_down, group)
    qkv, stats, attended_near, attended_here, first_sent = [], [], [], [], []
    for pair in range(pairs):
        after = first_sent[:1] + [near_down] * (pair == pairs - 1)
        pieces = project(me_list, first_normed, w_in, cos_near, sin_near, pair, group, after)
        first_sent.append(pieces)
        qkv.append(swap_heads(pieces, group))
    for pair in range(pairs):
        qkv[pair] = jnp.concatenate([delayed(qkv[pair][0], stats[-1:]), *qkv[pair][1:]], axis=0)
        mixed, stat = attend(qkv[pair], query_side, key_side)
        stats.append(stat)
        attended_near.append(mixed)
        mixed = delayed(mixed, attended_here[:1])
        attended_here.append(swap_heads(mixed.reshape(group, own_rows, PAIR), group))
    attended = place(me_list, attended_here, group)
    if far <= 4:
        for mask, after in zip(far_masks(far), (qkv[0][:8], attended)):
            near_down = doubled(near_down, "far", mask, far, 2, after)
    w_down = gather_direct(near_down, me_core, group, False)
    middle = inputs + product(attended, w_out)
    second_normed = layer_norm(middle, gain_two).astype(jnp.bfloat16)
    gate_up = product(second_normed, w_up)
    gate = gate_up[:, :FF]
    upward = gate_up[:, FF_WIDE : FF_WIDE + FF]
    hidden = gated(gate, upward).astype(jnp.bfloat16)
    result = middle + product(hidden, w_down)
    grad_top = cotangent[0] * live[:, None]
    grad_down = contract(hidden, grad_top).astype(jnp.bfloat16)
    grad_hidden = against(delayed(grad_top, grad_down), w_down)
    _, gate_back = jax.vjp(gated, gate, upward)
    grad_gate_up = spread_halves(jnp.concatenate(gate_back(grad_hidden), axis=1)).astype(
        jnp.bfloat16
    )
    down_share = lax.psum_scatter(grad_down, both, scatter_dimension=0, tiled=True)
    up_theirs = core_theirs(second_normed, grad_gate_up, core)
    grad_gate_up, up_theirs = lax.optimization_barrier((grad_gate_up, up_theirs))
    grad_second = against(grad_gate_up, w_up)
    _, second_back = jax.vjp(lambda v: layer_norm(v, gain_two), middle)
    (grad_from_norm,) = second_back(grad_second)
    grad_middle = grad_top.astype(jnp.float32) + grad_from_norm
    grad_branch = grad_middle.astype(jnp.bfloat16)
    sent = row_product(me_list, grad_branch, w_outup, group, (up_theirs,))
    grad_near = jnp.concatenate(swap_heads(sent, group), axis=0)
    out_theirs = core_theirs(attended, delayed(grad_branch, sent), core)
    up_share = jnp.concatenate(
        [
            core_mine(second_normed, grad_gate_up, core, up_theirs),
            core_mine(attended, grad_branch, core, out_theirs),
        ],
        axis=1,
    )
    grads_here, grads_near, in_theirs = [], [up_share], []
    for pair in range(pairs):
        grads = attend_back(
            qkv[pair], query_side, key_side, stats[pair], attended_near[pair], grad_near,
            cos, sin, pair, grads_near,
        )
        if pair == 0:
            up_halves = group_first(delayed(up_share, grad_near), group, grads)
            grads_near = [grads, *up_halves]
            down_share = delayed(down_share, grads)
        if pair == pairs - 1:
            up_half = group_second(up_halves, group, grads)
            down_stages = far_scatter(down_share, far, (grads, in_theirs), 1)
            down_early, down_share = down_stages[min(1, len(down_stages) - 1)], down_stages[-1]
        if pair > 0:
            grads = delayed(grads, (grads_here[0], down_early))
        grads_here.append(swap_heads(grads.reshape(group, own_rows, 3 * PAIR), group))
    grads_placed, grad_first = [], 0.0
    for pair in range(pairs):
        after = (up_half,) if pair == 0 else (in_theirs[0], down_share)
        placed = place(me_list, [grads_here[pair]], group, after)
        grads_placed.append(placed)
        in_theirs.append(core_theirs(first_normed, placed, core))
    in_share = jnp.concatenate(
        [
            core_mine(first_normed, grads_placed[pair], core, in_theirs[pair])
            for pair in range(pairs)
        ],
        axis=1,
    )
    in_first = group_first(in_share, group)
    in_half = group_second(in_first, group)
    in_stages = far_scatter(in_half, far)
    in_chunk, in_early = in_stages[-1], in_stages[min(1, len(in_stages) - 1)]
    for pair in range(pairs):
        width = 3 * PAIR * group
        part = w_in[:, pair * width : (pair + 1) * width]
        grad_first = grad_first + against(delayed(grads_placed[pair], in_share), part)
    up_chunk = far_scatter(up_half, far, (in_theirs[-1], in_share))[-1]
    up_chunk = spread(up_chunk, far, (in_first, in_half))
    up_final = doubled(up_chunk, "core", 1, 2, 1, in_early)
    total_up = up_final.astype(jnp.float32)
    wide = up_chunk.shape[1]
    total_out = jnp.concatenate([total_up[:, FF_WIDE:wide], total_up[:, wide + FF_WIDE :]], axis=1)
    total_up = jnp.concatenate([total_up[:, :FF], total_up[:, wide : wide + FF]], axis=1)
    down_share = spread(down_share, far, (in_share, in_first), 1)
    total_down = doubled(down_share, "core", 1, 2, 0, in_early).astype(jnp.float32)
    _, first_back = jax.vjp(lambda v: layer_norm(v, gain_one), inputs)
    (grad_inputs,) = first_back(grad_first)
    input_grad = (grad_middle + grad_inputs).astype(jnp.bfloat16)
    means = (inproj_mean, outproj_mean, upproj_mean, downproj_mean, gains_mean)
    squares = (inproj_square, outproj_square, upproj_square, downproj_square, gains_square)

    def update(index, total):
        return adam_update(masters[index], means[index], squares[index], total, rate_list[index])

    updates = [None, update(1, total_out), update(2, total_up), update(3, total_down), None]
    in_chunk = spread(in_chunk, far)
    total_in = merged_columns(
        core_list, in_chunk, exchange(in_chunk, "core", 1, 2), pairs, group,
        [updates[index][2] for index in (1, 2, 3)],
    ).astype(jnp.float32)
    low_in = inproj.astype(jnp.bfloat16).astype(jnp.float32)
    low_up = upproj.astype(jnp.bfloat16).astype(jnp.float32)
    low_gains = norm_gains.astype(jnp.bfloat16).astype(jnp.float32)
    total_gains = (
        jnp.stack([jnp.sum(low_in * total_in, axis=1), jnp.sum(low_up * total_up, axis=1)], axis=1)
        / low_gains
    )
    updates[0] = update(0, total_in)
    updates[4] = update(4, total_gains)
    return (
        result.astype(jnp.bfloat16)[None],
        input_grad[None],
        updates[0][0],
        updates[0][1],
        updates[0][2],
        updates[1][0],
        updates[1][1],
        updates[1][2],
        updates[2][0],
        updates[2][1],
        updates[2][2],
        updates[3][0],
        updates[3][1],
        updates[3][2],
        updates[4][0],
        updates[4][1],
        updates[4][2],
    )


def solution(mesh):
    group_size, replicas = mesh.devices.shape
    fine = Mesh(mesh.devices.reshape(group_size, replicas // 2, 2), ("grp", "far", "core"))
    placed = (
        P(("far", "core"), "grp", None),
        P(("far", "core"), "grp"),
        P(("far", "core"), "grp", None),
        P("grp", None),
        P("grp", None),
        P("grp", None),
        P("grp", None),
        P("grp", None),
        P("grp", None),
        P("grp", None),
        P("grp", None),
        P("grp", None),
        P("grp", None),
        P("grp", None),
        P("grp", None),
        P("grp", None),
        P("grp", None),
        P("grp", None),
    )
    return jax.shard_map(
        functools.partial(local, group_size, replicas // 2),
        mesh=fine,
        in_specs=placed,
        out_specs=(
            P(("far", "core"), "grp", None),
            P(("far", "core"), "grp", None),
            P("grp", None),
            P("grp", None),
            P("grp", None),
            P("grp", None),
            P("grp", None),
            P("grp", None),
            P("grp", None),
            P("grp", None),
            P("grp", None),
            P("grp", None),
            P("grp", None),
            P("grp", None),
            P("grp", None),
            P("grp", None),
            P("grp", None),
        ),
        check_vma=False,
    )
```

```python
import functools
import math

import jax
import jax.numpy as jnp
from jax import lax
from jax.experimental import pallas as pl
from jax.experimental.pallas import tpu as pltpu
from jax.sharding import Mesh, PartitionSpec as P

D = 1024
HEADS = 16
HEAD = 64
FF = 2624
FF_WIDE = 2688
STEP = 10
SEQ_SLOTS = 9
PAIR = 128
STAT_LANE = 16
VMEM_BYTES = 56 * 1024 * 1024


rope_base = 160000.0
norm_eps = 1e-05
rate_list = (0.1, 0.4, 0.08, 0.05, 0.6)


def layer_norm(values, gain):
    centred = values - jnp.mean(values, axis=-1, keepdims=True)
    spread = jnp.mean(centred * centred, axis=-1, keepdims=True)
    return centred * lax.rsqrt(spread + norm_eps) * gain


def positions(ids):
    live = ids >= 0
    counted = jnp.cumsum(live.astype(jnp.int32)) - 1
    onehot = (
        (ids[:, None] == jnp.arange(SEQ_SLOTS, dtype=jnp.int32)[None, :]) & live[:, None]
    ).astype(jnp.int32)
    counts = jnp.sum(onehot, axis=0)
    starts = jnp.cumsum(counts) - counts
    first = jnp.sum(onehot * starts[None, :], axis=1)
    return jnp.where(live, counted - first, 0)


def pair_tables(where_at):
    lane = jnp.arange(PAIR, dtype=jnp.int32)
    order = (lane % (HEAD // 2)).astype(jnp.float32)
    inverse = rope_base ** (-(order * 2.0 / HEAD))
    angles = where_at.astype(jnp.float32)[:, None] * inverse[None, :]
    signs = jnp.where(lane % HEAD < HEAD // 2, -1.0, 1.0)
    return jnp.cos(angles), jnp.sin(angles) * signs[None, :]


def slot_features(ids):
    lane = jnp.arange(PAIR, dtype=jnp.int32)[None, :]
    column = jnp.where(ids < 0, SEQ_SLOTS, ids)[:, None]
    own = lane == column
    query_side = jnp.where((lane <= SEQ_SLOTS) & (~own | (ids < 0)[:, None]), -1e30, 0.0)
    key_side = jnp.where(own | ((lane >= STAT_LANE) & (lane < STAT_LANE + 3)), 1.0, 0.0)
    return query_side.astype(jnp.bfloat16), key_side.astype(jnp.bfloat16)


def turned(values, cos, sin):
    lane = lax.broadcasted_iota(jnp.int32, values.shape, 1)
    half = HEAD // 2
    other = jnp.where(
        lane % HEAD < half, pltpu.roll(values, PAIR - half, 1), pltpu.roll(values, half, 1)
    )
    return values * cos + other * sin


def compiler_params():
    return pltpu.CompilerParams(vmem_limit_bytes=VMEM_BYTES)


def lower_kernel(pairs, group, core_ref, w_ref, out_ref):
    for pair in range(pairs):
        for owner in range(group):
            for part in range(3):
                source = ((part * group + owner) * pairs + pair) * PAIR
                target = ((pair * group + owner) * 3 + part) * PAIR
                out_ref[:, target : target + PAIR] = w_ref[:, source : source + PAIR].astype(
                    jnp.bfloat16
                )


def lower_half(core, weight, group):
    rows, columns = weight.shape[0] // 2, weight.shape[1]
    return pl.pallas_call(
        functools.partial(lower_kernel, D // PAIR // group, group),
        grid_spec=pltpu.PrefetchScalarGridSpec(
            num_scalar_prefetch=1,
            grid=(1,),
            in_specs=[pl.BlockSpec((rows, columns), lambda i, core: (core[0], 0))],
            out_specs=pl.BlockSpec((rows, columns), lambda i, core: (0, 0)),
        ),
        out_shape=jax.ShapeDtypeStruct((rows, columns), jnp.bfloat16),
        compiler_params=compiler_params(),
        name="lower_half",
    )(core, weight)


def project_kernel(me_ref, x_ref, w_ref, cos_ref, sin_ref, out_ref):
    got = jnp.dot(x_ref[...], w_ref[...], preferred_element_type=jnp.float32)
    cos, sin = cos_ref[0], sin_ref[0]
    query = turned(got[:, :PAIR], cos, sin) * HEAD ** (-0.5)
    keys = turned(got[:, PAIR : 2 * PAIR], cos, sin)
    out_ref[0, :, :PAIR] = query.astype(jnp.bfloat16)
    out_ref[0, :, PAIR : 2 * PAIR] = keys.astype(jnp.bfloat16)
    out_ref[0, :, 2 * PAIR :] = got[:, 2 * PAIR :].astype(jnp.bfloat16)


def skipping(kernel, before, extra):
    def body(*refs):
        kernel(*refs[:before], *refs[before + extra :])

    return body


def untouched(after):
    return [pl.BlockSpec(memory_space=pl.ANY)] * len(after)


def project(me, first_normed, w_in, cos, sin, pair, group, after=()):
    rows = first_normed.shape[0]
    return pl.pallas_call(
        skipping(project_kernel, 5, len(after)),
        grid_spec=pltpu.PrefetchScalarGridSpec(
            num_scalar_prefetch=1,
            grid=(group,),
            in_specs=[
                pl.BlockSpec((rows, D), lambda d, me: (0, 0)),
                pl.BlockSpec((D, 3 * PAIR), lambda d, me: (0, pair * group + (me[0] ^ d))),
                pl.BlockSpec((1, rows, PAIR), lambda d, me: (0, 0, 0)),
                pl.BlockSpec((1, rows, PAIR), lambda d, me: (0, 0, 0)),
                *untouched(after),
            ],
            out_specs=pl.BlockSpec((1, rows, 3 * PAIR), lambda d, me: (d, 0, 0)),
        ),
        out_shape=jax.ShapeDtypeStruct((group, rows, 3 * PAIR), jnp.bfloat16),
        compiler_params=compiler_params(),
        name="project",
    )(me, first_normed, w_in, cos, sin, *after)


def row_product_kernel(me_ref, x_ref, w_ref, out_ref):
    out_ref[0] = against(x_ref[...], w_ref[...]).astype(jnp.bfloat16)


def row_product(me, left, weight, group, after=()):
    rows = left.shape[0]
    wide = D // group
    return pl.pallas_call(
        skipping(row_product_kernel, 3, len(after)),
        grid_spec=pltpu.PrefetchScalarGridSpec(
            num_scalar_prefetch=1,
            grid=(group,),
            in_specs=[
                pl.BlockSpec((rows, D), lambda d, me: (0, 0)),
                pl.BlockSpec((wide, D), lambda d, me: (me[0] ^ d, 0)),
                *untouched(after),
            ],
            out_specs=pl.BlockSpec((1, rows, wide), lambda d, me: (d, 0, 0)),
        ),
        out_shape=jax.ShapeDtypeStruct((group, rows, wide), jnp.bfloat16),
        compiler_params=compiler_params(),
        name="row_product",
    )(me, left, weight, *after)


def place(me, pieces, group, after=()):
    rows, width = pieces[0][0].shape
    pairs = len(pieces)
    flat = [piece for near in pieces for piece in near]

    def kernel(me_ref, *refs):
        out_ref = refs[-1]
        for step in range(group):

            @pl.when(pl.program_id(0) == step)
            def _():
                for pair in range(pairs):
                    out_ref[:, pair * width : (pair + 1) * width] = refs[pair * group + step][...]

    return pl.pallas_call(
        kernel,
        grid_spec=pltpu.PrefetchScalarGridSpec(
            num_scalar_prefetch=1,
            grid=(group,),
            in_specs=[pl.BlockSpec((rows, width), lambda d, me: (0, 0))] * len(flat)
            + untouched(after),
            out_specs=pl.BlockSpec((rows, pairs * width), lambda d, me: (0, me[0] ^ d)),
        ),
        out_shape=jax.ShapeDtypeStruct((rows, group * pairs * width), jnp.bfloat16),
        compiler_params=compiler_params(),
        name="place",
    )(me, *flat, *after)


def exchange(array, axis, mask, size):
    return lax.ppermute(array, axis, [(i, i ^ mask) for i in range(size)])


def swap_heads(pieces, group):
    return [pieces[0]] + [exchange(pieces[d], "grp", d, group) for d in range(1, group)]


def assemble_kernel(me_ref, own_ref, other_ref, out_ref):
    @pl.when(pl.program_id(1) == 0)
    def _():
        out_ref[...] = own_ref[0]

    @pl.when(pl.program_id(1) == 1)
    def _():
        out_ref[...] = other_ref[0]


def near_parts(part, group):
    if group != 4:
        return jnp.stack([part] + [exchange(part, "grp", d, group) for d in range(1, group)])
    rows = part.shape[0] // 2
    first, second = [exchange(part, "grp", d, group) for d in (1, 2)]
    upper = exchange(second[:rows], "grp", 1, group)
    lower = exchange(first[rows:], "grp", 2, group)
    return jnp.stack([part, first, second, jnp.concatenate([upper, lower], axis=0)])


def gather_direct(own, me_core, group, by_rows):
    other = exchange(own, "core", 1, 2)
    rows, columns = own.shape[1:]
    if by_rows:
        shape = (2 * group * rows, columns)
        target = lambda d, side, me: ((me[0] ^ d) * 2 + (me[1] ^ side), 0)
    else:
        shape = (group * rows, 2 * columns)
        target = lambda d, side, me: (me[0] ^ d, me[1] ^ side)
    return pl.pallas_call(
        assemble_kernel,
        grid_spec=pltpu.PrefetchScalarGridSpec(
            num_scalar_prefetch=1,
            grid=(group, 2),
            in_specs=[pl.BlockSpec((1, rows, columns), lambda d, side, me: (d, 0, 0))] * 2,
            out_specs=pl.BlockSpec((rows, columns), target),
        ),
        out_shape=jax.ShapeDtypeStruct(shape, jnp.bfloat16),
        compiler_params=compiler_params(),
        name="assemble",
    )(me_core, own, other)


def merge_kernel(pairs, group, core_ref, own_ref, other_ref, out_ref):
    low, high = [], []
    half = 3 * PAIR * group // 2
    first = core_ref[0] == 0
    for part in range(3):
        for owner in range(group):
            for pair in range(pairs):
                side, within = divmod((owner * 3 + part) * PAIR, half)
                source = pl.ds(pair * half + within, PAIR)
                target = ((part * group + owner) * pairs + pair) * PAIR
                own, other = own_ref[:, source], other_ref[:, source]
                chosen = jnp.where(first, own, other) if side == 0 else jnp.where(first, other, own)
                out_ref[:, target : target + PAIR] = chosen


def merged_columns(core, own, other, pairs, group, after):
    rows, columns = own.shape
    block = pl.BlockSpec((rows, columns), lambda i, core: (0, 0))
    return pl.pallas_call(
        skipping(functools.partial(merge_kernel, pairs, group), 3, len(after)),
        grid_spec=pltpu.PrefetchScalarGridSpec(
            num_scalar_prefetch=1,
            grid=(1,),
            in_specs=[block, block, *untouched(after)],
            out_specs=pl.BlockSpec((rows, 2 * columns), lambda i, core: (0, 0)),
        ),
        out_shape=jax.ShapeDtypeStruct((rows, 2 * columns), jnp.bfloat16),
        compiler_params=compiler_params(),
        name="merge",
    )(core, own, other, *after)


def attend_kernel(q_ref, k_ref, v_ref, qf_ref, kf_ref, own_v_ref, own_f_ref, out_ref, stat_ref, ke):
    @pl.when(pl.program_id(0) == 0)
    def _():
        ke[:, :PAIR] = k_ref[...]
        ke[:, PAIR:] = kf_ref[...]

    query = q_ref[...]
    lane = lax.broadcasted_iota(jnp.int32, query.shape, 1)
    scores = []
    for head in range(2):
        mine = (lane < HEAD) == (head == 0)
        wide = jnp.concatenate([jnp.where(mine, query, 0), qf_ref[...]], axis=1)
        scores.append(against(wide, ke[...]))
    mixed, logs = [], []
    for head in range(2):
        top = jnp.max(scores[head], axis=1, keepdims=True)
        weights = jnp.exp(scores[head] - top)
        total = jnp.sum(weights, axis=1, keepdims=True)
        got = jnp.dot(
            weights.astype(jnp.bfloat16), v_ref[...], preferred_element_type=jnp.float32
        )
        mixed.append(got / total)
        logs.append(top + jnp.log(total))
    dead = own_f_ref[:, SEQ_SLOTS : SEQ_SLOTS + 1].astype(jnp.float32) > 0.5
    result = jnp.where(lane < HEAD, mixed[0], mixed[1]).astype(jnp.bfloat16)
    out_ref[...] = jnp.where(dead, own_v_ref[...], result)
    stat = jnp.where(lane == 0, logs[0], jnp.where(lane == 1, logs[1], 0.0))
    stat_ref[...] = jnp.where(dead, 0.0, stat)


def block_rows(rows):
    return 512 if rows <= 2048 else 256


def attend(qkv, query_side, key_side, after=()):
    rows = qkv.shape[0]
    block = block_rows(rows)

    def some(part):
        return pl.BlockSpec((block, PAIR), lambda i: (i, part))

    def whole(part):
        return pl.BlockSpec((rows, PAIR), lambda i: (0, part))

    return pl.pallas_call(
        skipping(attend_kernel, 7, len(after)),
        grid=(rows // block,),
        in_specs=[
            some(0), whole(1), whole(2), some(0), whole(0), some(2), some(0), *untouched(after),
        ],
        out_specs=[some(0), some(0)],
        out_shape=[
            jax.ShapeDtypeStruct((rows, PAIR), jnp.bfloat16),
            jax.ShapeDtypeStruct((rows, PAIR), jnp.float32),
        ],
        scratch_shapes=[pltpu.VMEM((rows, 2 * PAIR), jnp.bfloat16)],
        compiler_params=compiler_params(),
        name="attend",
    )(qkv, qkv, qkv, query_side, key_side, qkv, key_side, *after)


def in_three(column, lane):
    first = column.astype(jnp.bfloat16).astype(jnp.float32)
    second = (column - first).astype(jnp.bfloat16).astype(jnp.float32)
    third = column - first - second
    return jnp.where(
        lane == STAT_LANE,
        first,
        jnp.where(lane == STAT_LANE + 1, second, jnp.where(lane == STAT_LANE + 2, third, 0.0)),
    )


def attend_back_kernel(
    q_ref, k_ref, v_ref, qf_ref, kf_ref, stat_ref, att_ref, grad_ref, cos_ref, sin_ref,
    own_cos_ref, own_sin_ref, out_ref, ke, ve, kt, dk_sum, dv_sum,
):
    @pl.when(pl.program_id(0) == 0)
    def _():
        ke[:, :PAIR] = k_ref[...]
        ke[:, PAIR:] = kf_ref[...]
        ve[:, :PAIR] = v_ref[...]
        ve[:, PAIR:] = kf_ref[...]
        kt[...] = k_ref[...].T
        dk_sum[...] = jnp.zeros_like(dk_sum)
        dv_sum[...] = jnp.zeros_like(dv_sum)

    query, grad = q_ref[...], grad_ref[...]
    lane = lax.broadcasted_iota(jnp.int32, query.shape, 1)
    both = grad.astype(jnp.float32) * att_ref[...].astype(jnp.float32)
    stat = stat_ref[...]
    query_heads, grad_heads, weights, grad_scores, turned_grads = [], [], [], [], []
    for head in range(2):
        mine = (lane < HEAD) == (head == 0)
        query_head = jnp.where(mine, query, 0)
        grad_head = jnp.where(mine, grad, 0)
        log_total = jnp.sum(jnp.where(lane == head, stat, 0.0), axis=1, keepdims=True)
        centre = jnp.sum(jnp.where(mine, both, 0.0), axis=1, keepdims=True)
        side = (qf_ref[...].astype(jnp.float32) - in_three(log_total, lane)).astype(jnp.bfloat16)
        wide = jnp.concatenate([query_head, side], axis=1)
        weight = jnp.exp(against(ke[...], wide))
        wide_grad = jnp.concatenate(
            [grad_head, (-in_three(centre, lane)).astype(jnp.bfloat16)], axis=1
        )
        grad_score = (weight * against(ve[...], wide_grad)).astype(jnp.bfloat16)
        weights.append(weight.astype(jnp.bfloat16))
        grad_scores.append(grad_score)
        query_heads.append(query_head)
        grad_heads.append(grad_head)
        turned_grads.append(jnp.dot(kt[...], grad_score, preferred_element_type=jnp.float32))
    dv_sum[...] += jnp.dot(
        jnp.concatenate(weights, axis=1),
        jnp.concatenate(grad_heads, axis=0),
        preferred_element_type=jnp.float32,
    )
    dk_sum[...] += jnp.dot(
        jnp.concatenate(grad_scores, axis=1),
        jnp.concatenate(query_heads, axis=0),
        preferred_element_type=jnp.float32,
    )
    row = lax.broadcasted_iota(jnp.int32, turned_grads[0].shape, 0)
    grad_query = jnp.where(row < HEAD, turned_grads[0], turned_grads[1]).T * HEAD ** (-0.5)
    block = query.shape[0]
    own = pl.ds(pl.multiple_of(pl.program_id(0) * block, block), block)
    out_ref[own, :PAIR] = turned(grad_query, own_cos_ref[...], -own_sin_ref[...]).astype(
        jnp.bfloat16
    )

    @pl.when(pl.program_id(0) == pl.num_programs(0) - 1)
    def _():
        out_ref[:, PAIR : 2 * PAIR] = turned(dk_sum[...], cos_ref[...], -sin_ref[...]).astype(
            jnp.bfloat16
        )
        out_ref[:, 2 * PAIR :] = dv_sum[...].astype(jnp.bfloat16)


def attend_back(qkv, query_side, key_side, stat, attended, grad, cos, sin, pair, after=()):
    rows = qkv.shape[0]
    block = block_rows(rows)

    def some(part):
        return pl.BlockSpec((block, PAIR), lambda i: (i, part))

    def whole(part):
        return pl.BlockSpec((rows, PAIR), lambda i: (0, part))

    return pl.pallas_call(
        skipping(attend_back_kernel, 12, len(after)),
        grid=(rows // block,),
        in_specs=[
            some(0), whole(1), whole(2), some(0), whole(0), some(0), some(0), some(pair),
            whole(0), whole(0), some(0), some(0), *untouched(after),
        ],
        out_specs=pl.BlockSpec((rows, 3 * PAIR), lambda i: (0, 0)),
        out_shape=jax.ShapeDtypeStruct((rows, 3 * PAIR), jnp.bfloat16),
        scratch_shapes=[
            pltpu.VMEM((rows, 2 * PAIR), jnp.bfloat16),
            pltpu.VMEM((rows, 2 * PAIR), jnp.bfloat16),
            pltpu.VMEM((PAIR, rows), jnp.bfloat16),
            pltpu.VMEM((rows, PAIR), jnp.float32),
            pltpu.VMEM((rows, PAIR), jnp.float32),
        ],
        compiler_params=compiler_params(),
        name="attend_back",
    )(qkv, qkv, qkv, query_side, key_side, stat, attended, grad, cos, sin, cos, sin, *after)


def product(left, right):
    return jnp.dot(left, right, preferred_element_type=jnp.float32)


def contract(left, right):
    return lax.dot_general(
        left, right, (((0,), (0,)), ((), ())), preferred_element_type=jnp.float32
    )


def against(left, right):
    return lax.dot_general(
        left, right, (((1,), (1,)), ((), ())), preferred_element_type=jnp.float32
    )


def own_half(array, core):
    half = array.shape[0] // 2
    return lax.dynamic_slice_in_dim(array, core * half, half)


def gather_weight(weight, core):
    return lax.all_gather(
        own_half(weight, core).astype(jnp.bfloat16), ("grp", "core"), axis=0, tiled=True
    )


def pick(array, index, axis):
    return lax.dynamic_index_in_dim(array, index, axis, keepdims=False)


def added(*terms):
    return sum(term.astype(jnp.float32) for term in terms).astype(jnp.bfloat16)


def delayed(value, after):
    return lax.optimization_barrier((value, after))[0]


def halved(array, mask, group, dim, after=()):
    bit = (lax.axis_index("grp") // mask) % 2
    got = exchange(pick(array, 1 - bit, dim), "grp", mask, group)
    return added(delayed(pick(array, bit, dim), after), got)


def core_theirs(left, right, core):
    columns = right.shape[1] // 2
    theirs = lax.dynamic_slice_in_dim(right, (1 - core) * columns, columns, 1)
    return contract(left, theirs).astype(jnp.bfloat16)


def core_mine(left, right, core, sent):
    columns = right.shape[1] // 2
    mine = lax.dynamic_slice_in_dim(right, core * columns, columns, 1)
    got = exchange(sent, "core", 1, 2)
    return (contract(left, mine) + got.astype(jnp.float32)).astype(jnp.bfloat16)


def group_first(share, group, after=()):
    rows, columns = share.shape[0] // group, share.shape[1]
    if group != 4:
        return (lax.psum_scatter(share, "grp", scatter_dimension=0, tiled=True),)
    share = share.reshape(2, 2, rows, columns)
    return (
        halved(share[:, :, : rows // 2], 2, group, 0, after),
        halved(share[:, :, rows // 2 :], 1, group, 1, after),
    )


def group_second(halves, group, after=()):
    if group != 4:
        return halves[0]
    return jnp.concatenate(
        [halved(halves[0], 1, group, 0, after), halved(halves[1], 2, group, 0, after)], axis=0
    )


def far_masks(far):
    return [1 << bit for bit in range(far.bit_length() - 1)]


def far_scatter(share, far, waits=((), ()), dim=0):
    if far > 4:
        return [lax.psum(share, "far")]
    stages = [share]
    for mask, after in zip(far_masks(far), waits):
        share = stages[-1]
        bit = (lax.axis_index("far") // mask) % 2
        size = share.shape[dim] // 2
        got = exchange(
            lax.dynamic_slice_in_dim(share, (1 - bit) * size, size, dim), "far", mask, far
        )
        kept = lax.dynamic_slice_in_dim(share, bit * size, size, dim)
        stages.append(added(delayed(kept, after), got))
    return stages


def doubled(array, axis, mask, size, dim, after):
    bit = (lax.axis_index(axis) // mask) % 2
    got = exchange(array, axis, mask, size)
    array = delayed(array, after)
    low = jnp.where(bit == 0, array, got)
    high = jnp.where(bit == 0, got, array)
    return jnp.concatenate([low, high], axis=dim)


def spread(share, far, waits=((), ()), dim=0):
    if far <= 4:
        for mask, after in zip(far_masks(far)[::-1], waits):
            share = doubled(share, "far", mask, far, dim, after)
    return share


def spread_halves(array):
    spare = ((0, 0), (0, FF_WIDE - FF))
    return jnp.concatenate([jnp.pad(array[:, :FF], spare), jnp.pad(array[:, FF:], spare)], axis=1)


def adam_update(weight, mean, square, grad, rate):
    mean_new = 0.9 * mean + 0.1 * grad
    square_new = 0.999 * square + 0.001 * grad * grad
    step_size = mean_new / (1.0 - 0.9**STEP) / (jnp.sqrt(square_new / (1.0 - 0.999**STEP)) + 1e-08)
    return (mean_new, square_new, weight - rate * (step_size + 0.01 * weight))


def local(
    group,
    far,
    tokens,
    slot_ids,
    cotangent,
    inproj,
    outproj,
    upproj,
    downproj,
    norm_gains,
    inproj_mean,
    outproj_mean,
    upproj_mean,
    downproj_mean,
    gains_mean,
    inproj_square,
    outproj_square,
    upproj_square,
    downproj_square,
    gains_square,
):
    me = lax.axis_index("grp")
    core = lax.axis_index("core")
    me_list = me.reshape(1).astype(jnp.int32)
    core_list = core.reshape(1).astype(jnp.int32)
    pairs = D // PAIR // group
    masters = (inproj, outproj, upproj, downproj, norm_gains)
    own_rows = tokens.shape[1]
    own_gains = norm_gains.shape[0]
    both = ("grp", "core")
    w_in = lax.all_gather(lower_half(core_list, inproj, group), both, axis=0, tiled=True)
    me_core = jnp.stack([me, core]).astype(jnp.int32)
    w_outup = gather_weight(jnp.concatenate([outproj, spread_halves(upproj)], axis=1), core)
    w_out, w_up = w_outup[:, :D], w_outup[:, D:]
    packed = jnp.concatenate([norm_gains[:, 0], norm_gains[:, 1], slot_ids[0].astype(jnp.float32)])
    packed = lax.all_gather(packed.astype(jnp.bfloat16), "grp", axis=0, tiled=False)
    gain_one = packed[:, :own_gains].reshape(D).astype(jnp.float32)
    gain_two = packed[:, own_gains : 2 * own_gains].reshape(D).astype(jnp.float32)
    all_ids = packed[:, 2 * own_gains :].astype(jnp.int32).reshape(group * own_rows)
    group_rows = all_ids.shape[0]
    order = me ^ jnp.arange(group, dtype=jnp.int32)
    near_ids = all_ids.reshape(group, own_rows)[order].reshape(group_rows)
    where_at = positions(all_ids).reshape(group, own_rows)[order].reshape(group_rows)
    cos, sin = lax.optimization_barrier(pair_tables(where_at))
    query_side, key_side = slot_features(near_ids)
    live = (slot_ids[0] >= 0).astype(jnp.bfloat16)
    inputs = tokens[0].astype(jnp.float32)
    first_normed = layer_norm(inputs, gain_one).astype(jnp.bfloat16)
    cos_near = cos.reshape(group, own_rows, PAIR)
    sin_near = sin.reshape(group, own_rows, PAIR)
    shares = 2 * far if far <= 4 else 2
    place_of = core * far + lax.axis_index("far") if far <= 4 else core
    low_down = lax.dynamic_slice_in_dim(
        downproj, place_of * (D // shares), D // shares, 1
    ).astype(jnp.bfloat16)
    near_down = near_parts(low_down, group)
    qkv, stats, attended_near, attended_here, first_sent = [], [], [], [], []
    for pair in range(pairs):
        after = first_sent[:1] + [near_down] * (pair == pairs - 1)
        pieces = project(me_list, first_normed, w_in, cos_near, sin_near, pair, group, after)
        first_sent.append(pieces)
        qkv.append(swap_heads(pieces, group))
    for pair in range(pairs):
        qkv[pair] = jnp.concatenate([delayed(qkv[pair][0], stats[-1:]), *qkv[pair][1:]], axis=0)
        mixed, stat = attend(qkv[pair], query_side, key_side)
        stats.append(stat)
        attended_near.append(mixed)
        mixed = delayed(mixed, attended_here[:1])
        attended_here.append(swap_heads(mixed.reshape(group, own_rows, PAIR), group))
    attended = place(me_list, attended_here, group)
    if far <= 4:
        for mask, after in zip(far_masks(far), (qkv[0][:8], attended)):
            near_down = doubled(near_down, "far", mask, far, 2, after)
    w_down = gather_direct(near_down, me_core, group, False)
    middle = inputs + product(attended, w_out)
    second_normed = layer_norm(middle, gain_two).astype(jnp.bfloat16)
    gate_up = product(second_normed, w_up)
    gate = gate_up[:, :FF]
    upward = gate_up[:, FF_WIDE : FF_WIDE + FF]
    below = 0.5 + 0.5 * lax.erf(gate * 0.5**0.5)
    hidden = (gate * below * upward).astype(jnp.bfloat16)
    grad_top = cotangent[0] * live[:, None]
    grad_down = contract(hidden, grad_top).astype(jnp.bfloat16)
    grad_hidden = against(delayed(grad_top, grad_down), w_down)
    slope = below + gate * jnp.exp(-0.5 * gate * gate) * (2.0 * math.pi) ** -0.5
    grad_gate_up = spread_halves(
        jnp.concatenate([grad_hidden * upward * slope, grad_hidden * gate * below], axis=1)
    ).astype(jnp.bfloat16)
    down_share = lax.psum_scatter(grad_down, both, scatter_dimension=0, tiled=True)
    up_theirs = core_theirs(second_normed, grad_gate_up, core)
    grad_gate_up, up_theirs = lax.optimization_barrier((grad_gate_up, up_theirs))
    grad_second = against(grad_gate_up, w_up)
    _, second_back = jax.vjp(lambda v: layer_norm(v, gain_two), middle)
    (grad_from_norm,) = second_back(grad_second)
    grad_middle = grad_top.astype(jnp.float32) + grad_from_norm
    grad_branch = grad_middle.astype(jnp.bfloat16)
    sent = row_product(me_list, grad_branch, w_outup, group, (up_theirs,))
    grad_near = jnp.concatenate(swap_heads(sent, group), axis=0)
    out_theirs = core_theirs(attended, delayed(grad_branch, sent), core)
    up_share = jnp.concatenate(
        [
            core_mine(second_normed, grad_gate_up, core, up_theirs),
            core_mine(attended, grad_branch, core, out_theirs),
        ],
        axis=1,
    )
    grads_here, grads_near, in_theirs = [], [up_share], []
    for pair in range(pairs):
        grads = attend_back(
            qkv[pair], query_side, key_side, stats[pair], attended_near[pair], grad_near,
            cos, sin, pair, grads_near,
        )
        if pair == 0:
            up_halves = group_first(delayed(up_share, grad_near), group, grads)
            grads_near = [grads, down_share, *up_halves]
            result = middle + product(delayed(hidden, grads), w_down)
        if pair == pairs - 1:
            up_half = group_second(up_halves, group, grads)
        if pair > 0:
            grads = delayed(grads, grads_here[0])
        grads_here.append(swap_heads(grads.reshape(group, own_rows, 3 * PAIR), group))
    grads_placed, grad_first = [], 0.0
    for pair in range(pairs):
        after = (up_half,) if pair == 0 else (in_theirs[0],)
        placed = place(me_list, [grads_here[pair]], group, after)
        grads_placed.append(placed)
        in_theirs.append(core_theirs(first_normed, placed, core))
    in_share = jnp.concatenate(
        [
            core_mine(first_normed, grads_placed[pair], core, in_theirs[pair])
            for pair in range(pairs)
        ],
        axis=1,
    )
    in_first = group_first(in_share, group)
    in_half = group_second(in_first, group)
    in_stages = far_scatter(in_half, far)
    in_chunk, in_early = in_stages[-1], in_stages[min(1, len(in_stages) - 1)]
    for pair in range(pairs):
        width = 3 * PAIR * group
        part = w_in[:, pair * width : (pair + 1) * width]
        grad_first = grad_first + against(delayed(grads_placed[pair], in_share), part)
    up_chunk = far_scatter(up_half, far, (in_theirs[-1], in_share))[-1]
    up_chunk = spread(up_chunk, far, (in_first, in_half))
    up_final = doubled(up_chunk, "core", 1, 2, 1, in_early)
    total_up = up_final.astype(jnp.float32)
    wide = up_chunk.shape[1]
    total_out = jnp.concatenate([total_up[:, FF_WIDE:wide], total_up[:, wide + FF_WIDE :]], axis=1)
    total_up = jnp.concatenate([total_up[:, :FF], total_up[:, wide : wide + FF]], axis=1)
    down_share = delayed(down_share, in_theirs[0])
    down_share = far_scatter(down_share, far, (in_theirs[-1], in_share), 1)[-1]
    down_share = spread(down_share, far, (in_first, in_half), 1)
    total_down = doubled(down_share, "core", 1, 2, 0, in_chunk).astype(jnp.float32)
    _, first_back = jax.vjp(lambda v: layer_norm(v, gain_one), inputs)
    (grad_inputs,) = first_back(grad_first)
    input_grad = (grad_middle + grad_inputs).astype(jnp.bfloat16)
    means = (inproj_mean, outproj_mean, upproj_mean, downproj_mean, gains_mean)
    squares = (inproj_square, outproj_square, upproj_square, downproj_square, gains_square)

    def update(index, total):
        return adam_update(masters[index], means[index], squares[index], total, rate_list[index])

    updates = [None, update(1, total_out), update(2, total_up), update(3, total_down), None]
    in_chunk = spread(in_chunk, far)
    total_in = merged_columns(
        core_list, in_chunk, exchange(in_chunk, "core", 1, 2), pairs, group,
        [updates[index][2] for index in (1, 2, 3)],
    ).astype(jnp.float32)
    low_in = inproj.astype(jnp.bfloat16).astype(jnp.float32)
    low_up = upproj.astype(jnp.bfloat16).astype(jnp.float32)
    low_gains = norm_gains.astype(jnp.bfloat16).astype(jnp.float32)
    total_gains = (
        jnp.stack([jnp.sum(low_in * total_in, axis=1), jnp.sum(low_up * total_up, axis=1)], axis=1)
        / low_gains
    )
    updates[0] = update(0, total_in)
    updates[4] = update(4, total_gains)
    return (
        result.astype(jnp.bfloat16)[None],
        input_grad[None],
        updates[0][0],
        updates[0][1],
        updates[0][2],
        updates[1][0],
        updates[1][1],
        updates[1][2],
        updates[2][0],
        updates[2][1],
        updates[2][2],
        updates[3][0],
        updates[3][1],
        updates[3][2],
        updates[4][0],
        updates[4][1],
        updates[4][2],
    )


def solution(mesh):
    group_size, replicas = mesh.devices.shape
    fine = Mesh(mesh.devices.reshape(group_size, replicas // 2, 2), ("grp", "far", "core"))
    placed = (
        P(("far", "core"), "grp", None),
        P(("far", "core"), "grp"),
        P(("far", "core"), "grp", None),
        P("grp", None),
        P("grp", None),
        P("grp", None),
        P("grp", None),
        P("grp", None),
        P("grp", None),
        P("grp", None),
        P("grp", None),
        P("grp", None),
        P("grp", None),
        P("grp", None),
        P("grp", None),
        P("grp", None),
        P("grp", None),
        P("grp", None),
    )
    return jax.shard_map(
        functools.partial(local, group_size, replicas // 2),
        mesh=fine,
        in_specs=placed,
        out_specs=(
            P(("far", "core"), "grp", None),
            P(("far", "core"), "grp", None),
            P("grp", None),
            P("grp", None),
            P("grp", None),
            P("grp", None),
            P("grp", None),
            P("grp", None),
            P("grp", None),
            P("grp", None),
            P("grp", None),
            P("grp", None),
            P("grp", None),
            P("grp", None),
            P("grp", None),
            P("grp", None),
            P("grp", None),
        ),
        check_vma=False,
    )
```

```python
import functools
import math

import jax
import jax.numpy as jnp
from jax import lax
from jax.experimental import pallas as pl
from jax.experimental.pallas import tpu as pltpu
from jax.sharding import Mesh, PartitionSpec as P

D = 1024
HEADS = 16
HEAD = 64
FF = 2624
FF_WIDE = 2688
STEP = 10
SEQ_SLOTS = 9
PAIR = 128
STAT_LANE = 16
VMEM_BYTES = 56 * 1024 * 1024


rope_base = 160000.0
norm_eps = 1e-05
rate_list = (0.1, 0.4, 0.08, 0.05, 0.6)


def layer_norm(values, gain):
    centred = values - jnp.mean(values, axis=-1, keepdims=True)
    spread = jnp.mean(centred * centred, axis=-1, keepdims=True)
    return centred * lax.rsqrt(spread + norm_eps) * gain


def positions(ids):
    live = ids >= 0
    counted = jnp.cumsum(live.astype(jnp.int32)) - 1
    onehot = (
        (ids[:, None] == jnp.arange(SEQ_SLOTS, dtype=jnp.int32)[None, :]) & live[:, None]
    ).astype(jnp.int32)
    counts = jnp.sum(onehot, axis=0)
    starts = jnp.cumsum(counts) - counts
    first = jnp.sum(onehot * starts[None, :], axis=1)
    return jnp.where(live, counted - first, 0)


def pair_tables(where_at):
    lane = jnp.arange(PAIR, dtype=jnp.int32)
    order = (lane % (HEAD // 2)).astype(jnp.float32)
    inverse = rope_base ** (-(order * 2.0 / HEAD))
    angles = where_at.astype(jnp.float32)[:, None] * inverse[None, :]
    signs = jnp.where(lane % HEAD < HEAD // 2, -1.0, 1.0)
    return jnp.cos(angles), jnp.sin(angles) * signs[None, :]


def slot_features(ids):
    lane = jnp.arange(PAIR, dtype=jnp.int32)[None, :]
    column = jnp.where(ids < 0, SEQ_SLOTS, ids)[:, None]
    own = lane == column
    query_side = jnp.where((lane <= SEQ_SLOTS) & (~own | (ids < 0)[:, None]), -1e30, 0.0)
    key_side = jnp.where(own | ((lane >= STAT_LANE) & (lane < STAT_LANE + 3)), 1.0, 0.0)
    return query_side.astype(jnp.bfloat16), key_side.astype(jnp.bfloat16)


def turned(values, cos, sin):
    lane = lax.broadcasted_iota(jnp.int32, values.shape, 1)
    half = HEAD // 2
    other = jnp.where(
        lane % HEAD < half, pltpu.roll(values, PAIR - half, 1), pltpu.roll(values, half, 1)
    )
    return values * cos + other * sin


def compiler_params():
    return pltpu.CompilerParams(vmem_limit_bytes=VMEM_BYTES)


def lower_kernel(pairs, group, core_ref, w_ref, out_ref):
    for pair in range(pairs):
        for owner in range(group):
            for part in range(3):
                source = ((part * group + owner) * pairs + pair) * PAIR
                target = ((pair * group + owner) * 3 + part) * PAIR
                out_ref[:, target : target + PAIR] = w_ref[:, source : source + PAIR].astype(
                    jnp.bfloat16
                )


def lower_half(core, weight, group):
    rows, columns = weight.shape[0] // 2, weight.shape[1]
    return pl.pallas_call(
        functools.partial(lower_kernel, D // PAIR // group, group),
        grid_spec=pltpu.PrefetchScalarGridSpec(
            num_scalar_prefetch=1,
            grid=(1,),
            in_specs=[pl.BlockSpec((rows, columns), lambda i, core: (core[0], 0))],
            out_specs=pl.BlockSpec((rows, columns), lambda i, core: (0, 0)),
        ),
        out_shape=jax.ShapeDtypeStruct((rows, columns), jnp.bfloat16),
        compiler_params=compiler_params(),
        name="lower_half",
    )(core, weight)


def project_kernel(me_ref, x_ref, w_ref, cos_ref, sin_ref, out_ref):
    got = jnp.dot(x_ref[...], w_ref[...], preferred_element_type=jnp.float32)
    cos, sin = cos_ref[0], sin_ref[0]
    query = turned(got[:, :PAIR], cos, sin) * HEAD ** (-0.5)
    keys = turned(got[:, PAIR : 2 * PAIR], cos, sin)
    out_ref[0, :, :PAIR] = query.astype(jnp.bfloat16)
    out_ref[0, :, PAIR : 2 * PAIR] = keys.astype(jnp.bfloat16)
    out_ref[0, :, 2 * PAIR :] = got[:, 2 * PAIR :].astype(jnp.bfloat16)


def skipping(kernel, before, extra):
    def body(*refs):
        kernel(*refs[:before], *refs[before + extra :])

    return body


def untouched(after):
    return [pl.BlockSpec(memory_space=pl.ANY)] * len(after)


def project(me, first_normed, w_in, cos, sin, pair, group, after=()):
    rows = first_normed.shape[0]
    return pl.pallas_call(
        skipping(project_kernel, 5, len(after)),
        grid_spec=pltpu.PrefetchScalarGridSpec(
            num_scalar_prefetch=1,
            grid=(group,),
            in_specs=[
                pl.BlockSpec((rows, D), lambda d, me: (0, 0)),
                pl.BlockSpec((D, 3 * PAIR), lambda d, me: (0, pair * group + (me[0] ^ d))),
                pl.BlockSpec((1, rows, PAIR), lambda d, me: (0, 0, 0)),
                pl.BlockSpec((1, rows, PAIR), lambda d, me: (0, 0, 0)),
                *untouched(after),
            ],
            out_specs=pl.BlockSpec((1, rows, 3 * PAIR), lambda d, me: (d, 0, 0)),
        ),
        out_shape=jax.ShapeDtypeStruct((group, rows, 3 * PAIR), jnp.bfloat16),
        compiler_params=compiler_params(),
        name="project",
    )(me, first_normed, w_in, cos, sin, *after)


def row_product_kernel(me_ref, x_ref, w_ref, out_ref):
    out_ref[0] = against(x_ref[...], w_ref[...]).astype(jnp.bfloat16)


def row_product(me, left, weight, group, after=()):
    rows = left.shape[0]
    wide = D // group
    return pl.pallas_call(
        skipping(row_product_kernel, 3, len(after)),
        grid_spec=pltpu.PrefetchScalarGridSpec(
            num_scalar_prefetch=1,
            grid=(group,),
            in_specs=[
                pl.BlockSpec((rows, D), lambda d, me: (0, 0)),
                pl.BlockSpec((wide, D), lambda d, me: (me[0] ^ d, 0)),
                *untouched(after),
            ],
            out_specs=pl.BlockSpec((1, rows, wide), lambda d, me: (d, 0, 0)),
        ),
        out_shape=jax.ShapeDtypeStruct((group, rows, wide), jnp.bfloat16),
        compiler_params=compiler_params(),
        name="row_product",
    )(me, left, weight, *after)


def place(me, pieces, group, after=()):
    rows, width = pieces[0][0].shape
    pairs = len(pieces)
    flat = [piece for near in pieces for piece in near]

    def kernel(me_ref, *refs):
        out_ref = refs[-1]
        for step in range(group):

            @pl.when(pl.program_id(0) == step)
            def _():
                for pair in range(pairs):
                    out_ref[:, pair * width : (pair + 1) * width] = refs[pair * group + step][...]

    return pl.pallas_call(
        kernel,
        grid_spec=pltpu.PrefetchScalarGridSpec(
            num_scalar_prefetch=1,
            grid=(group,),
            in_specs=[pl.BlockSpec((rows, width), lambda d, me: (0, 0))] * len(flat)
            + untouched(after),
            out_specs=pl.BlockSpec((rows, pairs * width), lambda d, me: (0, me[0] ^ d)),
        ),
        out_shape=jax.ShapeDtypeStruct((rows, group * pairs * width), jnp.bfloat16),
        compiler_params=compiler_params(),
        name="place",
    )(me, *flat, *after)


def exchange(array, axis, mask, size):
    return lax.ppermute(array, axis, [(i, i ^ mask) for i in range(size)])


def swap_heads(pieces, group):
    return [pieces[0]] + [exchange(pieces[d], "grp", d, group) for d in range(1, group)]


def assemble_kernel(me_ref, own_ref, other_ref, out_ref):
    @pl.when(pl.program_id(1) == 0)
    def _():
        out_ref[...] = own_ref[0]

    @pl.when(pl.program_id(1) == 1)
    def _():
        out_ref[...] = other_ref[0]


def near_parts(part, group):
    if group != 4:
        return jnp.stack([part] + [exchange(part, "grp", d, group) for d in range(1, group)])
    rows = part.shape[0] // 2
    first, second = [exchange(part, "grp", d, group) for d in (1, 2)]
    upper = exchange(second[:rows], "grp", 1, group)
    lower = exchange(first[rows:], "grp", 2, group)
    return jnp.stack([part, first, second, jnp.concatenate([upper, lower], axis=0)])


def gather_direct(own, me_core, group, by_rows):
    other = exchange(own, "core", 1, 2)
    rows, columns = own.shape[1:]
    if by_rows:
        shape = (2 * group * rows, columns)
        target = lambda d, side, me: ((me[0] ^ d) * 2 + (me[1] ^ side), 0)
    else:
        shape = (group * rows, 2 * columns)
        target = lambda d, side, me: (me[0] ^ d, me[1] ^ side)
    return pl.pallas_call(
        assemble_kernel,
        grid_spec=pltpu.PrefetchScalarGridSpec(
            num_scalar_prefetch=1,
            grid=(group, 2),
            in_specs=[pl.BlockSpec((1, rows, columns), lambda d, side, me: (d, 0, 0))] * 2,
            out_specs=pl.BlockSpec((rows, columns), target),
        ),
        out_shape=jax.ShapeDtypeStruct(shape, jnp.bfloat16),
        compiler_params=compiler_params(),
        name="assemble",
    )(me_core, own, other)


def merge_kernel(pairs, group, core_ref, own_ref, other_ref, out_ref):
    low, high = [], []
    half = 3 * PAIR * group // 2
    first = core_ref[0] == 0
    for part in range(3):
        for owner in range(group):
            for pair in range(pairs):
                side, within = divmod((owner * 3 + part) * PAIR, half)
                source = pl.ds(pair * half + within, PAIR)
                target = ((part * group + owner) * pairs + pair) * PAIR
                own, other = own_ref[:, source], other_ref[:, source]
                chosen = jnp.where(first, own, other) if side == 0 else jnp.where(first, other, own)
                out_ref[:, target : target + PAIR] = chosen


def merged_columns(core, own, other, pairs, group, after):
    rows, columns = own.shape
    block = pl.BlockSpec((rows, columns), lambda i, core: (0, 0))
    return pl.pallas_call(
        skipping(functools.partial(merge_kernel, pairs, group), 3, len(after)),
        grid_spec=pltpu.PrefetchScalarGridSpec(
            num_scalar_prefetch=1,
            grid=(1,),
            in_specs=[block, block, *untouched(after)],
            out_specs=pl.BlockSpec((rows, 2 * columns), lambda i, core: (0, 0)),
        ),
        out_shape=jax.ShapeDtypeStruct((rows, 2 * columns), jnp.bfloat16),
        compiler_params=compiler_params(),
        name="merge",
    )(core, own, other, *after)


def attend_kernel(q_ref, k_ref, v_ref, qf_ref, kf_ref, own_v_ref, own_f_ref, out_ref, stat_ref, ke):
    @pl.when(pl.program_id(0) == 0)
    def _():
        ke[:, :PAIR] = k_ref[...]
        ke[:, PAIR:] = kf_ref[...]

    query = q_ref[...]
    lane = lax.broadcasted_iota(jnp.int32, query.shape, 1)
    scores = []
    for head in range(2):
        mine = (lane < HEAD) == (head == 0)
        wide = jnp.concatenate([jnp.where(mine, query, 0), qf_ref[...]], axis=1)
        scores.append(against(wide, ke[...]))
    mixed, logs = [], []
    for head in range(2):
        top = jnp.max(scores[head], axis=1, keepdims=True)
        weights = jnp.exp(scores[head] - top)
        total = jnp.sum(weights, axis=1, keepdims=True)
        got = jnp.dot(
            weights.astype(jnp.bfloat16), v_ref[...], preferred_element_type=jnp.float32
        )
        mixed.append(got / total)
        logs.append(top + jnp.log(total))
    dead = own_f_ref[:, SEQ_SLOTS : SEQ_SLOTS + 1].astype(jnp.float32) > 0.5
    result = jnp.where(lane < HEAD, mixed[0], mixed[1]).astype(jnp.bfloat16)
    out_ref[...] = jnp.where(dead, own_v_ref[...], result)
    stat = jnp.where(lane == 0, logs[0], jnp.where(lane == 1, logs[1], 0.0))
    stat_ref[...] = jnp.where(dead, 0.0, stat)


def block_rows(rows):
    return 512 if rows <= 2048 else 256


def attend(qkv, query_side, key_side, after=()):
    rows = qkv.shape[0]
    block = block_rows(rows)

    def some(part):
        return pl.BlockSpec((block, PAIR), lambda i: (i, part))

    def whole(part):
        return pl.BlockSpec((rows, PAIR), lambda i: (0, part))

    return pl.pallas_call(
        skipping(attend_kernel, 7, len(after)),
        grid=(rows // block,),
        in_specs=[
            some(0), whole(1), whole(2), some(0), whole(0), some(2), some(0), *untouched(after),
        ],
        out_specs=[some(0), some(0)],
        out_shape=[
            jax.ShapeDtypeStruct((rows, PAIR), jnp.bfloat16),
            jax.ShapeDtypeStruct((rows, PAIR), jnp.float32),
        ],
        scratch_shapes=[pltpu.VMEM((rows, 2 * PAIR), jnp.bfloat16)],
        compiler_params=compiler_params(),
        cost_estimate=pl.CostEstimate(
            flops=8 * rows * rows * HEAD,
            transcendentals=2 * rows * rows,
            bytes_accessed=16 * rows * PAIR,
        ),
        name="attend",
    )(qkv, qkv, qkv, query_side, key_side, qkv, key_side, *after)


def in_three(column, lane):
    first = column.astype(jnp.bfloat16).astype(jnp.float32)
    second = (column - first).astype(jnp.bfloat16).astype(jnp.float32)
    third = column - first - second
    return jnp.where(
        lane == STAT_LANE,
        first,
        jnp.where(lane == STAT_LANE + 1, second, jnp.where(lane == STAT_LANE + 2, third, 0.0)),
    )


def attend_back_kernel(
    q_ref, k_ref, v_ref, qf_ref, kf_ref, stat_ref, att_ref, grad_ref, cos_ref, sin_ref,
    own_cos_ref, own_sin_ref, out_ref, ke, ve, kt, dk_sum, dv_sum,
):
    @pl.when(pl.program_id(0) == 0)
    def _():
        ke[:, :PAIR] = k_ref[...]
        ke[:, PAIR:] = kf_ref[...]
        ve[:, :PAIR] = v_ref[...]
        ve[:, PAIR:] = kf_ref[...]
        kt[...] = k_ref[...].T
        dk_sum[...] = jnp.zeros_like(dk_sum)
        dv_sum[...] = jnp.zeros_like(dv_sum)

    query, grad = q_ref[...], grad_ref[...]
    lane = lax.broadcasted_iota(jnp.int32, query.shape, 1)
    both = grad.astype(jnp.float32) * att_ref[...].astype(jnp.float32)
    stat = stat_ref[...]
    query_heads, grad_heads, weights, grad_scores, turned_grads = [], [], [], [], []
    for head in range(2):
        mine = (lane < HEAD) == (head == 0)
        query_head = jnp.where(mine, query, 0)
        grad_head = jnp.where(mine, grad, 0)
        log_total = jnp.sum(jnp.where(lane == head, stat, 0.0), axis=1, keepdims=True)
        centre = jnp.sum(jnp.where(mine, both, 0.0), axis=1, keepdims=True)
        side = (qf_ref[...].astype(jnp.float32) - in_three(log_total, lane)).astype(jnp.bfloat16)
        wide = jnp.concatenate([query_head, side], axis=1)
        weight = jnp.exp(against(ke[...], wide))
        wide_grad = jnp.concatenate(
            [grad_head, (-in_three(centre, lane)).astype(jnp.bfloat16)], axis=1
        )
        grad_score = (weight * against(ve[...], wide_grad)).astype(jnp.bfloat16)
        weights.append(weight.astype(jnp.bfloat16))
        grad_scores.append(grad_score)
        query_heads.append(query_head)
        grad_heads.append(grad_head)
        turned_grads.append(jnp.dot(kt[...], grad_score, preferred_element_type=jnp.float32))
    dv_sum[...] += jnp.dot(
        jnp.concatenate(weights, axis=1),
        jnp.concatenate(grad_heads, axis=0),
        preferred_element_type=jnp.float32,
    )
    dk_sum[...] += jnp.dot(
        jnp.concatenate(grad_scores, axis=1),
        jnp.concatenate(query_heads, axis=0),
        preferred_element_type=jnp.float32,
    )
    row = lax.broadcasted_iota(jnp.int32, turned_grads[0].shape, 0)
    grad_query = jnp.where(row < HEAD, turned_grads[0], turned_grads[1]).T * HEAD ** (-0.5)
    block = query.shape[0]
    own = pl.ds(pl.multiple_of(pl.program_id(0) * block, block), block)
    out_ref[own, :PAIR] = turned(grad_query, own_cos_ref[...], -own_sin_ref[...]).astype(
        jnp.bfloat16
    )

    @pl.when(pl.program_id(0) == pl.num_programs(0) - 1)
    def _():
        out_ref[:, PAIR : 2 * PAIR] = turned(dk_sum[...], cos_ref[...], -sin_ref[...]).astype(
            jnp.bfloat16
        )
        out_ref[:, 2 * PAIR :] = dv_sum[...].astype(jnp.bfloat16)


def attend_back(qkv, query_side, key_side, stat, attended, grad, cos, sin, pair, after=()):
    rows = qkv.shape[0]
    block = block_rows(rows)

    def some(part):
        return pl.BlockSpec((block, PAIR), lambda i: (i, part))

    def whole(part):
        return pl.BlockSpec((rows, PAIR), lambda i: (0, part))

    return pl.pallas_call(
        skipping(attend_back_kernel, 12, len(after)),
        grid=(rows // block,),
        in_specs=[
            some(0), whole(1), whole(2), some(0), whole(0), some(0), some(0), some(pair),
            whole(0), whole(0), some(0), some(0), *untouched(after),
        ],
        out_specs=pl.BlockSpec((rows, 3 * PAIR), lambda i: (0, 0)),
        out_shape=jax.ShapeDtypeStruct((rows, 3 * PAIR), jnp.bfloat16),
        scratch_shapes=[
            pltpu.VMEM((rows, 2 * PAIR), jnp.bfloat16),
            pltpu.VMEM((rows, 2 * PAIR), jnp.bfloat16),
            pltpu.VMEM((PAIR, rows), jnp.bfloat16),
            pltpu.VMEM((rows, PAIR), jnp.float32),
            pltpu.VMEM((rows, PAIR), jnp.float32),
        ],
        compiler_params=compiler_params(),
        cost_estimate=pl.CostEstimate(
            flops=20 * rows * rows * HEAD,
            transcendentals=2 * rows * rows,
            bytes_accessed=20 * rows * PAIR,
        ),
        name="attend_back",
    )(qkv, qkv, qkv, query_side, key_side, stat, attended, grad, cos, sin, cos, sin, *after)


def product(left, right):
    return jnp.dot(left, right, preferred_element_type=jnp.float32)


def contract(left, right):
    return lax.dot_general(
        left, right, (((0,), (0,)), ((), ())), preferred_element_type=jnp.float32
    )


def against(left, right):
    return lax.dot_general(
        left, right, (((1,), (1,)), ((), ())), preferred_element_type=jnp.float32
    )


def own_half(array, core):
    half = array.shape[0] // 2
    return lax.dynamic_slice_in_dim(array, core * half, half)


def gather_weight(weight, core):
    return lax.all_gather(
        own_half(weight, core).astype(jnp.bfloat16), ("grp", "core"), axis=0, tiled=True
    )


def pick(array, index, axis):
    return lax.dynamic_index_in_dim(array, index, axis, keepdims=False)


def added(*terms):
    return sum(term.astype(jnp.float32) for term in terms).astype(jnp.bfloat16)


def delayed(value, after):
    return lax.optimization_barrier((value, after))[0]


def halved(array, mask, group, dim, after=()):
    bit = (lax.axis_index("grp") // mask) % 2
    got = exchange(pick(array, 1 - bit, dim), "grp", mask, group)
    return added(delayed(pick(array, bit, dim), after), got)


def core_theirs(left, right, core):
    columns = right.shape[1] // 2
    theirs = lax.dynamic_slice_in_dim(right, (1 - core) * columns, columns, 1)
    return contract(left, theirs).astype(jnp.bfloat16)


def core_mine(left, right, core, sent):
    columns = right.shape[1] // 2
    mine = lax.dynamic_slice_in_dim(right, core * columns, columns, 1)
    got = exchange(sent, "core", 1, 2)
    return (contract(left, mine) + got.astype(jnp.float32)).astype(jnp.bfloat16)


def group_first(share, group, after=()):
    rows, columns = share.shape[0] // group, share.shape[1]
    if group != 4:
        return (lax.psum_scatter(share, "grp", scatter_dimension=0, tiled=True),)
    share = share.reshape(2, 2, rows, columns)
    return (
        halved(share[:, :, : rows // 2], 2, group, 0, after),
        halved(share[:, :, rows // 2 :], 1, group, 1, after),
    )


def group_second(halves, group, after=()):
    if group != 4:
        return halves[0]
    return jnp.concatenate(
        [halved(halves[0], 1, group, 0, after), halved(halves[1], 2, group, 0, after)], axis=0
    )


def far_masks(far):
    return [1 << bit for bit in range(far.bit_length() - 1)]


def far_scatter(share, far, waits=((), ()), dim=0):
    if far > 4:
        return [lax.psum(share, "far")]
    stages = [share]
    for mask, after in zip(far_masks(far), waits):
        share = stages[-1]
        bit = (lax.axis_index("far") // mask) % 2
        size = share.shape[dim] // 2
        got = exchange(
            lax.dynamic_slice_in_dim(share, (1 - bit) * size, size, dim), "far", mask, far
        )
        kept = lax.dynamic_slice_in_dim(share, bit * size, size, dim)
        stages.append(added(delayed(kept, after), got))
    return stages


def doubled(array, axis, mask, size, dim, after):
    bit = (lax.axis_index(axis) // mask) % 2
    got = exchange(array, axis, mask, size)
    array = delayed(array, after)
    low = jnp.where(bit == 0, array, got)
    high = jnp.where(bit == 0, got, array)
    return jnp.concatenate([low, high], axis=dim)


def spread(share, far, waits=((), ()), dim=0):
    if far <= 4:
        for mask, after in zip(far_masks(far)[::-1], waits):
            share = doubled(share, "far", mask, far, dim, after)
    return share


def spread_halves(array):
    spare = ((0, 0), (0, FF_WIDE - FF))
    return jnp.concatenate([jnp.pad(array[:, :FF], spare), jnp.pad(array[:, FF:], spare)], axis=1)


def adam_update(weight, mean, square, grad, rate):
    mean_new = 0.9 * mean + 0.1 * grad
    square_new = 0.999 * square + 0.001 * grad * grad
    step_size = mean_new / (1.0 - 0.9**STEP) / (jnp.sqrt(square_new / (1.0 - 0.999**STEP)) + 1e-08)
    return (mean_new, square_new, weight - rate * (step_size + 0.01 * weight))


def local(
    group,
    far,
    tokens,
    slot_ids,
    cotangent,
    inproj,
    outproj,
    upproj,
    downproj,
    norm_gains,
    inproj_mean,
    outproj_mean,
    upproj_mean,
    downproj_mean,
    gains_mean,
    inproj_square,
    outproj_square,
    upproj_square,
    downproj_square,
    gains_square,
):
    me = lax.axis_index("grp")
    core = lax.axis_index("core")
    me_list = me.reshape(1).astype(jnp.int32)
    core_list = core.reshape(1).astype(jnp.int32)
    pairs = D // PAIR // group
    masters = (inproj, outproj, upproj, downproj, norm_gains)
    own_rows = tokens.shape[1]
    own_gains = norm_gains.shape[0]
    both = ("grp", "core")
    w_in = lax.all_gather(lower_half(core_list, inproj, group), both, axis=0, tiled=True)
    me_core = jnp.stack([me, core]).astype(jnp.int32)
    w_outup = gather_weight(jnp.concatenate([outproj, spread_halves(upproj)], axis=1), core)
    w_out, w_up = w_outup[:, :D], w_outup[:, D:]
    packed = jnp.concatenate([norm_gains[:, 0], norm_gains[:, 1], slot_ids[0].astype(jnp.float32)])
    packed = lax.all_gather(packed.astype(jnp.bfloat16), "grp", axis=0, tiled=False)
    gain_one = packed[:, :own_gains].reshape(D).astype(jnp.float32)
    gain_two = packed[:, own_gains : 2 * own_gains].reshape(D).astype(jnp.float32)
    all_ids = packed[:, 2 * own_gains :].astype(jnp.int32).reshape(group * own_rows)
    group_rows = all_ids.shape[0]
    order = me ^ jnp.arange(group, dtype=jnp.int32)
    near_ids = all_ids.reshape(group, own_rows)[order].reshape(group_rows)
    where_at = positions(all_ids).reshape(group, own_rows)[order].reshape(group_rows)
    cos, sin = lax.optimization_barrier(pair_tables(where_at))
    query_side, key_side = slot_features(near_ids)
    live = (slot_ids[0] >= 0).astype(jnp.bfloat16)
    inputs = tokens[0].astype(jnp.float32)
    first_normed = layer_norm(inputs, gain_one).astype(jnp.bfloat16)
    cos_near = cos.reshape(group, own_rows, PAIR)
    sin_near = sin.reshape(group, own_rows, PAIR)
    shares = 2 * far if far <= 4 else 2
    place_of = core * far + lax.axis_index("far") if far <= 4 else core
    low_down = lax.dynamic_slice_in_dim(
        downproj, place_of * (D // shares), D // shares, 1
    ).astype(jnp.bfloat16)
    near_down = near_parts(low_down, group)
    qkv, stats, attended_near, attended_here, first_sent = [], [], [], [], []
    for pair in range(pairs):
        after = first_sent[:1] + [near_down] * (pair == pairs - 1)
        pieces = project(me_list, first_normed, w_in, cos_near, sin_near, pair, group, after)
        first_sent.append(pieces)
        qkv.append(swap_heads(pieces, group))
    for pair in range(pairs):
        qkv[pair] = jnp.concatenate([delayed(qkv[pair][0], stats[-1:]), *qkv[pair][1:]], axis=0)
        mixed, stat = attend(qkv[pair], query_side, key_side)
        stats.append(stat)
        attended_near.append(mixed)
        mixed = delayed(mixed, attended_here[:1])
        attended_here.append(swap_heads(mixed.reshape(group, own_rows, PAIR), group))
    attended = place(me_list, attended_here, group)
    if far <= 4:
        for mask, after in zip(far_masks(far), (qkv[0][:8], attended)):
            near_down = doubled(near_down, "far", mask, far, 2, after)
    w_down = gather_direct(near_down, me_core, group, False)
    middle = inputs + product(attended, w_out)
    second_normed = layer_norm(middle, gain_two).astype(jnp.bfloat16)
    gate_up = product(second_normed, w_up)
    gate = gate_up[:, :FF]
    upward = gate_up[:, FF_WIDE : FF_WIDE + FF]
    below = 0.5 + 0.5 * lax.erf(gate * 0.5**0.5)
    hidden = (gate * below * upward).astype(jnp.bfloat16)
    grad_top = cotangent[0] * live[:, None]
    grad_down = contract(hidden, grad_top).astype(jnp.bfloat16)
    grad_hidden = against(delayed(grad_top, grad_down), w_down)
    slope = below + gate * jnp.exp(-0.5 * gate * gate) * (2.0 * math.pi) ** -0.5
    grad_gate_up = spread_halves(
        jnp.concatenate([grad_hidden * upward * slope, grad_hidden * gate * below], axis=1)
    ).astype(jnp.bfloat16)
    down_share = lax.psum_scatter(grad_down, both, scatter_dimension=0, tiled=True)
    up_theirs = core_theirs(second_normed, grad_gate_up, core)
    grad_gate_up, up_theirs = lax.optimization_barrier((grad_gate_up, up_theirs))
    grad_second = against(grad_gate_up, w_up)
    _, second_back = jax.vjp(lambda v: layer_norm(v, gain_two), middle)
    (grad_from_norm,) = second_back(grad_second)
    grad_middle = grad_top.astype(jnp.float32) + grad_from_norm
    grad_branch = grad_middle.astype(jnp.bfloat16)
    sent = row_product(me_list, grad_branch, w_outup, group, (up_theirs,))
    grad_near = jnp.concatenate(swap_heads(sent, group), axis=0)
    out_theirs = core_theirs(attended, delayed(grad_branch, sent), core)
    up_share = jnp.concatenate(
        [
            core_mine(second_normed, grad_gate_up, core, up_theirs),
            core_mine(attended, grad_branch, core, out_theirs),
        ],
        axis=1,
    )
    grads_here, grads_near, in_theirs = [], [up_share], []
    for pair in range(pairs):
        grads = attend_back(
            qkv[pair], query_side, key_side, stats[pair], attended_near[pair], grad_near,
            cos, sin, pair, grads_near,
        )
        if pair == 0:
            up_halves = group_first(delayed(up_share, grad_near), group, grads)
            grads_near = [grads, down_share, *up_halves]
            result = middle + product(delayed(hidden, grads), w_down)
        if pair > 0:
            grads = delayed(grads, grads_here[0])
        grads_here.append(swap_heads(grads.reshape(group, own_rows, 3 * PAIR), group))
    grads_placed, grad_first = [], 0.0
    for pair in range(pairs):
        after = () if pair == 0 else (in_theirs[0],)
        placed = place(me_list, [grads_here[pair]], group, after)
        grads_placed.append(placed)
        in_theirs.append(core_theirs(first_normed, placed, core))
    up_half = group_second(up_halves, group, in_theirs[-1])
    in_share = jnp.concatenate(
        [
            core_mine(first_normed, grads_placed[pair], core, in_theirs[pair])
            for pair in range(pairs)
        ],
        axis=1,
    )
    in_first = group_first(in_share, group)
    in_half = group_second(in_first, group)
    in_stages = far_scatter(in_half, far)
    in_chunk, in_early = in_stages[-1], in_stages[min(1, len(in_stages) - 1)]
    for pair in range(pairs):
        width = 3 * PAIR * group
        part = w_in[:, pair * width : (pair + 1) * width]
        grad_first = grad_first + against(delayed(grads_placed[pair], in_share), part)
    up_chunk = far_scatter(up_half, far, (in_theirs[-1], in_share))[-1]
    up_chunk = spread(up_chunk, far, (in_first, in_half))
    up_final = doubled(up_chunk, "core", 1, 2, 1, in_early)
    total_up = up_final.astype(jnp.float32)
    wide = up_chunk.shape[1]
    total_out = jnp.concatenate([total_up[:, FF_WIDE:wide], total_up[:, wide + FF_WIDE :]], axis=1)
    total_up = jnp.concatenate([total_up[:, :FF], total_up[:, wide : wide + FF]], axis=1)
    down_share = delayed(down_share, in_theirs[0])
    down_share = far_scatter(down_share, far, (in_theirs[-1], in_share), 1)[-1]
    down_share = spread(down_share, far, (in_first, in_half), 1)
    total_down = doubled(down_share, "core", 1, 2, 0, in_chunk).astype(jnp.float32)
    _, first_back = jax.vjp(lambda v: layer_norm(v, gain_one), inputs)
    (grad_inputs,) = first_back(grad_first)
    input_grad = (grad_middle + grad_inputs).astype(jnp.bfloat16)
    means = (inproj_mean, outproj_mean, upproj_mean, downproj_mean, gains_mean)
    squares = (inproj_square, outproj_square, upproj_square, downproj_square, gains_square)

    def update(index, total):
        return adam_update(masters[index], means[index], squares[index], total, rate_list[index])

    updates = [None, update(1, total_out), update(2, total_up), update(3, total_down), None]
    in_chunk = spread(in_chunk, far)
    total_in = merged_columns(
        core_list, in_chunk, exchange(in_chunk, "core", 1, 2), pairs, group,
        [updates[index][2] for index in (1, 2, 3)],
    ).astype(jnp.float32)
    low_in = inproj.astype(jnp.bfloat16).astype(jnp.float32)
    low_up = upproj.astype(jnp.bfloat16).astype(jnp.float32)
    low_gains = norm_gains.astype(jnp.bfloat16).astype(jnp.float32)
    total_gains = (
        jnp.stack([jnp.sum(low_in * total_in, axis=1), jnp.sum(low_up * total_up, axis=1)], axis=1)
        / low_gains
    )
    updates[0] = update(0, total_in)
    updates[4] = update(4, total_gains)
    return (
        result.astype(jnp.bfloat16)[None],
        input_grad[None],
        updates[0][0],
        updates[0][1],
        updates[0][2],
        updates[1][0],
        updates[1][1],
        updates[1][2],
        updates[2][0],
        updates[2][1],
        updates[2][2],
        updates[3][0],
        updates[3][1],
        updates[3][2],
        updates[4][0],
        updates[4][1],
        updates[4][2],
    )


def solution(mesh):
    group_size, replicas = mesh.devices.shape
    fine = Mesh(mesh.devices.reshape(group_size, replicas // 2, 2), ("grp", "far", "core"))
    placed = (
        P(("far", "core"), "grp", None),
        P(("far", "core"), "grp"),
        P(("far", "core"), "grp", None),
        P("grp", None),
        P("grp", None),
        P("grp", None),
        P("grp", None),
        P("grp", None),
        P("grp", None),
        P("grp", None),
        P("grp", None),
        P("grp", None),
        P("grp", None),
        P("grp", None),
        P("grp", None),
        P("grp", None),
        P("grp", None),
        P("grp", None),
    )
    return jax.shard_map(
        functools.partial(local, group_size, replicas // 2),
        mesh=fine,
        in_specs=placed,
        out_specs=(
            P(("far", "core"), "grp", None),
            P(("far", "core"), "grp", None),
            P("grp", None),
            P("grp", None),
            P("grp", None),
            P("grp", None),
            P("grp", None),
            P("grp", None),
            P("grp", None),
            P("grp", None),
            P("grp", None),
            P("grp", None),
            P("grp", None),
            P("grp", None),
            P("grp", None),
            P("grp", None),
            P("grp", None),
        ),
        check_vma=False,
    )
```
